128 devices in a mesh: blk: 16 (over x, z_hi, core), group: 8 (over z_lo, y).
Axes of the slice: x: 4, y: 4, z: 4 (z_hi: 2, z_lo: 2; z = z_hi * 2 + z_lo), core: 2. Of those that a mesh axis runs over, the one named last changes fastest.
Arguments:
- queries: bfloat16 [32768, 4096], P(('blk', 'group')), may hold values from -12 to 12
- keys: bfloat16 [32768, 512], P(('blk', 'group')), may hold values from -12 to 12
- values: bfloat16 [32768, 512], P(('blk', 'group')), may hold values from -6 to 6
- plan: int32 [32768], P(('blk', 'group')), may hold values from 0 to 32767, as said below
- doc_lengths: int32 [8, 4], P('group'), may hold values from 1 to 2048, 4096 in all within a row
Outputs:
- attended: bfloat16 [32768, 4096], P(('blk', 'group'))
The draws below stay inside these ranges and needn't reach their ends.
Inputs may be any that keep to these rules, and one draw needn't show every extreme that they name: `plan`: A permutation of the slots; the tokens of one device go to at most 4 slots of any one device, and to exactly 4 slots of some device.
All inputs are finite; a program needn't handle non-finite values.
Results may differ from the reference program's by a relative error of at most 0.0091.
Values may be sent and summed in bfloat16 or wider, within the bound.
A program may use at most 64 MiB of HBM per device.

```python
import math
import jax
import jax.numpy as jnp
import numpy as np
from jax import lax

QUERY_HEADS = 32
KEY_VALUE_HEADS = 4
HEAD_SIZE = 128
TOK_DEV = 256
DOCS = 4
TOKEN_TOTAL = 32768
CYCLES = 8
CYCLE = 4096
DOC_MOST = 2048
N_BLK = 16
N_GROUP = 8


def base_keys(key):
    return jax.random.normal(key, (TOKEN_TOTAL, KEY_VALUE_HEADS * HEAD_SIZE), jnp.float32)


def draw_keys(key, part):
    shared_part = base_keys(key)
    return jnp.clip(shared_part, -6.0, 6.0).astype(jnp.bfloat16)


def draw_queries(key, part):
    key = jax.random.fold_in(key, 7)
    key_fresh = jax.random.fold_in(key, 0)
    newly_arrived = jax.random.normal(key_fresh, (TOKEN_TOTAL, QUERY_HEADS * HEAD_SIZE), jnp.float32)
    return jnp.clip(newly_arrived, -6.0, 6.0).astype(jnp.bfloat16)


def draw_plan(key, part):
    key = jax.random.fold_in(key, 11)
    devices = TOKEN_TOTAL // TOK_DEV
    capacity = 2 * TOK_DEV // devices
    heavy = 3 * capacity // 4
    light = capacity // 4
    key_start, key_offset, key_shuffle = jax.random.split(key, 3)
    window_start = jax.random.permutation(key_start, devices)
    offset = jax.random.randint(key_offset, (), 1, devices // 2)
    device_ids = jnp.arange(devices, dtype=jnp.int32)
    first_window = (device_ids[None, :] - window_start[:, None]) % devices < devices // 2
    second_window = (device_ids[None, :] - window_start[:, None] - offset) % devices < devices // 2
    counts = heavy * first_window.astype(jnp.int32) + light * second_window.astype(jnp.int32)
    earlier = jnp.cumsum(counts, 0) - counts
    inclusive = jnp.cumsum(counts, 1)
    own_start = inclusive - counts

    def owner_slots(incl_row, earlier_row, start_row):
        entry = jnp.arange(TOK_DEV, dtype=jnp.int32)
        target = jnp.sum((entry[:, None] >= incl_row[None, :]).astype(jnp.int32), 1)
        selected = target[:, None] == device_ids[None, :]
        before = jnp.sum(jnp.where(selected, earlier_row[None, :], 0), 1)
        begun = jnp.sum(jnp.where(selected, start_row[None, :], 0), 1)
        return target * TOK_DEV + before + entry - begun
    slots = jax.vmap(owner_slots)(inclusive, earlier, own_start)
    shuffle_keys = jax.random.split(key_shuffle, devices)
    shuffled = jax.vmap(lambda one_key, row_slots: jax.random.permutation(one_key, row_slots))(shuffle_keys, slots)
    return shuffled.reshape(TOKEN_TOTAL).astype(jnp.int32)


def block_levels(key, extent, pieces, low, top_value):
    level = 1.0
    for dim, shards_of in pieces:
        draws = jax.random.uniform(jax.random.fold_in(jax.random.fold_in(key, 6), dim), (shards_of,), jnp.float32, low / len(pieces), top_value / len(pieces))
        level = level * jnp.repeat(jnp.exp(draws), extent[dim] // shards_of).reshape((-1,) + (1,) * (len(extent) - 1 - dim))
    return level


def length_profile(amount, total, bound, skew):
    loads = [(1 << 20) // math.isqrt(standing ** skew) + 1 for standing in range(2, amount + 1)]
    spare, given = total - bound - (amount - 1), [1] * (amount - 1)
    while spare > 0:
        free = [i for i in range(amount - 1) if given[i] < bound]
        whole, budget = sum([loads[i] for i in free]), spare
        for i in free:
            addition = min(bound - given[i], max(1, budget * loads[i] // whole), spare)
            given[i] = given[i] + addition
            spare = spare - addition
    return np.array([bound] + given)


def ragged(own_key, amount, total, most, lean):
    if amount == 2:
        one = jax.random.randint(own_key, (), max(1, total - most), min(most, total - 1) + 1)
        return jnp.stack([one, total - one])
    sizes = jnp.asarray(length_profile(amount, total, most, lean), jnp.int32)
    pairs = (amount - 1) // 2
    donor, taker = sizes[1:1 + 2 * pairs:2], sizes[2:2 + 2 * pairs:2]
    slack = jnp.minimum(donor - 1, most - taker)
    shifted = jax.random.randint(jax.random.fold_in(own_key, 1), (pairs,), 0, 1 << 20) % (slack + 1)
    sizes = sizes.at[1:1 + 2 * pairs:2].set(donor - shifted).at[2:2 + 2 * pairs:2].set(taker + shifted)
    return sizes[jax.random.permutation(jax.random.fold_in(own_key, 2), amount)]


def normal_values(stream_key, extent, scale, reach, cuts=(), kind=jnp.bfloat16):
    level = block_levels(stream_key, extent, cuts, -0.22, 0.18) if cuts else 1.0
    array = jax.random.normal(stream_key, extent, jnp.float32) * scale * level
    return jnp.minimum(jnp.maximum(array, -reach), reach).astype(kind)


def setup_inputs(seed: int = 0) -> dict:
    key_of = jax.random.split(jax.random.key(seed), 6)
    return {
        "queries": draw_queries(jax.random.fold_in(key_of[5], 71), 0),
        "keys": draw_keys(jax.random.fold_in(key_of[5], 71), 0),
        "values": normal_values(key_of[2], (TOKEN_TOTAL, KEY_VALUE_HEADS * HEAD_SIZE), 1.0, 6.0, ((0, 128),)),
        "plan": draw_plan(jax.random.fold_in(key_of[5], 71), 0),
        "doc_lengths": jax.vmap(lambda own: ragged(own, DOCS, CYCLE, DOC_MOST, 1))(jax.random.split(key_of[4], CYCLES)).reshape((CYCLES, DOCS)).astype(jnp.int32),
    }


THETA = 500000.0

def apply_rotary(entries, token_position, head_width):
    half_width = head_width // 2
    inv_freq = jnp.exp(-jnp.log(THETA) * (2.0 * jnp.arange(half_width, dtype=jnp.float32) / head_width))
    angles = token_position.astype(jnp.float32)[:, None] * inv_freq[None, :]
    cosine = jnp.cos(angles)[:, None, :]
    sines = jnp.sin(angles)[:, None, :]
    front_half = entries[..., :half_width]
    back_half = entries[..., half_width:]
    return jnp.concatenate([front_half * cosine - back_half * sines, back_half * cosine + front_half * sines], -1)

def locate(cycle_index, lengths):
    doc_ends = jnp.cumsum(lengths).astype(jnp.int32)
    document = lax.optimization_barrier(jnp.sum((cycle_index[:, None] >= doc_ends[None, :]).astype(jnp.int32), 1))
    starts = doc_ends - lengths
    chosen = document[:, None] == jnp.arange(lengths.shape[0], dtype=jnp.int32)[None, :]
    doc_begin = lax.optimization_barrier(jnp.sum(jnp.where(chosen, starts[None, :], 0), 1)).astype(jnp.int32)
    return (document, cycle_index - doc_begin)

def folded_index(position, offset, rows, positions):
    half_rows = rows // 2
    return jnp.where(offset < half_rows, position * half_rows + offset, (2 * positions - 1 - position) * half_rows + offset - half_rows).astype(jnp.int32)

def cycle_attend(q_all, key_value_whole, lengths):
    extent_length = q_all.shape[0]
    head_groups = QUERY_HEADS // KEY_VALUE_HEADS
    row_number = jnp.arange(extent_length, dtype=jnp.int32)
    cycle_index = folded_index(row_number // TOK_DEV, row_number % TOK_DEV, TOK_DEV, N_BLK)
    document, token_position = locate(cycle_index, lengths)
    query_rotated = apply_rotary(q_all.astype(jnp.float32).reshape(extent_length, QUERY_HEADS, HEAD_SIZE), token_position, HEAD_SIZE).astype(jnp.bfloat16)
    query_rotated = query_rotated.reshape(extent_length, KEY_VALUE_HEADS, head_groups, HEAD_SIZE)
    key_rotated = apply_rotary(key_value_whole[:, :KEY_VALUE_HEADS * HEAD_SIZE].astype(jnp.float32).reshape(extent_length, KEY_VALUE_HEADS, HEAD_SIZE), token_position, HEAD_SIZE).astype(jnp.bfloat16)
    value_whole = key_value_whole[:, KEY_VALUE_HEADS * HEAD_SIZE:].reshape(extent_length, KEY_VALUE_HEADS, HEAD_SIZE)
    score_scale = 1.0 / math.sqrt(HEAD_SIZE)

    def one_block(block_start):
        q_part = lax.dynamic_slice_in_dim(query_rotated, block_start, TOK_DEV, 0)
        doc_part = lax.dynamic_slice_in_dim(document, block_start, TOK_DEV, 0)
        index_part = lax.dynamic_slice_in_dim(cycle_index, block_start, TOK_DEV, 0)
        scores = jnp.einsum('qhgd,khd->qhgk', q_part.astype(jnp.float32), key_rotated.astype(jnp.float32)) * score_scale
        allowed = (doc_part[:, None] == document[None, :]) & (index_part[:, None] >= cycle_index[None, :])
        scores = jnp.where(allowed[:, None, None, :], scores, -jnp.inf)
        peak = lax.optimization_barrier(jnp.max(scores, -1, keepdims=True))
        weights = jnp.exp(scores - peak)
        row_total = lax.optimization_barrier(jnp.sum(weights, -1))
        rounded = lax.optimization_barrier(weights.astype(jnp.bfloat16))
        blended = jnp.einsum('qhgk,khd->qhgd', rounded.astype(jnp.float32), value_whole.astype(jnp.float32))
        return (blended / row_total[..., None]).astype(jnp.bfloat16).reshape(TOK_DEV, QUERY_HEADS * HEAD_SIZE)
    block_starts = jnp.arange(N_BLK, dtype=jnp.int32) * TOK_DEV
    return lax.map(one_block, block_starts).reshape(extent_length, QUERY_HEADS * HEAD_SIZE)

def reference(queries, keys, values, plan, doc_lengths):
    extent_length = N_BLK * TOK_DEV
    inverse = jnp.zeros((TOKEN_TOTAL,), jnp.int32).at[plan].set(jnp.arange(TOKEN_TOTAL, dtype=jnp.int32))

    def cycle_view(table):
        table = table[inverse]
        table = table.reshape(N_BLK, N_GROUP, TOK_DEV, table.shape[1])
        return table.transpose(1, 0, 2, 3).reshape(N_GROUP, extent_length, table.shape[3])
    q_cycle = cycle_view(queries)
    kv_cycle = cycle_view(jnp.concatenate([keys, values], 1))
    cycle_out = lax.map(lambda item: cycle_attend(item[0], item[1], item[2]), (q_cycle, kv_cycle, doc_lengths))
    slot_out = cycle_out.reshape(N_GROUP, N_BLK, TOK_DEV, QUERY_HEADS * HEAD_SIZE).transpose(1, 0, 2, 3).reshape(TOKEN_TOTAL, QUERY_HEADS * HEAD_SIZE)
    return slot_out[plan]
```

```python
import math

import jax
import jax.numpy as jnp
from jax import lax
from jax.experimental import pallas as pl
from jax.experimental.pallas import tpu as pltpu
from jax.sharding import PartitionSpec as P

QUERY_HEADS = 32
KEY_VALUE_HEADS = 4
HEAD_SIZE = 128
THETA = 500000.0

TOK = 256
SLOT = 64
KEYS = 512
BLOCK = 256
TILE = 32
SUPER = 256
HALF = QUERY_HEADS // 2 * HEAD_SIZE
WIDE = HALF + 128
ROWS = 16 * SLOT
NEG = -1e30
SCALE = math.log2(math.e) / math.sqrt(HEAD_SIZE)
MESH = pl.DeviceIdType.MESH
VMEM_LIMIT = 60 * 1024 * 1024


def coords():
    b = lax.axis_index("blk")
    g = lax.axis_index("group")
    return b // 4, g % 4, (b // 2) % 2 * 2 + g // 4, b % 2


def device(x, y, z, core):
    x, y, z = lax.rem(x + 4, 4), lax.rem(y + 4, 4), lax.rem(z + 4, 4)
    return x * 4 + z // 2 * 2 + core, lax.rem(z, 2) * 4 + y


def moved(sign, delta, core):
    x, y, z, _ = coords()
    return device(x + sign * (delta // 4), y + sign * (delta // 2 % 2), z + sign * (delta % 2), core)


def opposite(bit):
    x, y, z, core = coords()
    return device(x + 2 * (bit == 4), y + 2 * (bit == 2), z + 2 * (bit == 1), core)


def sign_of(core):
    return 1 - 2 * core


def signal(target):
    pl.semaphore_signal(pltpu.get_barrier_semaphore(), inc=1, device_id=target, device_id_type=MESH)


def remote(src, dst, send, recv, target):
    return pltpu.make_async_remote_copy(
        src_ref=src, dst_ref=dst, send_sem=send, recv_sem=recv, device_id=target, device_id_type=MESH
    )


THIRDS = ((0, 176, (4, 2, 1)), (176, 176, (2, 1, 4)), (352, 160, (1, 4, 2)))


def exchange_kernel(q_ref, kv_ref, got_ref, all_ref, q_send, q_recv, kv_send, kv_recv, local_sem):
    x, y, z, core = coords()
    place = x // 2 * 4 + y // 2 * 2 + z // 2
    mine = sign_of(core)
    other = 1 - core

    for delta in range(1, 8):
        for source in range(2):
            signal(moved(-sign_of(source), delta, source))
    signal(moved(0, 0, other))
    for bit in (4, 2, 1):
        signal(opposite(bit))
    pl.semaphore_wait(pltpu.get_barrier_semaphore(), 18)

    own_q = pltpu.make_async_copy(
        q_ref.at[0, :, pl.ds(pl.multiple_of(core * WIDE, 128), WIDE)], got_ref.at[0, core], local_sem.at[0]
    )
    own_kv = pltpu.make_async_copy(kv_ref, all_ref.at[place], local_sem.at[1])
    own_kv.start()
    own_q.start()

    def flip(mask):
        out = 0
        for bit in (4, 2, 1):
            digit = place // bit % 2
            out = out + bit * ((1 - digit) if mask & bit else digit)
        return out

    def kv_copy(third, index):
        start, size, (b1, b2, b3) = THIRDS[third]
        mask, axis = ((0, b1), (0, b2), (0, b3), (b1, b2), (b1, b3), (b2, b3), (b1 ^ b2, b3))[index]
        rows = pl.ds(start, size)
        block = flip(mask)
        src = kv_ref.at[rows] if mask == 0 else all_ref.at[block, rows]
        return remote(
            src, all_ref.at[block, rows], kv_send.at[third, index], kv_recv.at[third, index], opposite(axis)
        )

    def kv_landed(third, index):
        start, size, (b1, b2, b3) = THIRDS[third]
        mask = (b1, b2, b3, b1 ^ b2, b1 ^ b3, b2 ^ b3, 7)[index]
        here = all_ref.at[flip(mask), pl.ds(start, size)]
        remote(here, here, kv_send.at[third, index], kv_recv.at[third, index], opposite(4)).wait_recv()

    copies = []

    def start(copy):
        copy.start()
        copies.append(copy)

    for index in range(3):
        for third in range(3):
            start(kv_copy(third, index))

    def q_copy(delta, to_core, target):
        columns = pl.ds(pl.multiple_of(to_core * WIDE, 128), WIDE)
        slot = delta * 2 + to_core if delta else 0
        return remote(
            q_ref.at[delta, :, columns], got_ref.at[delta, core], q_send.at[slot], q_recv.at[delta, core], target
        )

    start(q_copy(0, other, moved(0, 0, other)))
    for delta in (7, 6, 5, 3, 4, 2, 1):
        for to_core in range(2):
            start(q_copy(delta, to_core, moved(mine, delta, to_core)))

    for third in range(3):
        kv_landed(third, 0)
        start(kv_copy(third, 3))
        start(kv_copy(third, 4))
    for third in range(3):
        kv_landed(third, 1)
        start(kv_copy(third, 5))
    for third in range(3):
        kv_landed(third, 3)
        start(kv_copy(third, 6))
    for index in (2, 4, 5, 6):
        for third in range(3):
            kv_landed(third, index)

    def q_landed(delta, source):
        here = got_ref.at[delta, source]
        remote(here, here, q_send.at[0], q_recv.at[delta, source], moved(0, 0, other)).wait_recv()

    q_landed(0, other)
    for delta in range(1, 8):
        for source in range(2):
            q_landed(delta, source)
    own_q.wait()
    own_kv.wait()
    for copy in copies:
        copy.wait_send()


def exchange(q, kv):
    return pl.pallas_call(
        exchange_kernel,
        out_shape=(
            jax.ShapeDtypeStruct((8, 2, SLOT, WIDE), jnp.bfloat16),
            jax.ShapeDtypeStruct((8, KEYS, 512), jnp.bfloat16),
        ),
        in_specs=[pl.BlockSpec(memory_space=pl.ANY)] * 2,
        out_specs=[pl.BlockSpec(memory_space=pl.ANY)] * 2,
        scratch_shapes=[
            pltpu.SemaphoreType.DMA((16,)),
            pltpu.SemaphoreType.DMA((8, 2)),
            pltpu.SemaphoreType.DMA((3, 7)),
            pltpu.SemaphoreType.DMA((3, 7)),
            pltpu.SemaphoreType.DMA((2,)),
        ],
        compiler_params=pltpu.CompilerParams(collective_id=0, has_side_effects=True),
        name="exchange",
    )(q, kv)


def back_kernel(out_ref, ret_ref, send, recv, local_sem):
    x, y, z, core = coords()
    mine = sign_of(core)
    other = 1 - core
    for delta in range(1, 8):
        for worker in range(2):
            signal(moved(mine, delta, worker))
    signal(moved(0, 0, other))
    pl.semaphore_wait(pltpu.get_barrier_semaphore(), 15)

    columns = pl.ds(pl.multiple_of(core * HALF, 128), HALF)
    own = pltpu.make_async_copy(out_ref.at[0, core], ret_ref.at[0, :, columns], local_sem)
    own.start()
    copies = [
        remote(
            out_ref.at[0, other],
            ret_ref.at[0, :, columns],
            send.at[0],
            recv.at[0, core],
            moved(0, 0, other),
        )
    ]
    for delta in (7, 6, 5, 3, 4, 2, 1):
        for source in range(2):
            copies.append(
                remote(
                    out_ref.at[delta, source],
                    ret_ref.at[delta, :, columns],
                    send.at[delta * 2 + source],
                    recv.at[delta, core],
                    moved(-sign_of(source), delta, source),
                )
            )
    for copy in copies:
        copy.start()

    def landed(delta, worker):
        here = ret_ref.at[delta, :, pl.ds(pl.multiple_of(worker * HALF, 128), HALF)]
        remote(here, here, send.at[0], recv.at[delta, worker], moved(0, 0, other)).wait_recv()

    landed(0, other)
    for delta in range(1, 8):
        for worker in range(2):
            landed(delta, worker)
    own.wait()
    for copy in copies:
        copy.wait_send()


def back(out):
    return pl.pallas_call(
        back_kernel,
        out_shape=jax.ShapeDtypeStruct((8, SLOT, 2 * HALF), jnp.bfloat16),
        in_specs=[pl.BlockSpec(memory_space=pl.ANY)],
        out_specs=pl.BlockSpec(memory_space=pl.ANY),
        scratch_shapes=[
            pltpu.SemaphoreType.DMA((16,)),
            pltpu.SemaphoreType.DMA((8, 2)),
            pltpu.SemaphoreType.DMA(()),
        ],
        compiler_params=pltpu.CompilerParams(collective_id=1, has_side_effects=True),
        name="back",
    )(out)


def attend_kernel(
    low_ref, high_ref, count_ref, rank_row, rank_col, u_ref, begin_ref, cos_ref, sin_ref, q_ref, kv_ref,
    out_ref, turned, made, peak, total,
):
    ones = jnp.ones((BLOCK, HEAD_SIZE), jnp.bfloat16)
    out_ref[...] = jnp.zeros_like(out_ref)
    lanes = lax.broadcasted_iota(jnp.int32, (TILE * 8, BLOCK), 1)

    def one_super(sup, carry):
        base = pl.multiple_of(sup * SUPER, SUPER)
        pick = (
            lax.broadcasted_iota(jnp.int32, (SUPER, ROWS), 0) + base == rank_row[...]
        ).astype(jnp.bfloat16)
        cos = cos_ref[pl.ds(base, SUPER), :]
        sin = sin_ref[pl.ds(base, SUPER), :]
        for head in range(2):
            for part in range(2):
                columns = slice(head * 1024 + part * 512, head * 1024 + part * 512 + 512)
                rows = jnp.dot(pick, q_ref[:, columns], preferred_element_type=jnp.float32)
                for one in range(4):
                    entry = rows[:, one * HEAD_SIZE : (one + 1) * HEAD_SIZE]
                    entry = entry * cos + pltpu.roll(entry, HEAD_SIZE // 2, 1) * sin
                    turned[head, part * 4 + one] = entry.astype(jnp.bfloat16)

        def one_tile(tile, carry):
            first = pl.multiple_of(tile * TILE, TILE)
            where = pl.multiple_of(base + first, TILE)
            low = low_ref[sup * (SUPER // TILE) + tile]
            high = high_ref[sup * (SUPER // TILE) + tile]
            begin = begin_ref[pl.ds(where, TILE), :]
            begin = jnp.concatenate([begin] * 8, 0)
            last = u_ref[pl.ds(where, TILE), :]
            last = jnp.concatenate([last] * 8, 0)
            peak[...] = jnp.full_like(peak, NEG)
            total[...] = jnp.zeros_like(total)

            def one_block(block, carry):
                holder = jnp.where(block < 8, block, 15 - block)
                rows = pl.ds(pl.multiple_of(jnp.where(block < 8, 0, BLOCK), BLOCK), BLOCK)
                place = lanes + block * BLOCK
                allowed = (place >= begin) & (place <= last)
                for head in range(2):
                    query = turned[head, :, pl.ds(first, TILE), :].reshape(TILE * 8, HEAD_SIZE)
                    key = kv_ref[holder, rows, head * HEAD_SIZE : (head + 1) * HEAD_SIZE]
                    value = kv_ref[holder, rows, (2 + head) * HEAD_SIZE : (3 + head) * HEAD_SIZE]
                    score = lax.dot_general(
                        query, key, (((1,), (1,)), ((), ())), preferred_element_type=jnp.float32
                    )
                    score = jnp.where(allowed, score, NEG)
                    old = peak[head]
                    new = jnp.maximum(old, jnp.max(score, 1, keepdims=True))
                    weight = jnp.exp2(score - jnp.concatenate([new, new], 1)).astype(jnp.bfloat16)
                    decay = jnp.exp2(old - new)
                    peak[head] = new
                    total[head] = total[head] * jnp.concatenate([decay, decay], 1) + jnp.dot(
                        weight, jnp.concatenate([value, ones], 1), preferred_element_type=jnp.float32
                    )
                return carry

            lax.fori_loop(low, high + 1, one_block, 0)
            for head in range(2):
                result = total[head, :, :HEAD_SIZE] / jnp.maximum(total[head, :, HEAD_SIZE:], 1e-30)
                result = result.astype(jnp.bfloat16)
                for one in range(8):
                    made[pl.ds(first, TILE), pl.ds((head * 8 + one) * HEAD_SIZE, HEAD_SIZE)] = result[
                        one * TILE : (one + 1) * TILE
                    ]
            return carry

        lax.fori_loop(0, SUPER // TILE, one_tile, 0)
        put = (
            lax.broadcasted_iota(jnp.int32, (ROWS, SUPER), 1) + base == rank_col[...]
        ).astype(jnp.bfloat16)
        for part in range(4):
            columns = slice(part * 512, part * 512 + 512)
            out_ref[:, columns] += jnp.dot(put, made[:, columns], preferred_element_type=jnp.float32).astype(
                jnp.bfloat16
            )
        return carry

    lax.fori_loop(0, count_ref[0], one_super, 0)


def attend(low, high, count, rank, u, begin, cos, sin, q, kv):
    smem = pl.BlockSpec(memory_space=pltpu.SMEM)
    vmem = pl.BlockSpec(memory_space=pltpu.VMEM)
    return pl.pallas_call(
        attend_kernel,
        out_shape=jax.ShapeDtypeStruct((ROWS, HALF), jnp.bfloat16),
        in_specs=[smem] * 3 + [vmem] * 8,
        out_specs=vmem,
        scratch_shapes=[
            pltpu.VMEM((2, 8, SUPER, HEAD_SIZE), jnp.bfloat16),
            pltpu.VMEM((SUPER, HALF), jnp.bfloat16),
            pltpu.VMEM((2, TILE * 8, HEAD_SIZE), jnp.float32),
            pltpu.VMEM((2, TILE * 8, 2 * HEAD_SIZE), jnp.float32),
        ],
        compiler_params=pltpu.CompilerParams(vmem_limit_bytes=VMEM_LIMIT),
        name="attend",
    )(low, high, count, rank[None, :], rank[:, None], u[:, None], begin[:, None], cos, sin, q, kv)


def document_start(u, lengths):
    ends = jnp.cumsum(lengths)
    return jnp.sum(jnp.where(u[:, None] >= ends[None, :], lengths[None, :], 0), 1)


def angles_of(position):
    half = HEAD_SIZE // 2
    inv_freq = jnp.exp(-jnp.log(THETA) * (2.0 * jnp.arange(half, dtype=jnp.float32) / HEAD_SIZE))
    angle = position.astype(jnp.float32)[:, None] * inv_freq[None, :]
    return jnp.cos(angle), jnp.sin(angle)


def one_hot(index, size):
    return (jnp.arange(size, dtype=jnp.int32)[:, None] == index[None, :]).astype(jnp.bfloat16)


def local(queries, keys, values, plan, doc_lengths):
    x, y, z, core = coords()
    my_cycle = x % 2 * 4 + y % 2 * 2 + z % 2
    my_place = x // 2 * 4 + y // 2 * 2 + z // 2

    owner = plan // TOK
    cycle = owner % 8
    p = owner // 8
    offset = plan % TOK
    front = offset < 128
    u = jnp.where(front, p * 128 + offset, (31 - p) * 128 + offset - 128)
    place = p // 2
    row = jnp.where(front, p % 2 * 128 + offset, 256 + (1 - p % 2) * 128 + offset - 128)
    order = jnp.arange(TOK, dtype=jnp.int32)
    earlier = order[None, :] < order[:, None]
    rank_slot = jnp.sum((earlier & (owner[:, None] == owner[None, :])).astype(jnp.int32), 1)
    rank_cycle = jnp.sum((earlier & (cycle[:, None] == cycle[None, :])).astype(jnp.int32), 1)
    to_x = place // 4 * 2 + cycle // 4
    to_y = place // 2 % 2 * 2 + cycle // 2 % 2
    to_z = place % 2 * 2 + cycle % 2
    chip = (to_x * 2 + to_z // 2) * 8 + to_z % 2 * 4 + to_y
    send_kv = one_hot(chip * 8 + p % 2 * 4 + rank_slot, 512)
    delta = jnp.bitwise_xor(cycle, my_cycle)
    send_q = one_hot(delta * SLOT + rank_cycle, 8 * SLOT)

    fields = jnp.stack([jnp.where(row < 256, row + 1, 0), jnp.where(row < 256, 0, row - 255)], 1)
    fields = jnp.pad(fields, ((0, 0), (0, 126))).astype(jnp.bfloat16)
    lengths = doc_lengths[0]
    known = jnp.concatenate([lengths // 256, lengths % 256])
    known = jnp.pad(known, (512 + 2, 128 - 2 - 8)).astype(jnp.bfloat16)
    halves = []
    for half in range(2):
        columns = slice(half * 256, half * 256 + 256)
        table = jnp.concatenate([keys[:, columns], values[:, columns], fields], 1)
        sent = jnp.dot(send_kv, table, preferred_element_type=jnp.float32).astype(jnp.bfloat16)
        halves.append((sent + known[None, :]).reshape(8, 1, 8, 8, 640))
    got = lax.all_to_all(
        jnp.concatenate(halves, 1).reshape(128, 8, 640),
        ("blk", "group"),
        split_axis=0,
        concat_axis=0,
        tiled=True,
    )
    known = lax.dynamic_slice(got, (my_cycle, 0, 512 + 2), (1, 1, 8)).reshape(8).astype(jnp.int32)
    lengths = known[:4] * 256 + known[4:]
    got = got.reshape(1024, 640)
    lower = got[:, 512].astype(jnp.int32)
    upper = got[:, 513].astype(jnp.int32)
    row = jnp.where(lower > 0, lower - 1, jnp.where(upper > 0, upper + 255, -1))
    kv = jnp.dot(one_hot(row, KEYS), got[:, :512], preferred_element_type=jnp.float32)
    rows = jnp.arange(KEYS, dtype=jnp.int32)
    key_u = jnp.where(rows < 256, my_place * 256 + rows, (15 - my_place) * 256 + rows - 256)
    cosine, sine = angles_of(key_u - document_start(key_u, lengths))
    cosine, sine = cosine[:, None, :], sine[:, None, :]
    k = kv[:, :256].reshape(KEYS, 2, HEAD_SIZE)
    a, b = k[..., :64], k[..., 64:]
    k = jnp.concatenate([a * cosine - b * sine, b * cosine + a * sine], -1)
    kv = jnp.concatenate([k.reshape(KEYS, 256), kv[:, 256:]], 1).astype(jnp.bfloat16)

    fields = jnp.pad(jnp.stack([u // 256 + 1, u % 256], 1), ((0, 0), (0, 126))).astype(jnp.bfloat16)
    table = jnp.concatenate([queries[:, :HALF], fields, queries[:, HALF:], fields], 1)
    q = jnp.dot(send_q, table, preferred_element_type=jnp.float32).astype(jnp.bfloat16)
    q, kv = exchange(q.reshape(8, SLOT, 2 * WIDE), kv)
    q = q.reshape(ROWS, WIDE)

    lead = q[:, HALF].astype(jnp.int32)
    u = (lead - 1) * 256 + q[:, HALF + 1].astype(jnp.int32)
    valid = lead > 0
    index = jnp.arange(ROWS, dtype=jnp.int32)
    sort_key = jnp.where(valid, u, 4096 + index)
    rank = jnp.sum((sort_key[None, :] < sort_key[:, None]).astype(jnp.int32), 1)
    sorted_u = jnp.sum(jnp.where(index[:, None] == rank[None, :], sort_key[None, :], 0), 1)
    count = jnp.sum(valid.astype(jnp.int32))
    live = sorted_u < 4096
    begin = jnp.where(live, document_start(sorted_u, lengths), 8192)
    cosine, sine = angles_of(jnp.where(live, sorted_u - begin, 0))
    cosine = jnp.concatenate([cosine, cosine], 1) * SCALE
    sine = jnp.concatenate([-sine, sine], 1) * SCALE
    low = jnp.where(live, begin // BLOCK, 0).reshape(ROWS // TILE, TILE)[:, 0]
    high = jnp.max(jnp.where(live, sorted_u // BLOCK, -1).reshape(ROWS // TILE, TILE), 1)
    supers = (count + SUPER - 1) // SUPER
    out = attend(low, high, supers.reshape(1), rank, sorted_u, begin, cosine, sine, q, kv)

    ret = back(out.reshape(8, 2, SLOT, HALF)).reshape(8 * SLOT, 2 * HALF)
    return lax.dot_general(
        send_q, ret, (((0,), (0,)), ((), ())), preferred_element_type=jnp.float32
    ).astype(jnp.bfloat16)


def solution(mesh):
    return jax.shard_map(
        local,
        mesh=mesh,
        in_specs=(
            P(("blk", "group"), None),
            P(("blk", "group"), None),
            P(("blk", "group"), None),
            P(("blk", "group")),
            P("group", None),
        ),
        out_specs=P(("blk", "group"), None),
        check_vma=False,
    )
```

```python
import math

import jax
import jax.numpy as jnp
from jax import lax
from jax.experimental import pallas as pl
from jax.experimental.pallas import tpu as pltpu
from jax.sharding import PartitionSpec as P

QUERY_HEADS = 32
KEY_VALUE_HEADS = 4
HEAD_SIZE = 128
THETA = 500000.0

TOK = 256
SLOT = 64
KEYS = 512
BLOCK = 256
TILE = 32
SUPER = 256
HALF = QUERY_HEADS // 2 * HEAD_SIZE
WIDE = HALF + 128
ROWS = 16 * SLOT
NEG = -1e30
SCALE = math.log2(math.e) / math.sqrt(HEAD_SIZE)
MESH = pl.DeviceIdType.MESH
VMEM_LIMIT = 60 * 1024 * 1024


def coords():
    b = lax.axis_index("blk")
    g = lax.axis_index("group")
    return b // 4, g % 4, (b // 2) % 2 * 2 + g // 4, b % 2


def device(x, y, z, core):
    x, y, z = lax.rem(x + 4, 4), lax.rem(y + 4, 4), lax.rem(z + 4, 4)
    return x * 4 + z // 2 * 2 + core, lax.rem(z, 2) * 4 + y


def moved(sign, delta, core):
    x, y, z, _ = coords()
    return device(x + sign * (delta // 4), y + sign * (delta // 2 % 2), z + sign * (delta % 2), core)


def sign_of(core):
    return 1 - 2 * core


def signal(target):
    pl.semaphore_signal(pltpu.get_barrier_semaphore(), inc=1, device_id=target, device_id_type=MESH)


def remote(src, dst, send, recv, target):
    return pltpu.make_async_remote_copy(
        src_ref=src, dst_ref=dst, send_sem=send, recv_sem=recv, device_id=target, device_id_type=MESH
    )


THIRDS = ((0, 176, (4, 2, 1)), (176, 176, (2, 1, 4)), (352, 160, (1, 4, 2)))
PAIR = 640
PART = 128


def iota(shape, axis):
    return lax.broadcasted_iota(jnp.int32, shape, axis)


def bf16(flags):
    return jnp.where(flags, 1.0, 0.0).astype(jnp.bfloat16)


def dot(a, b):
    return jnp.dot(a, b, preferred_element_type=jnp.float32)


def cycle_of(plan):
    return (plan >> 8) & 7


def cycle_index(plan):
    p = plan >> 11
    offset = plan & 255
    return jnp.where(offset < 128, p * 128 + offset, (31 - p) * 128 + offset - 128)


def document_start(u, lengths):
    end = jnp.zeros((1, 1), jnp.int32)
    start = jnp.zeros_like(u)
    for one in range(4):
        length = lengths[0:1, one : one + 1]
        end = end + length
        start = start + jnp.where(u >= end, length, 0)
    return start


def turning(position):
    half = HEAD_SIZE // 2
    lane = iota((1, HEAD_SIZE), 1)
    spot = (lane & (half - 1)).astype(jnp.float32)
    inv_freq = jnp.exp(-math.log(THETA) * (2.0 * spot / HEAD_SIZE))
    angle = position.astype(jnp.float32) * inv_freq
    both = jnp.cos(jnp.where(lane < half, angle, angle - math.pi / 2))
    other = pltpu.roll(both, half, 1)
    first = jnp.broadcast_to(lane < half, both.shape)
    return jnp.where(first, both, other), jnp.where(first, -other, both)


def exchange_kernel(
    queries_ref, keys_ref, values_ref, plan_col, plan_row, lengths_ref,
    sorted_ref, all_ref, places_ref, rank_ref,
    q_out, q_got, kv_out, kv_got, part_out, part_got, own_ref, len_got, key_ref, cos_ref, sin_ref,
    q_send, q_recv, a_send, a_recv, b_send, b_recv, kv_send, kv_recv, len_send, len_recv, local_sem,
):
    x, y, z, core = coords()
    place = x // 2 * 4 + y // 2 * 2 + z // 2
    my_cycle = x % 2 * 4 + y % 2 * 2 + z % 2
    mine = sign_of(core)
    other = 1 - core

    block_at, group_at = lax.axis_index("blk"), lax.axis_index("group")
    spot = block_at // 2
    to_device = device(
        spot // 4 * 2 + group_at // 4, spot // 2 % 2 * 2 + group_at // 2 % 2, spot % 2 * 2 + group_at % 2, block_at % 2
    )
    from_block = place * 2 + core
    at_home = (from_block == block_at) & (my_cycle == group_at)

    for delta in range(1, 8):
        for source in range(2):
            signal(moved(-sign_of(source), delta, source))
    signal(moved(0, 0, other))
    for mask in range(1, 8):
        signal(across_cycle(mask))

    @pl.when(jnp.logical_not(at_home))
    def _():
        signal((from_block, my_cycle))

    plan_c, plan_r = plan_col[...], plan_row[...]
    same = (cycle_of(plan_c) == cycle_of(plan_r)) & (iota((TOK, TOK), 0) < iota((TOK, TOK), 1))
    rank = jnp.sum(jnp.where(same, 1, 0), 0, keepdims=True)
    row = jnp.bitwise_xor(cycle_of(plan_r), my_cycle) * SLOT + rank
    choose = bf16(iota((8 * SLOT, TOK), 0) == row)
    u = cycle_index(plan_c)
    lane = iota((TOK, 128), 1)
    fields = jnp.where(lane == 0, (u >> 8) + 1, jnp.where(lane == 1, u & 255, 0))
    fields = fields.astype(jnp.float32).astype(jnp.bfloat16)
    chosen_k = dot(choose, keys_ref[...]).astype(jnp.bfloat16)
    chosen_v = dot(choose, values_ref[...]).astype(jnp.bfloat16)
    chosen_f = dot(choose, fields).astype(jnp.bfloat16)
    for delta in range(8):
        rows = slice(delta * SLOT, (delta + 1) * SLOT)
        for half in range(2):
            kv_out[delta, :, half * PAIR : half * PAIR + 256] = chosen_k[rows, half * 256 : half * 256 + 256]
            kv_out[delta, :, half * PAIR + 256 : half * PAIR + 512] = chosen_v[rows, half * 256 : half * 256 + 256]
            kv_out[delta, :, half * PAIR + 512 : half * PAIR + 640] = chosen_f[rows, :]

    pl.semaphore_wait(pltpu.get_barrier_semaphore(), jnp.where(at_home, 22, 23))

    copies = []

    def start(copy):
        copy.start()
        copies.append(copy)

    def lengths_copy():
        return remote(lengths_ref, len_got, len_send, len_recv, to_device)

    @pl.when(jnp.logical_not(at_home))
    def _():
        lengths_copy().start()

    def out_copy(src, dst, send, recv, width, delta, to_core):
        columns = pl.ds(pl.multiple_of(to_core * width, 128), width)
        slot = delta * 2 + to_core if delta else 0
        return remote(
            src.at[delta, :, columns],
            dst.at[delta, core],
            send.at[slot],
            recv.at[delta, core],
            moved(mine, delta, to_core) if delta else moved(0, 0, other),
        )

    def landed(dst, send, recv, delta, source):
        here = dst.at[delta, source]
        remote(here, here, send.at[0], recv.at[delta, source], moved(0, 0, other)).wait_recv()

    order = (7, 6, 5, 3, 4, 2, 1)
    start(out_copy(kv_out, kv_got, a_send, a_recv, PAIR, 0, other))
    for delta in order:
        for to_core in range(2):
            start(out_copy(kv_out, kv_got, a_send, a_recv, PAIR, delta, to_core))
    own_a = pltpu.make_async_copy(
        kv_out.at[0, :, pl.ds(pl.multiple_of(core * PAIR, 128), PAIR)], kv_got.at[0, core], local_sem.at[0]
    )
    own_a.start()

    for part in range(8):
        columns = slice(part * 512, part * 512 + 512)
        chosen = dot(choose, queries_ref[:, columns]).astype(jnp.bfloat16)
        for delta in range(8):
            q_out[delta, :, columns] = chosen[delta * SLOT : (delta + 1) * SLOT, :]
    start(out_copy(q_out, q_got, q_send, q_recv, HALF, 0, other))
    for delta in order:
        for to_core in range(2):
            start(out_copy(q_out, q_got, q_send, q_recv, HALF, delta, to_core))
    own_q = pltpu.make_async_copy(
        q_out.at[0, :, pl.ds(pl.multiple_of(core * HALF, 128), HALF)], q_got.at[0, core], local_sem.at[1]
    )
    own_q.start()

    own_a.wait()
    landed(kv_got, a_send, a_recv, 0, other)
    for delta in range(1, 8):
        for source in range(2):
            landed(kv_got, a_send, a_recv, delta, source)

    def fields_of(table):
        fields = table.reshape(ROWS, 128).astype(jnp.float32)
        flat = fields.T
        out = []
        for lead, low in ((fields[:, 0:1], fields[:, 1:2]), (flat[0:1, :], flat[1:2, :])):
            lead = lead.astype(jnp.int32)
            out.append((lead > 0, (lead - 1) * 256 + low.astype(jnp.int32)))
        return out

    def holder_of(u):
        block = u >> 8
        return jnp.where(block < 8, block, 15 - block)

    (valid_c, u_c), (valid_r, u_r) = fields_of(kv_got[:, :, :, 512:])
    key_c = jnp.where(valid_c, holder_of(u_c), -1)
    key_r = jnp.where(valid_r, holder_of(u_r), -2)
    key_ref[...] = jnp.broadcast_to(key_c, (ROWS, 128))

    def count_before(step, total):
        base = pl.multiple_of(step * 128, 128)
        chunk = key_ref[pl.ds(base, 128), 0:1]
        hits = (chunk == key_r) & (iota((128, ROWS), 0) + base < iota((128, ROWS), 1))
        return total + jnp.sum(jnp.where(hits, 1, 0), 0, keepdims=True)

    before = lax.fori_loop(0, ROWS // 128, count_before, jnp.zeros((1, ROWS), jnp.int32))
    target = jnp.where(valid_r, key_r * PART + before, -1)

    def fill(step, carry):
        base = pl.multiple_of(step * PART, PART)
        part_out[step] = dot(bf16(iota((PART, ROWS), 0) + base == target), kv_got[...].reshape(ROWS, PAIR)).astype(
            jnp.bfloat16
        )
        return carry

    lax.fori_loop(0, 8, fill, 0)

    def flip(mask):
        out = 0
        for bit in (4, 2, 1):
            digit = place // bit % 2
            out = out + bit * ((1 - digit) if mask & bit else digit)
        return out

    for mask in order:
        start(
            remote(
                part_out.at[flip(mask)], part_got.at[place], b_send.at[mask], b_recv.at[mask], across_cycle(mask)
            )
        )
    part_got[place] = part_out[place]

    index_c, index_r = iota((ROWS, 1), 0), iota((1, ROWS), 1)
    key_c = jnp.where(valid_c, u_c, 4096 + index_c)
    key_r = jnp.where(valid_r, u_r, 4096 + index_r)
    key_ref[...] = jnp.broadcast_to(key_c, (ROWS, 128))

    def rank_step(step, total):
        base = pl.multiple_of(step * 128, 128)
        chunk = key_ref[pl.ds(base, 128), 0:1]
        counts = jnp.sum(jnp.where(key_r < chunk, 1, 0), 1, keepdims=True)
        rank_ref[pl.ds(base, 128), :] = jnp.broadcast_to(counts, (128, 128))
        return total + jnp.sum(jnp.where(chunk < key_r, 1, 0), 0, keepdims=True)

    rank_r = lax.fori_loop(0, ROWS // 128, rank_step, jnp.zeros((1, ROWS), jnp.int32))

    def sort_step(step, total):
        base = pl.multiple_of(step * 128, 128)
        chunk = key_ref[pl.ds(base, 128), 0:1]
        ranks = rank_ref[pl.ds(base, 128), 0:1]
        return total + jnp.sum(jnp.where(ranks == iota((128, ROWS), 1), chunk, 0), 0, keepdims=True)

    sorted_r = lax.fori_loop(0, ROWS // 128, sort_step, jnp.zeros((1, ROWS), jnp.int32))

    @pl.when(at_home)
    def _():
        len_got[...] = lengths_ref[...]

    @pl.when(jnp.logical_not(at_home))
    def _():
        lengths_copy().wait()

    lengths = len_got[...]
    places_ref[0:1, :] = sorted_r
    places_ref[1:2, :] = jnp.where(sorted_r < 4096, document_start(sorted_r, lengths), 8192)
    places_ref[2:8, :] = jnp.zeros((6, ROWS), jnp.int32)

    def turn_step(step, carry):
        base = pl.multiple_of(step * 128, 128)
        hits = iota((128, ROWS), 0) + base == rank_r
        u = jnp.sum(jnp.where(hits, key_r, 0), 1, keepdims=True)
        u = jnp.where(u < 4096, u, 0)
        cos, sin = turning(u - document_start(u, lengths))
        cos_ref[pl.ds(base, 128), :] = cos * SCALE
        sin_ref[pl.ds(base, 128), :] = sin * SCALE
        return carry

    lax.fori_loop(0, ROWS // 128, turn_step, 0)
    rows_c = iota((KEYS, 1), 0)
    key_u = jnp.where(rows_c < BLOCK, place * BLOCK + rows_c, (15 - place) * BLOCK + rows_c - BLOCK)
    key_cos, key_sin = turning(key_u - document_start(key_u, lengths))

    for mask in range(1, 8):
        here = part_got.at[flip(mask)]
        remote(here, here, b_send.at[mask], b_recv.at[mask], across_cycle(mask)).wait_recv()

    _, (valid, u) = fields_of(part_got[:, :, 512:])
    target = jnp.where(valid, jnp.where(u >= 2048, BLOCK, 0) + (u & 255), -1)
    placed = dot(bf16(iota((KEYS, ROWS), 0) == target), part_got[:, :, :512].reshape(ROWS, 512))
    for head in range(2):
        columns = slice(head * HEAD_SIZE, (head + 1) * HEAD_SIZE)
        entry = placed[:, columns]
        entry = entry * key_cos + pltpu.roll(entry, HEAD_SIZE // 2, 1) * key_sin
        own_ref[:, columns] = entry.astype(jnp.bfloat16)
    for half in range(2):
        rows = slice(half * BLOCK, (half + 1) * BLOCK)
        own_ref[rows, 256:] = placed[rows, 256:].T.astype(jnp.bfloat16)

    own_kv = pltpu.make_async_copy(own_ref, all_ref.at[place], local_sem.at[2])
    own_kv.start()

    def kv_copy(third, index):
        start, size, (b1, b2, b3) = THIRDS[third]
        mask, axis = ((0, b1), (0, b2), (0, b3), (b1, b2), (b1, b3), (b2, b3), (b1 ^ b2, b3))[index]
        rows = pl.ds(start, size)
        block = flip(mask)
        src = own_ref.at[rows] if mask == 0 else all_ref.at[block, rows]
        return remote(
            src, all_ref.at[block, rows], kv_send.at[third, index], kv_recv.at[third, index], across_cycle(axis)
        )

    def kv_landed(third, index):
        start, size, (b1, b2, b3) = THIRDS[third]
        mask = (b1, b2, b3, b1 ^ b2, b1 ^ b3, b2 ^ b3, 7)[index]
        here = all_ref.at[flip(mask), pl.ds(start, size)]
        remote(here, here, kv_send.at[third, index], kv_recv.at[third, index], across_cycle(4)).wait_recv()

    for index in range(3):
        for third in range(3):
            start(kv_copy(third, index))

    landed(q_got, q_send, q_recv, 0, other)
    for delta in range(1, 8):
        for source in range(2):
            landed(q_got, q_send, q_recv, delta, source)
    own_q.wait()

    def order_queries(sup):
        base = sup * SUPER
        pick = bf16(iota((SUPER, ROWS), 0) + base == rank_r)
        cos = cos_ref[base : base + SUPER, :]
        sin = sin_ref[base : base + SUPER, :]

        def one_part(part, carry):
            columns = pl.ds(pl.multiple_of(part * 256, 256), 256)
            rows = dot(pick, q_got[:, :, :, columns].reshape(ROWS, 256))
            for one in range(2):
                entry = rows[:, one * HEAD_SIZE : (one + 1) * HEAD_SIZE]
                entry = entry * cos + pltpu.roll(entry, HEAD_SIZE // 2, 1) * sin
                entry = entry.astype(jnp.bfloat16)
                first = pl.multiple_of((part % 4 * 2 + one) * TILE, TILE)
                for tile in range(SUPER // TILE):
                    sorted_ref[part // 4, sup * (SUPER // TILE) + tile, pl.ds(first, TILE), :] = entry[
                        tile * TILE : (tile + 1) * TILE
                    ]
            return carry

        lax.fori_loop(0, 8, one_part, 0)

    for third in range(3):
        kv_landed(third, 0)
        start(kv_copy(third, 3))
        start(kv_copy(third, 4))
    for third in range(3):
        kv_landed(third, 1)
        start(kv_copy(third, 5))
    order_queries(0)
    for third in range(3):
        kv_landed(third, 3)
        start(kv_copy(third, 6))
    for sup in range(1, 4):
        order_queries(sup)
    for index in (2, 4, 5, 6):
        for third in range(3):
            kv_landed(third, index)
    own_kv.wait()
    for copy in copies:
        copy.wait_send()


def across_cycle(mask):
    x, y, z, core = coords()
    return device(x + 2 * (mask // 4), y + 2 * (mask // 2 % 2), z + 2 * (mask % 2), core)


def exchange(queries, keys, values, plan_col, plan_row, lengths):
    vmem = pl.BlockSpec(memory_space=pltpu.VMEM)
    dma = pltpu.SemaphoreType.DMA
    return pl.pallas_call(
        exchange_kernel,
        out_shape=(
            jax.ShapeDtypeStruct((2, ROWS // TILE, TILE * 8, HEAD_SIZE), jnp.bfloat16),
            jax.ShapeDtypeStruct((8, KEYS, 512), jnp.bfloat16),
            jax.ShapeDtypeStruct((8, ROWS), jnp.int32),
            jax.ShapeDtypeStruct((ROWS, 128), jnp.int32),
        ),
        in_specs=[vmem] * 6,
        out_specs=[vmem, pl.BlockSpec(memory_space=pl.ANY), vmem, vmem],
        scratch_shapes=[
            pltpu.VMEM((8, SLOT, 2 * HALF), jnp.bfloat16),
            pltpu.VMEM((8, 2, SLOT, HALF), jnp.bfloat16),
            pltpu.VMEM((8, SLOT, 2 * PAIR), jnp.bfloat16),
            pltpu.VMEM((8, 2, SLOT, PAIR), jnp.bfloat16),
            pltpu.VMEM((8, PART, PAIR), jnp.bfloat16),
            pltpu.VMEM((8, PART, PAIR), jnp.bfloat16),
            pltpu.VMEM((KEYS, 512), jnp.bfloat16),
            pltpu.VMEM((8, 128), jnp.int32),
            pltpu.VMEM((ROWS, 128), jnp.int32),
            pltpu.VMEM((ROWS, HEAD_SIZE), jnp.float32),
            pltpu.VMEM((ROWS, HEAD_SIZE), jnp.float32),
            dma((16,)), dma((8, 2)), dma((16,)), dma((8, 2)), dma((8,)), dma((8,)), dma((3, 7)), dma((3, 7)),
            dma(()), dma(()), dma((3,)),
        ],
        compiler_params=pltpu.CompilerParams(
            collective_id=0, has_side_effects=True, vmem_limit_bytes=VMEM_LIMIT
        ),
        name="exchange",
    )(queries, keys, values, plan_col, plan_row, lengths)


def back_kernel(
    made_ref, rank_ref, plan_col, plan_row, out_ref, send_ref, ret_ref, send, recv, local_sem
):
    x, y, z, core = coords()
    my_cycle = x % 2 * 4 + y % 2 * 2 + z % 2
    mine = sign_of(core)
    other = 1 - core
    for delta in range(1, 8):
        for worker in range(2):
            signal(moved(mine, delta, worker))
    signal(moved(0, 0, other))

    columns = pl.ds(pl.multiple_of(core * HALF, 128), HALF)

    def place_rows(first):
        rows = slice(first * 2 * SLOT, first * 2 * SLOT + 4 * SLOT)
        put = bf16(rank_ref[rows, 0:1] == iota((4 * SLOT, ROWS), 1))

        def one_part(part, carry):
            here = pl.ds(pl.multiple_of(part * 512, 512), 512)
            chosen = dot(put, made_ref[:, here]).astype(jnp.bfloat16)
            for one in range(4):
                send_ref[first + one // 2, one % 2, :, here] = chosen[one * SLOT : (one + 1) * SLOT, :]
            return carry

        lax.fori_loop(0, 4, one_part, 0)

    copies = []

    def start(delta, source):
        copy = remote(
            send_ref.at[delta, source],
            ret_ref.at[delta, :, columns],
            send.at[delta * 2 + source],
            recv.at[delta, core],
            moved(-sign_of(source), delta, source),
        )
        copy.start()
        copies.append(copy)

    place_rows(6)
    pl.semaphore_wait(pltpu.get_barrier_semaphore(), 15)
    for first in (6, 4, 2, 0):
        if first < 6:
            place_rows(first)
        for delta in (first + 1, first):
            if delta:
                for source in range(2):
                    start(delta, source)
    own = pltpu.make_async_copy(send_ref.at[0, core], ret_ref.at[0, :, columns], local_sem)
    own.start()
    copy = remote(
        send_ref.at[0, other], ret_ref.at[0, :, columns], send.at[0], recv.at[0, core], moved(0, 0, other)
    )
    copy.start()
    copies.append(copy)

    plan_c, plan_r = plan_col[...], plan_row[...]
    same = (cycle_of(plan_c) == cycle_of(plan_r)) & (iota((TOK, TOK), 1) < iota((TOK, TOK), 0))
    rank = jnp.sum(jnp.where(same, 1, 0), 1, keepdims=True)
    row = jnp.bitwise_xor(cycle_of(plan_c), my_cycle) * SLOT + rank
    choose = bf16(iota((TOK, 8 * SLOT), 1) == row)

    def landed(delta, worker):
        here = ret_ref.at[delta, :, pl.ds(pl.multiple_of(worker * HALF, 128), HALF)]
        remote(here, here, send.at[0], recv.at[delta, worker], moved(0, 0, other)).wait_recv()

    own.wait()
    landed(0, other)
    for delta in range(1, 8):
        for worker in range(2):
            landed(delta, worker)

    def finish(part, carry):
        here = pl.ds(pl.multiple_of(part * 512, 512), 512)
        out_ref[:, here] = dot(choose, ret_ref[:, :, here].reshape(8 * SLOT, 512)).astype(jnp.bfloat16)
        return carry

    lax.fori_loop(0, 8, finish, 0)
    for copy in copies:
        copy.wait_send()


def back(made, rank, plan_col, plan_row):
    vmem = pl.BlockSpec(memory_space=pltpu.VMEM)
    return pl.pallas_call(
        back_kernel,
        out_shape=jax.ShapeDtypeStruct((TOK, 2 * HALF), jnp.bfloat16),
        in_specs=[vmem] * 4,
        out_specs=vmem,
        scratch_shapes=[
            pltpu.VMEM((8, 2, SLOT, HALF), jnp.bfloat16),
            pltpu.VMEM((8, SLOT, 2 * HALF), jnp.bfloat16),
            pltpu.SemaphoreType.DMA((16,)),
            pltpu.SemaphoreType.DMA((8, 2)),
            pltpu.SemaphoreType.DMA(()),
        ],
        compiler_params=pltpu.CompilerParams(
            collective_id=1, has_side_effects=True, vmem_limit_bytes=VMEM_LIMIT
        ),
        name="back",
    )(made, rank, plan_col, plan_row)


def attend_kernel(
    low_ref, high_ref, u_ref, begin_ref, turned, kv_ref,
    made, peak, total, summed, decays, scores0, scores1, weights0, weights1,
):
    across = iota((BLOCK, TILE * 8), 0)

    def one_tile(tile, carry):
        low = low_ref[tile]
        high = high_ref[tile]
        there = pl.multiple_of(tile * TILE, TILE)

        @pl.when(high < low)
        def _():
            made[pl.ds(there, TILE), :] = jnp.zeros((TILE, HALF), jnp.bfloat16)

        @pl.when(high >= low)
        def _():
            live_tile(tile, low, high, there)

        return carry

    def live_tile(tile, low, high, there):
        begin = begin_ref[pl.ds(tile, 1), :]
        last = u_ref[pl.ds(tile, 1), :]
        peak[...] = jnp.full_like(peak, NEG)
        summed[...] = jnp.zeros_like(summed)
        total[...] = jnp.zeros_like(total)
        decays[...] = jnp.ones_like(decays)
        weights1[...] = jnp.zeros_like(weights1)

        def spot(block):
            block = jnp.minimum(block, 15)
            return jnp.where(block < 8, block, 15 - block), jnp.where(block < 8, 0, BLOCK)

        def score_of(block, scores):
            holder, row = spot(block)
            place = across + block * BLOCK
            allowed = (place >= begin) & (place <= last)
            for head in range(2):
                key = kv_ref[
                    holder,
                    pl.ds(pl.multiple_of(row, BLOCK), BLOCK),
                    head * HEAD_SIZE : (head + 1) * HEAD_SIZE,
                ]
                score = lax.dot_general(
                    key, turned[head, tile], (((1,), (1,)), ((), ())), preferred_element_type=jnp.float32
                )
                scores[head] = jnp.where(allowed, score, NEG)

        def weigh(scores, weights, head):
            score = scores[head]
            old = peak[head]
            new = jnp.maximum(old, jnp.max(score, 0, keepdims=True))
            decay = jnp.exp2(old - new)
            peak[head] = new
            weight = jnp.exp2(score - new)
            summed[head] = summed[head] * decay + jnp.sum(weight, 0, keepdims=True)
            weights[head] = weight.astype(jnp.bfloat16)
            decays[head] = decay

        def add(block, weights, head):
            holder, row = spot(block)
            value = kv_ref[
                holder,
                pl.ds(pl.multiple_of(row + head * HEAD_SIZE, HEAD_SIZE), HEAD_SIZE),
                2 * HEAD_SIZE :,
            ]
            total[head] = total[head] * decays[head] + jnp.dot(
                value, weights[head], preferred_element_type=jnp.float32
            )

        score_of(low, scores0)

        def one_step(step, carry):
            block = low + step * 2
            for head in range(2):
                add(jnp.maximum(block - 1, 0), weights1, head)
            score_of(block + 1, scores1)
            for head in range(2):
                weigh(scores0, weights0, head)
            for head in range(2):
                add(block, weights0, head)
            score_of(block + 2, scores0)
            for head in range(2):
                weigh(scores1, weights1, head)
            return carry

        steps = (high - low + 2) // 2
        lax.fori_loop(0, steps, one_step, 0)
        for head in range(2):
            add(jnp.maximum(low + steps * 2 - 1, 0), weights1, head)
        for head in range(2):
            result = (total[head] / jnp.maximum(summed[head], 1e-30)).T.astype(jnp.bfloat16)
            for one in range(8):
                made[pl.ds(there, TILE), pl.ds((head * 8 + one) * HEAD_SIZE, HEAD_SIZE)] = result[
                    one * TILE : (one + 1) * TILE
                ]

    lax.fori_loop(0, ROWS // TILE, one_tile, 0)


def per_tile(column):
    return jnp.tile(column.reshape(ROWS // TILE, TILE), (1, 8))


def attend(low, high, u, begin, q, kv):
    smem = pl.BlockSpec(memory_space=pltpu.SMEM)
    vmem = pl.BlockSpec(memory_space=pltpu.VMEM)
    lanes = TILE * 8
    return pl.pallas_call(
        attend_kernel,
        out_shape=jax.ShapeDtypeStruct((ROWS, HALF), jnp.bfloat16),
        in_specs=[smem] * 2 + [vmem] * 4,
        out_specs=vmem,
        scratch_shapes=[
            pltpu.VMEM((2, 1, lanes), jnp.float32),
            pltpu.VMEM((2, HEAD_SIZE, lanes), jnp.float32),
            pltpu.VMEM((2, 1, lanes), jnp.float32),
            pltpu.VMEM((2, 1, lanes), jnp.float32),
            pltpu.VMEM((2, BLOCK, lanes), jnp.float32),
            pltpu.VMEM((2, BLOCK, lanes), jnp.float32),
            pltpu.VMEM((2, BLOCK, lanes), jnp.bfloat16),
            pltpu.VMEM((2, BLOCK, lanes), jnp.bfloat16),
        ],
        compiler_params=pltpu.CompilerParams(vmem_limit_bytes=VMEM_LIMIT),
        name="attend",
    )(low, high, per_tile(u), per_tile(begin), q, kv)


def local(queries, keys, values, plan, doc_lengths):
    plan_col, plan_row = plan[:, None], plan[None, :]
    lengths = jnp.pad(doc_lengths, ((0, 7), (0, 124)))
    q, kv, places, rank = exchange(queries, keys, values, plan_col, plan_row, lengths)
    u, begin = places[0], places[1]
    live = u < 4096
    low = jnp.where(live, begin // BLOCK, 0).reshape(ROWS // TILE, TILE)[:, 0]
    high = jnp.max(jnp.where(live, u // BLOCK, -1).reshape(ROWS // TILE, TILE), 1)
    made = attend(low, high, u, begin, q, kv)
    return back(made, rank, plan_col, plan_row)


def solution(mesh):
    return jax.shard_map(
        local,
        mesh=mesh,
        in_specs=(
            P(("blk", "group"), None),
            P(("blk", "group"), None),
            P(("blk", "group"), None),
            P(("blk", "group")),
            P("group", None),
        ),
        out_specs=P(("blk", "group"), None),
        check_vma=False,
    )
```

```python
import math

import jax
import jax.numpy as jnp
from jax import lax
from jax.experimental import pallas as pl
from jax.experimental.pallas import tpu as pltpu
from jax.sharding import PartitionSpec as P

QUERY_HEADS = 32
KEY_VALUE_HEADS = 4
HEAD_SIZE = 128
THETA = 500000.0

TOK = 256
SLOT = 64
KEYS = 512
BLOCK = 256
TILE = 32
SUPER = 256
HALF = QUERY_HEADS // 2 * HEAD_SIZE
WIDE = HALF + 128
ROWS = 16 * SLOT
NEG = -1e30
SCALE = math.log2(math.e) / math.sqrt(HEAD_SIZE)
MESH = pl.DeviceIdType.MESH
VMEM_LIMIT = 60 * 1024 * 1024


def coords():
    b = lax.axis_index("blk")
    g = lax.axis_index("group")
    return b // 4, g % 4, (b // 2) % 2 * 2 + g // 4, b % 2


def device(x, y, z, core):
    x, y, z = lax.rem(x + 4, 4), lax.rem(y + 4, 4), lax.rem(z + 4, 4)
    return x * 4 + z // 2 * 2 + core, lax.rem(z, 2) * 4 + y


def moved(sign, delta, core):
    x, y, z, _ = coords()
    return device(x + sign * (delta // 4), y + sign * (delta // 2 % 2), z + sign * (delta % 2), core)


def sign_of(core):
    return 1 - 2 * core


def signal(target):
    pl.semaphore_signal(pltpu.get_barrier_semaphore(), inc=1, device_id=target, device_id_type=MESH)


def remote(src, dst, send, recv, target):
    return pltpu.make_async_remote_copy(
        src_ref=src, dst_ref=dst, send_sem=send, recv_sem=recv, device_id=target, device_id_type=MESH
    )


THIRDS = ((0, 176, (4, 2, 1)), (176, 176, (2, 1, 4)), (352, 160, (1, 4, 2)))
PAIR = 640
PART = 128


def iota(shape, axis):
    return lax.broadcasted_iota(jnp.int32, shape, axis)


def bf16(flags):
    return jnp.where(flags, 1.0, 0.0).astype(jnp.bfloat16)


def dot(a, b):
    return jnp.dot(a, b, preferred_element_type=jnp.float32)


def cycle_of(plan):
    return (plan >> 8) & 7


def cycle_index(plan):
    p = plan >> 11
    offset = plan & 255
    return jnp.where(offset < 128, p * 128 + offset, (31 - p) * 128 + offset - 128)


def column_of(row):
    size = row.shape[1]
    return jnp.sum(jnp.where(iota((size, size), 0) == iota((size, size), 1), row, 0), 1, keepdims=True)


def document_start(u, lengths):
    end = jnp.zeros((1, 1), jnp.int32)
    start = jnp.zeros_like(u)
    for one in range(4):
        length = lengths[0:1, one : one + 1]
        end = end + length
        start = start + jnp.where(u >= end, length, 0)
    return start


def turning(position):
    half = HEAD_SIZE // 2
    lane = iota((1, HEAD_SIZE), 1)
    spot = (lane & (half - 1)).astype(jnp.float32)
    inv_freq = jnp.exp(-math.log(THETA) * (2.0 * spot / HEAD_SIZE))
    angle = position.astype(jnp.float32) * inv_freq
    both = jnp.cos(jnp.where(lane < half, angle, angle - math.pi / 2))
    other = pltpu.roll(both, half, 1)
    first = jnp.broadcast_to(lane < half, both.shape)
    return jnp.where(first, both, other), jnp.where(first, -other, both)


def exchange_kernel(
    queries_ref, keys_ref, values_ref, plan_row, lengths_ref,
    turned_ref, all_ref, last_ref, begin_ref, bounds_ref, rank_ref,
    q_out, q_got, kv_out, kv_got, part_out, part_got, own_ref, len_out, len_got, key_ref, cos_ref, sin_ref, sorted_ref,
    q_send, q_recv, a_send, a_recv, b_send, b_recv, kv_send, kv_recv, len_send, len_recv, local_sem, out_sem,
):
    x, y, z, core = coords()
    place = x // 2 * 4 + y // 2 * 2 + z // 2
    my_cycle = x % 2 * 4 + y % 2 * 2 + z % 2
    mine = sign_of(core)
    other = 1 - core

    block_at, group_at = lax.axis_index("blk"), lax.axis_index("group")
    spot = block_at // 2
    to_device = device(
        spot // 4 * 2 + group_at // 4, spot // 2 % 2 * 2 + group_at // 2 % 2, spot % 2 * 2 + group_at % 2, block_at % 2
    )
    from_block = place * 2 + core
    at_home = (from_block == block_at) & (my_cycle == group_at)

    for delta in range(1, 8):
        for source in range(2):
            signal(moved(-sign_of(source), delta, source))
    signal(moved(0, 0, other))
    for mask in range(1, 8):
        signal(across_cycle(mask))

    @pl.when(jnp.logical_not(at_home))
    def _():
        signal((from_block, my_cycle))

    len_out[...] = jnp.zeros_like(len_out)
    len_out[0:1, 0:4] = lengths_ref[...]
    plan_r = plan_row[...]
    plan_c = column_of(plan_r)
    same = (cycle_of(plan_c) == cycle_of(plan_r)) & (iota((TOK, TOK), 0) < iota((TOK, TOK), 1))
    rank = jnp.sum(jnp.where(same, 1, 0), 0, keepdims=True)
    row = jnp.bitwise_xor(cycle_of(plan_r), my_cycle) * SLOT + rank
    choose = bf16(iota((8 * SLOT, TOK), 0) == row)
    u = cycle_index(plan_c)
    lane = iota((TOK, 128), 1)
    fields = jnp.where(lane == 0, (u >> 8) + 1, jnp.where(lane == 1, u & 255, 0))
    fields = fields.astype(jnp.float32).astype(jnp.bfloat16)
    chosen_k = dot(choose, keys_ref[...]).astype(jnp.bfloat16)
    chosen_v = dot(choose, values_ref[...]).astype(jnp.bfloat16)
    chosen_f = dot(choose, fields).astype(jnp.bfloat16)
    for delta in range(8):
        rows = slice(delta * SLOT, (delta + 1) * SLOT)
        for half in range(2):
            kv_out[delta, :, half * PAIR : half * PAIR + 256] = chosen_k[rows, half * 256 : half * 256 + 256]
            kv_out[delta, :, half * PAIR + 256 : half * PAIR + 512] = chosen_v[rows, half * 256 : half * 256 + 256]
            kv_out[delta, :, half * PAIR + 512 : half * PAIR + 640] = chosen_f[rows, :]

    pl.semaphore_wait(pltpu.get_barrier_semaphore(), jnp.where(at_home, 22, 23))

    copies = []

    def start(copy):
        copy.start()
        copies.append(copy)

    def lengths_copy():
        return remote(len_out, len_got, len_send, len_recv, to_device)

    @pl.when(jnp.logical_not(at_home))
    def _():
        lengths_copy().start()

    def out_copy(src, dst, send, recv, width, delta, to_core):
        columns = pl.ds(pl.multiple_of(to_core * width, 128), width)
        slot = delta * 2 + to_core if delta else 0
        return remote(
            src.at[delta, :, columns],
            dst.at[delta, core],
            send.at[slot],
            recv.at[delta, core],
            moved(mine, delta, to_core) if delta else moved(0, 0, other),
        )

    def landed(dst, send, recv, delta, source):
        here = dst.at[delta, source]
        remote(here, here, send.at[0], recv.at[delta, source], moved(0, 0, other)).wait_recv()

    order = (7, 6, 5, 3, 4, 2, 1)
    start(out_copy(kv_out, kv_got, a_send, a_recv, PAIR, 0, other))
    for delta in order:
        for to_core in range(2):
            start(out_copy(kv_out, kv_got, a_send, a_recv, PAIR, delta, to_core))
    own_a = pltpu.make_async_copy(
        kv_out.at[0, :, pl.ds(pl.multiple_of(core * PAIR, 128), PAIR)], kv_got.at[0, core], local_sem.at[0]
    )
    own_a.start()

    for part in range(8):
        columns = slice(part * 512, part * 512 + 512)
        chosen = dot(choose, queries_ref[:, columns]).astype(jnp.bfloat16)
        for delta in range(8):
            q_out[delta, :, columns] = chosen[delta * SLOT : (delta + 1) * SLOT, :]
    start(out_copy(q_out, q_got, q_send, q_recv, HALF, 0, other))
    for chunk in range(SLOT // 16):
        for delta in order:
            for to_core in range(2):
                columns = pl.ds(to_core * HALF, HALF)
                rows = pl.ds(chunk * 16, 16)
                remote(
                    q_out.at[delta, rows, columns],
                    q_got.at[delta, core, rows],
                    q_send.at[delta * 2 + to_core],
                    q_recv.at[delta, core],
                    moved(mine, delta, to_core),
                ).start()
    for delta in order:
        for to_core in range(2):
            copies.append(out_copy(q_out, q_got, q_send, q_recv, HALF, delta, to_core))
    own_q = pltpu.make_async_copy(
        q_out.at[0, :, pl.ds(pl.multiple_of(core * HALF, 128), HALF)], q_got.at[0, core], local_sem.at[1]
    )
    own_q.start()

    own_a.wait()
    landed(kv_got, a_send, a_recv, 0, other)
    for delta in range(1, 8):
        for source in range(2):
            landed(kv_got, a_send, a_recv, delta, source)

    def fields_of(table):
        fields = table.reshape(ROWS, 128).astype(jnp.float32)
        flat = fields.T
        out = []
        for lead, low in ((fields[:, 0:1], fields[:, 1:2]), (flat[0:1, :], flat[1:2, :])):
            lead = lead.astype(jnp.int32)
            out.append((lead > 0, (lead - 1) * 256 + low.astype(jnp.int32)))
        return out

    def holder_of(u):
        block = u >> 8
        return jnp.where(block < 8, block, 15 - block)

    (valid_c, u_c), (valid_r, u_r) = fields_of(kv_got[:, :, :, 512:])
    key_c = jnp.where(valid_c, holder_of(u_c), -1)
    key_r = jnp.where(valid_r, holder_of(u_r), -2)
    key_ref[...] = jnp.broadcast_to(key_c, (ROWS, 128))

    def count_before(step, total):
        base = pl.multiple_of(step * 128, 128)
        chunk = key_ref[pl.ds(base, 128), 0:1]
        hits = (chunk == key_r) & (iota((128, ROWS), 0) + base < iota((128, ROWS), 1))
        return total + jnp.sum(jnp.where(hits, 1, 0), 0, keepdims=True)

    before = lax.fori_loop(0, ROWS // 128, count_before, jnp.zeros((1, ROWS), jnp.int32))
    target = jnp.where(valid_r, key_r * PART + before, -1)

    def fill(step, carry):
        base = pl.multiple_of(step * 4 * PART, 4 * PART)
        rows = dot(bf16(iota((4 * PART, ROWS), 0) + base == target), kv_got[...].reshape(ROWS, PAIR))
        part_out[pl.ds(step * 4, 4)] = rows.astype(jnp.bfloat16).reshape(4, PART, PAIR)
        return carry

    lax.fori_loop(0, 2, fill, 0)

    def flip(mask):
        out = 0
        for bit in (4, 2, 1):
            digit = place // bit % 2
            out = out + bit * ((1 - digit) if mask & bit else digit)
        return out

    for mask in order:
        start(
            remote(
                part_out.at[flip(mask)], part_got.at[place], b_send.at[mask], b_recv.at[mask], across_cycle(mask)
            )
        )
    part_got[place] = part_out[place]

    index_c, index_r = iota((ROWS, 1), 0), iota((1, ROWS), 1)
    key_c = jnp.where(valid_c, u_c, 4096 + index_c)
    key_r = jnp.where(valid_r, u_r, 4096 + index_r)
    key_ref[...] = jnp.broadcast_to(key_c, (ROWS, 128))

    def rank_step(step, total):
        base = pl.multiple_of(step * 128, 128)
        chunk = key_ref[pl.ds(base, 128), 0:1]
        counts = jnp.sum(jnp.where(key_r < chunk, 1, 0), 1, keepdims=True)
        rank_ref[pl.ds(base, 128), :] = jnp.broadcast_to(counts, (128, 128))
        return total + jnp.sum(jnp.where(chunk < key_r, 1, 0), 0, keepdims=True)

    rank_r = lax.fori_loop(0, ROWS // 128, rank_step, jnp.zeros((1, ROWS), jnp.int32))

    def sort_step(step, total):
        base = pl.multiple_of(step * 128, 128)
        chunk = key_ref[pl.ds(base, 128), 0:1]
        ranks = rank_ref[pl.ds(base, 128), 0:1]
        return total + jnp.sum(jnp.where(ranks == iota((128, ROWS), 1), chunk, 0), 0, keepdims=True)

    sorted_r = lax.fori_loop(0, ROWS // 128, sort_step, jnp.zeros((1, ROWS), jnp.int32))

    @pl.when(at_home)
    def _():
        len_got[...] = len_out[...]

    @pl.when(jnp.logical_not(at_home))
    def _():
        lengths_copy().wait()

    lengths = len_got[...]
    begin_r = jnp.where(sorted_r < 4096, document_start(sorted_r, lengths), 8192)

    own_tile = iota((ROWS // TILE, ROWS), 1) >> 5 == iota((ROWS // TILE, ROWS), 0)
    spread = bf16(iota((ROWS, TILE * 8), 0) & (TILE - 1) == iota((ROWS, TILE * 8), 1) & (TILE - 1))
    for values, tiles_ref in ((sorted_r, last_ref), (begin_r, begin_ref)):
        parts = [
            dot(jnp.where(own_tile, half, 0).astype(jnp.float32).astype(jnp.bfloat16), spread).astype(jnp.int32)
            for half in (values >> 8, values & 255)
        ]
        tiles_ref[...] = parts[0] * 256 + parts[1]

    def turn_step(step, carry):
        low, high = carry
        base = pl.multiple_of(step * 128, 128)
        hits = iota((128, ROWS), 0) + base == rank_r
        u = jnp.sum(jnp.where(hits, key_r, 0), 1, keepdims=True)
        live = u < 4096
        start = document_start(u, lengths)
        index, tile = iota((128, 128), 0) + base, iota((128, 128), 1)
        low = low + jnp.sum(jnp.where((index == tile * TILE) & live, start >> 8, 0), 0, keepdims=True)
        high = jnp.maximum(
            high, jnp.max(jnp.where((index >> 5 == tile) & live, u >> 8, -1), 0, keepdims=True)
        )
        cos, sin = turning(jnp.where(live, u - start, 0))
        cos_ref[pl.ds(base, 128), :] = cos * SCALE
        sin_ref[pl.ds(base, 128), :] = sin * SCALE
        return low, high

    low, high = lax.fori_loop(
        0, ROWS // 128, turn_step, (jnp.zeros((1, 128), jnp.int32), jnp.full((1, 128), -1, jnp.int32))
    )
    bounds_ref[...] = jnp.zeros_like(bounds_ref)
    bounds_ref[0:1, :] = low
    bounds_ref[1:2, :] = high
    rows_c = iota((KEYS, 1), 0)
    key_u = jnp.where(rows_c < BLOCK, place * BLOCK + rows_c, (15 - place) * BLOCK + rows_c - BLOCK)
    key_cos, key_sin = turning(key_u - document_start(key_u, lengths))

    for mask in range(1, 8):
        here = part_got.at[flip(mask)]
        remote(here, here, b_send.at[mask], b_recv.at[mask], across_cycle(mask)).wait_recv()

    _, (valid, u) = fields_of(part_got[:, :, 512:])
    target = jnp.where(valid, jnp.where(u >= 2048, BLOCK, 0) + (u & 255), -1)
    placed = dot(bf16(iota((KEYS, ROWS), 0) == target), part_got[:, :, :512].reshape(ROWS, 512))
    for head in range(2):
        columns = slice(head * HEAD_SIZE, (head + 1) * HEAD_SIZE)
        entry = placed[:, columns]
        entry = entry * key_cos + pltpu.roll(entry, HEAD_SIZE // 2, 1) * key_sin
        own_ref[:, columns] = entry.astype(jnp.bfloat16)
    for half in range(2):
        rows = slice(half * BLOCK, (half + 1) * BLOCK)
        own_ref[rows, 256:] = placed[rows, 256:].T.astype(jnp.bfloat16)

    own_kv = pltpu.make_async_copy(own_ref, all_ref.at[place], local_sem.at[2])
    own_kv.start()

    def kv_copy(third, index):
        start, size, (b1, b2, b3) = THIRDS[third]
        mask, axis = ((0, b1), (0, b2), (0, b3), (b1, b2), (b1, b3), (b2, b3), (b1 ^ b2, b3))[index]
        rows = pl.ds(start, size)
        block = flip(mask)
        src = own_ref.at[rows] if mask == 0 else all_ref.at[block, rows]
        return remote(
            src, all_ref.at[block, rows], kv_send.at[third, index], kv_recv.at[third, index], across_cycle(axis)
        )

    def kv_landed(third, index):
        start, size, (b1, b2, b3) = THIRDS[third]
        mask = (b1, b2, b3, b1 ^ b2, b1 ^ b3, b2 ^ b3, 7)[index]
        here = all_ref.at[flip(mask), pl.ds(start, size)]
        remote(here, here, kv_send.at[third, index], kv_recv.at[third, index], across_cycle(4)).wait_recv()

    for index in range(3):
        for third in range(3):
            start(kv_copy(third, index))

    landed(q_got, q_send, q_recv, 0, other)
    for delta in range(1, 8):
        for source in range(2):
            landed(q_got, q_send, q_recv, delta, source)
    own_q.wait()

    def order_queries(sup):
        base = sup * SUPER
        pick = bf16(iota((SUPER, ROWS), 0) + base == rank_r)
        cos = cos_ref[base : base + SUPER, :]
        sin = sin_ref[base : base + SUPER, :]

        def one_part(part, carry):
            columns = pl.ds(pl.multiple_of(part * 256, 256), 256)
            rows = dot(pick, q_got[:, :, :, columns].reshape(ROWS, 256))
            for one in range(2):
                entry = rows[:, one * HEAD_SIZE : (one + 1) * HEAD_SIZE]
                entry = entry * cos + pltpu.roll(entry, HEAD_SIZE // 2, 1) * sin
                entry = entry.astype(jnp.bfloat16)
                first = pl.multiple_of((part % 4 * 2 + one) * TILE, TILE)
                for tile in range(SUPER // TILE):
                    sorted_ref[part // 4, sup * (SUPER // TILE) + tile, pl.ds(first, TILE), :] = entry[
                        tile * TILE : (tile + 1) * TILE
                    ]
            return carry

        lax.fori_loop(0, 8, one_part, 0)
        turned_copy(sup).start()

    def turned_copy(sup):
        tiles = pl.ds(sup * (SUPER // TILE), SUPER // TILE)
        return pltpu.make_async_copy(sorted_ref.at[:, tiles], turned_ref.at[:, tiles], out_sem.at[sup])

    for third in range(3):
        kv_landed(third, 0)
        start(kv_copy(third, 3))
        start(kv_copy(third, 4))
    for third in range(3):
        kv_landed(third, 1)
        start(kv_copy(third, 5))
    order_queries(0)
    for third in range(3):
        kv_landed(third, 3)
        start(kv_copy(third, 6))
    for sup in range(1, 4):
        order_queries(sup)
    for index in (2, 4, 5, 6):
        for third in range(3):
            kv_landed(third, index)
    own_kv.wait()
    for sup in range(4):
        turned_copy(sup).wait()
    for copy in copies:
        copy.wait_send()


def across_cycle(mask):
    x, y, z, core = coords()
    return device(x + 2 * (mask // 4), y + 2 * (mask // 2 % 2), z + 2 * (mask % 2), core)


def exchange(queries, keys, values, plan_row, lengths):
    vmem = pl.BlockSpec(memory_space=pltpu.VMEM)
    dma = pltpu.SemaphoreType.DMA
    return pl.pallas_call(
        exchange_kernel,
        out_shape=(
            jax.ShapeDtypeStruct((2, ROWS // TILE, TILE * 8, HEAD_SIZE), jnp.bfloat16),
            jax.ShapeDtypeStruct((8, KEYS, 512), jnp.bfloat16),
            jax.ShapeDtypeStruct((ROWS // TILE, TILE * 8), jnp.int32),
            jax.ShapeDtypeStruct((ROWS // TILE, TILE * 8), jnp.int32),
            jax.ShapeDtypeStruct((8, 128), jnp.int32),
            jax.ShapeDtypeStruct((ROWS, 128), jnp.int32),
        ),
        in_specs=[vmem] * 5,
        out_specs=[pl.BlockSpec(memory_space=pl.ANY)] * 2 + [vmem] * 4,
        scratch_shapes=[
            pltpu.VMEM((8, SLOT, 2 * HALF), jnp.bfloat16),
            pltpu.VMEM((8, 2, SLOT, HALF), jnp.bfloat16),
            pltpu.VMEM((8, SLOT, 2 * PAIR), jnp.bfloat16),
            pltpu.VMEM((8, 2, SLOT, PAIR), jnp.bfloat16),
            pltpu.VMEM((8, PART, PAIR), jnp.bfloat16),
            pltpu.VMEM((8, PART, PAIR), jnp.bfloat16),
            pltpu.VMEM((KEYS, 512), jnp.bfloat16),
            pltpu.VMEM((8, 128), jnp.int32),
            pltpu.VMEM((8, 128), jnp.int32),
            pltpu.VMEM((ROWS, 128), jnp.int32),
            pltpu.VMEM((ROWS, HEAD_SIZE), jnp.float32),
            pltpu.VMEM((ROWS, HEAD_SIZE), jnp.float32),
            pltpu.VMEM((2, ROWS // TILE, TILE * 8, HEAD_SIZE), jnp.bfloat16),
            dma((16,)), dma((8, 2)), dma((16,)), dma((8, 2)), dma((8,)), dma((8,)), dma((3, 7)), dma((3, 7)),
            dma(()), dma(()), dma((3,)), dma((4,)),
        ],
        compiler_params=pltpu.CompilerParams(
            collective_id=0, has_side_effects=True, vmem_limit_bytes=VMEM_LIMIT
        ),
        name="exchange",
    )(queries, keys, values, plan_row, lengths)


def back_kernel(made_ref, rank_ref, ret_ref, send_ref, send, recv, local_sem):
    x, y, z, core = coords()
    mine = sign_of(core)
    other = 1 - core
    for delta in range(1, 8):
        for worker in range(2):
            signal(moved(mine, delta, worker))
    signal(moved(0, 0, other))

    columns = pl.ds(pl.multiple_of(core * HALF, 128), HALF)

    def place_rows(first):
        rows = slice(first * 2 * SLOT, first * 2 * SLOT + 4 * SLOT)
        put = bf16(rank_ref[rows, 0:1] == iota((4 * SLOT, ROWS), 1))

        def one_part(part, carry):
            here = pl.ds(pl.multiple_of(part * 512, 512), 512)
            chosen = dot(put, made_ref[:, here]).astype(jnp.bfloat16)
            for one in range(4):
                send_ref[first + one // 2, one % 2, :, here] = chosen[one * SLOT : (one + 1) * SLOT, :]
            return carry

        lax.fori_loop(0, 4, one_part, 0)

    copies = []

    def back_copy(delta, source, first, size):
        rows = pl.ds(first, size)
        return remote(
            send_ref.at[delta, source, rows],
            ret_ref.at[delta, rows, columns],
            send.at[delta * 2 + source],
            recv.at[delta, core],
            moved(-sign_of(source), delta, source),
        )

    place_rows(6)
    pl.semaphore_wait(pltpu.get_barrier_semaphore(), 15)
    for first in (6, 4, 2, 0):
        if first < 6:
            place_rows(first)
        deltas = [delta for delta in (first + 1, first) if delta]
        for chunk in range(SLOT // 16):
            for delta in deltas:
                for source in range(2):
                    back_copy(delta, source, chunk * 16, 16).start()
        for delta in deltas:
            for source in range(2):
                copies.append(back_copy(delta, source, 0, SLOT))
    own = pltpu.make_async_copy(send_ref.at[0, core], ret_ref.at[0, :, columns], local_sem)
    own.start()
    copy = remote(
        send_ref.at[0, other], ret_ref.at[0, :, columns], send.at[0], recv.at[0, core], moved(0, 0, other)
    )
    copy.start()
    copies.append(copy)

    def landed(delta, worker):
        here = ret_ref.at[delta, :, pl.ds(pl.multiple_of(worker * HALF, 128), HALF)]
        remote(here, here, send.at[0], recv.at[delta, worker], moved(0, 0, other)).wait_recv()

    own.wait()
    landed(0, other)
    for delta in range(1, 8):
        for worker in range(2):
            landed(delta, worker)

    for copy in copies:
        copy.wait_send()


def back(made, rank):
    vmem = pl.BlockSpec(memory_space=pltpu.VMEM)
    return pl.pallas_call(
        back_kernel,
        out_shape=jax.ShapeDtypeStruct((8, SLOT, 2 * HALF), jnp.bfloat16),
        in_specs=[vmem] * 2,
        out_specs=pl.BlockSpec(memory_space=pl.ANY),
        scratch_shapes=[
            pltpu.VMEM((8, 2, SLOT, HALF), jnp.bfloat16),
            pltpu.SemaphoreType.DMA((16,)),
            pltpu.SemaphoreType.DMA((8, 2)),
            pltpu.SemaphoreType.DMA(()),
        ],
        compiler_params=pltpu.CompilerParams(
            collective_id=1, has_side_effects=True, vmem_limit_bytes=VMEM_LIMIT
        ),
        name="back",
    )(made, rank)


def restore_kernel(cycle_ref, plan_row, ret_ref, out_ref, choose_ref):
    @pl.when(pl.program_id(0) == 0)
    def _():
        plan_r = plan_row[...]
        plan_c = column_of(plan_r)
        same = (cycle_of(plan_c) == cycle_of(plan_r)) & (iota((TOK, TOK), 1) < iota((TOK, TOK), 0))
        rank = jnp.sum(jnp.where(same, 1, 0), 1, keepdims=True)
        row = jnp.bitwise_xor(cycle_of(plan_c), cycle_ref[0]) * SLOT + rank
        choose_ref[...] = bf16(iota((TOK, 8 * SLOT), 1) == row)

    rows = ret_ref[...].reshape(8 * SLOT, ret_ref.shape[2])
    out_ref[...] = dot(choose_ref[...], rows).astype(jnp.bfloat16)


def restore(my_cycle, plan_row, ret):
    width = 1024
    return pl.pallas_call(
        restore_kernel,
        grid=(2 * HALF // width,),
        out_shape=jax.ShapeDtypeStruct((TOK, 2 * HALF), jnp.bfloat16),
        in_specs=[
            pl.BlockSpec(memory_space=pltpu.SMEM),
            pl.BlockSpec((1, TOK), lambda i: (0, 0)),
            pl.BlockSpec((8, SLOT, width), lambda i: (0, 0, i)),
        ],
        out_specs=pl.BlockSpec((TOK, width), lambda i: (0, i)),
        scratch_shapes=[pltpu.VMEM((TOK, 8 * SLOT), jnp.bfloat16)],
        compiler_params=pltpu.CompilerParams(vmem_limit_bytes=VMEM_LIMIT),
        name="restore",
    )(my_cycle, plan_row, ret)


def attend_kernel(
    bounds_ref, last_ref, begin_ref, turned_ref, kv_ref,
    made_ref, turned, made, peak, total, summed, decays, scores0, scores1, weights0, weights1, in_sem, out_sem,
):
    across = iota((BLOCK, TILE * 8), 0)
    group = SUPER // TILE

    def load(sup):
        tiles = pl.ds(sup * group, group)
        return pltpu.make_async_copy(turned_ref.at[:, tiles], turned.at[:, tiles], in_sem.at[sup])

    def store(sup):
        rows = pl.ds(sup * SUPER, SUPER)
        return pltpu.make_async_copy(made.at[rows], made_ref.at[rows], out_sem.at[sup])

    for sup in range(ROWS // SUPER):
        load(sup).start()

    def one_tile(tile, carry):
        low = bounds_ref[0, tile]
        high = bounds_ref[1, tile]
        there = pl.multiple_of(tile * TILE, TILE)

        @pl.when(high < low)
        def _():
            made[pl.ds(there, TILE), :] = jnp.zeros((TILE, HALF), jnp.bfloat16)

        @pl.when(high >= low)
        def _():
            live_tile(tile, low, high, there)

        return carry

    def live_tile(tile, low, high, there):
        begin = begin_ref[pl.ds(tile, 1), :]
        span = jnp.maximum(last_ref[pl.ds(tile, 1), :] - begin + 1, 0).astype(jnp.uint32)
        peak[...] = jnp.full_like(peak, NEG)
        summed[...] = jnp.zeros_like(summed)
        total[...] = jnp.zeros_like(total)
        decays[...] = jnp.ones_like(decays)
        weights1[...] = jnp.zeros_like(weights1)

        def spot(block):
            block = jnp.minimum(block, 15)
            return jnp.where(block < 8, block, 15 - block), jnp.where(block < 8, 0, BLOCK)

        def score_of(block, scores):
            holder, row = spot(block)
            allowed = (across + (block * BLOCK - begin)).astype(jnp.uint32) < span
            for head in range(2):
                key = kv_ref[
                    holder,
                    pl.ds(pl.multiple_of(row, BLOCK), BLOCK),
                    head * HEAD_SIZE : (head + 1) * HEAD_SIZE,
                ]
                score = lax.dot_general(
                    key, turned[head, tile], (((1,), (1,)), ((), ())), preferred_element_type=jnp.float32
                )
                scores[head] = jnp.where(allowed, score, NEG)

        def weigh(scores, weights, head):
            score = scores[head]
            old = peak[head]
            new = jnp.maximum(old, jnp.max(score, 0, keepdims=True))
            decay = jnp.exp2(old - new)
            peak[head] = new
            weight = jnp.exp2(score - new)
            summed[head] = summed[head] * decay + jnp.sum(weight, 0, keepdims=True)
            weights[head] = weight.astype(jnp.bfloat16)
            decays[head] = decay

        def add(block, weights, head):
            holder, row = spot(block)
            value = kv_ref[
                holder,
                pl.ds(pl.multiple_of(row + head * HEAD_SIZE, HEAD_SIZE), HEAD_SIZE),
                2 * HEAD_SIZE :,
            ]
            total[head] = total[head] * decays[head] + jnp.dot(
                value, weights[head], preferred_element_type=jnp.float32
            )

        score_of(low, scores0)

        def one_step(step, carry):
            block = low + step * 2
            for head in range(2):
                add(jnp.maximum(block - 1, 0), weights1, head)
            score_of(block + 1, scores1)
            for head in range(2):
                weigh(scores0, weights0, head)
            for head in range(2):
                add(block, weights0, head)
            score_of(block + 2, scores0)
            for head in range(2):
                weigh(scores1, weights1, head)
            return carry

        steps = (high - low + 2) // 2
        lax.fori_loop(0, steps, one_step, 0)
        for head in range(2):
            add(jnp.maximum(low + steps * 2 - 1, 0), weights1, head)
        for head in range(2):
            result = (total[head] / jnp.maximum(summed[head], 1e-30)).T.astype(jnp.bfloat16)
            for one in range(8):
                made[pl.ds(there, TILE), pl.ds((head * 8 + one) * HEAD_SIZE, HEAD_SIZE)] = result[
                    one * TILE : (one + 1) * TILE
                ]

    for sup in range(ROWS // SUPER):
        load(sup).wait()
        lax.fori_loop(sup * group, (sup + 1) * group, one_tile, 0)
        store(sup).start()
    for sup in range(ROWS // SUPER):
        store(sup).wait()


def attend(bounds, last, begin, q, kv):
    smem = pl.BlockSpec(memory_space=pltpu.SMEM)
    vmem = pl.BlockSpec(memory_space=pltpu.VMEM)
    hbm = pl.BlockSpec(memory_space=pl.ANY)
    lanes = TILE * 8
    return pl.pallas_call(
        attend_kernel,
        out_shape=jax.ShapeDtypeStruct((ROWS, HALF), jnp.bfloat16),
        in_specs=[smem, vmem, vmem, hbm, vmem],
        out_specs=hbm,
        scratch_shapes=[
            pltpu.VMEM((2, ROWS // TILE, lanes, HEAD_SIZE), jnp.bfloat16),
            pltpu.VMEM((ROWS, HALF), jnp.bfloat16),
            pltpu.VMEM((2, 1, lanes), jnp.float32),
            pltpu.VMEM((2, HEAD_SIZE, lanes), jnp.float32),
            pltpu.VMEM((2, 1, lanes), jnp.float32),
            pltpu.VMEM((2, 1, lanes), jnp.float32),
            pltpu.VMEM((2, BLOCK, lanes), jnp.float32),
            pltpu.VMEM((2, BLOCK, lanes), jnp.float32),
            pltpu.VMEM((2, BLOCK, lanes), jnp.bfloat16),
            pltpu.VMEM((2, BLOCK, lanes), jnp.bfloat16),
            pltpu.SemaphoreType.DMA((ROWS // SUPER,)),
            pltpu.SemaphoreType.DMA((ROWS // SUPER,)),
        ],
        compiler_params=pltpu.CompilerParams(vmem_limit_bytes=VMEM_LIMIT),
        name="attend",
    )(bounds, last, begin, q, kv)


def local(queries, keys, values, plan, doc_lengths):
    x, y, z, _ = coords()
    my_cycle = x % 2 * 4 + y % 2 * 2 + z % 2
    plan_row = plan[None, :]
    q, kv, last, begin, bounds, rank = exchange(queries, keys, values, plan_row, doc_lengths)
    made = attend(bounds, last, begin, q, kv)
    ret = back(made, rank)
    return restore(jnp.reshape(my_cycle, (1,)).astype(jnp.int32), plan_row, ret)


def solution(mesh):
    return jax.shard_map(
        local,
        mesh=mesh,
        in_specs=(
            P(("blk", "group"), None),
            P(("blk", "group"), None),
            P(("blk", "group"), None),
            P(("blk", "group")),
            P("group", None),
        ),
        out_specs=P(("blk", "group"), None),
        check_vma=False,
    )
```

```python
import math

import jax
import jax.numpy as jnp
from jax import lax
from jax.experimental import pallas as pl
from jax.experimental.pallas import tpu as pltpu
from jax.sharding import PartitionSpec as P

QUERY_HEADS = 32
KEY_VALUE_HEADS = 4
HEAD_SIZE = 128
THETA = 500000.0

TOK = 256
SLOT = 64
KEYS = 512
BLOCK = 256
TILE = 64
TILE_BITS = 6
SUPER = 256
HALF = QUERY_HEADS // 2 * HEAD_SIZE
WIDE = HALF + 128
ROWS = 16 * SLOT
NEG = -1e30
SCALE = math.log2(math.e) / math.sqrt(HEAD_SIZE)
MESH = pl.DeviceIdType.MESH
VMEM_LIMIT = 60 * 1024 * 1024


def coords():
    b = lax.axis_index("blk")
    g = lax.axis_index("group")
    return b // 4, g % 4, (b // 2) % 2 * 2 + g // 4, b % 2


def device(x, y, z, core):
    x, y, z = lax.rem(x + 4, 4), lax.rem(y + 4, 4), lax.rem(z + 4, 4)
    return x * 4 + z // 2 * 2 + core, lax.rem(z, 2) * 4 + y


def moved(sign, delta, core):
    x, y, z, _ = coords()
    return device(x + sign * (delta // 4), y + sign * (delta // 2 % 2), z + sign * (delta % 2), core)


def sign_of(core):
    return 1 - 2 * core


def signal(target):
    pl.semaphore_signal(pltpu.get_barrier_semaphore(), inc=1, device_id=target, device_id_type=MESH)


def remote(src, dst, send, recv, target):
    return pltpu.make_async_remote_copy(
        src_ref=src, dst_ref=dst, send_sem=send, recv_sem=recv, device_id=target, device_id_type=MESH
    )


THIRDS = ((0, 176, (4, 2, 1)), (176, 176, (2, 1, 4)), (352, 160, (1, 4, 2)))
PAIR = 640
PART = 128


def iota(shape, axis):
    return lax.broadcasted_iota(jnp.int32, shape, axis)


def bf16(flags):
    return jnp.where(flags, 1.0, 0.0).astype(jnp.bfloat16)


def dot(a, b):
    return jnp.dot(a, b, preferred_element_type=jnp.float32)


def cycle_of(plan):
    return (plan >> 8) & 7


def cycle_index(plan):
    p = plan >> 11
    offset = plan & 255
    return jnp.where(offset < 128, p * 128 + offset, (31 - p) * 128 + offset - 128)


def column_of(row):
    size = row.shape[1]
    return jnp.sum(jnp.where(iota((size, size), 0) == iota((size, size), 1), row, 0), 1, keepdims=True)


def document_start(u, lengths):
    end = jnp.zeros((1, 1), jnp.int32)
    start = jnp.zeros_like(u)
    for one in range(4):
        length = lengths[0:1, one : one + 1]
        end = end + length
        start = start + jnp.where(u >= end, length, 0)
    return start


def turning(position):
    half = HEAD_SIZE // 2
    lane = iota((1, HEAD_SIZE), 1)
    spot = (lane & (half - 1)).astype(jnp.float32)
    inv_freq = jnp.exp(-math.log(THETA) * (2.0 * spot / HEAD_SIZE))
    angle = position.astype(jnp.float32) * inv_freq
    both = jnp.cos(jnp.where(lane < half, angle, angle - math.pi / 2))
    other = pltpu.roll(both, half, 1)
    first = jnp.broadcast_to(lane < half, both.shape)
    return jnp.where(first, both, other), jnp.where(first, -other, both)


def exchange_kernel(
    queries_ref, keys_ref, values_ref, plan_row, lengths_ref,
    turned_ref, all_ref, last_ref, begin_ref, bounds_ref, rank_ref,
    q_out, q_got, kv_out, kv_got, part_out, part_got, own_ref, len_out, len_got, key_ref, cos_ref, sin_ref, sorted_ref,
    q_send, q_recv, a_send, a_recv, b_send, b_recv, kv_send, kv_recv, len_send, len_recv, local_sem, out_sem,
):
    x, y, z, core = coords()
    place = x // 2 * 4 + y // 2 * 2 + z // 2
    my_cycle = x % 2 * 4 + y % 2 * 2 + z % 2
    mine = sign_of(core)
    other = 1 - core

    block_at, group_at = lax.axis_index("blk"), lax.axis_index("group")
    spot = block_at // 2
    to_device = device(
        spot // 4 * 2 + group_at // 4, spot // 2 % 2 * 2 + group_at // 2 % 2, spot % 2 * 2 + group_at % 2, block_at % 2
    )
    from_block = place * 2 + core
    at_home = (from_block == block_at) & (my_cycle == group_at)

    for delta in range(1, 8):
        for source in range(2):
            signal(moved(-sign_of(source), delta, source))
    signal(moved(0, 0, other))
    for mask in range(1, 8):
        signal(across_cycle(mask))

    @pl.when(jnp.logical_not(at_home))
    def _():
        signal((from_block, my_cycle))

    len_out[...] = jnp.zeros_like(len_out)
    len_out[0:1, 0:4] = lengths_ref[...]
    plan_r = plan_row[...]
    plan_c = column_of(plan_r)
    same = (cycle_of(plan_c) == cycle_of(plan_r)) & (iota((TOK, TOK), 0) < iota((TOK, TOK), 1))
    rank = jnp.sum(jnp.where(same, 1, 0), 0, keepdims=True)
    row = jnp.bitwise_xor(cycle_of(plan_r), my_cycle) * SLOT + rank
    choose = bf16(iota((8 * SLOT, TOK), 0) == row)
    u = cycle_index(plan_c)
    lane = iota((TOK, 128), 1)
    fields = jnp.where(lane == 0, (u >> 8) + 1, jnp.where(lane == 1, u & 255, 0))
    fields = fields.astype(jnp.float32).astype(jnp.bfloat16)
    chosen_k = dot(choose, keys_ref[...]).astype(jnp.bfloat16)
    chosen_v = dot(choose, values_ref[...]).astype(jnp.bfloat16)
    chosen_f = dot(choose, fields).astype(jnp.bfloat16)
    for delta in range(8):
        rows = slice(delta * SLOT, (delta + 1) * SLOT)
        for half in range(2):
            kv_out[delta, :, half * PAIR : half * PAIR + 256] = chosen_k[rows, half * 256 : half * 256 + 256]
            kv_out[delta, :, half * PAIR + 256 : half * PAIR + 512] = chosen_v[rows, half * 256 : half * 256 + 256]
            kv_out[delta, :, half * PAIR + 512 : half * PAIR + 640] = chosen_f[rows, :]

    pl.semaphore_wait(pltpu.get_barrier_semaphore(), jnp.where(at_home, 22, 23))

    copies = []

    def start(copy):
        copy.start()
        copies.append(copy)

    def lengths_copy():
        return remote(len_out, len_got, len_send, len_recv, to_device)

    @pl.when(jnp.logical_not(at_home))
    def _():
        lengths_copy().start()

    def out_copy(src, dst, send, recv, width, delta, to_core):
        columns = pl.ds(pl.multiple_of(to_core * width, 128), width)
        slot = delta * 2 + to_core if delta else 0
        return remote(
            src.at[delta, :, columns],
            dst.at[delta, core],
            send.at[slot],
            recv.at[delta, core],
            moved(mine, delta, to_core) if delta else moved(0, 0, other),
        )

    def landed(dst, send, recv, delta, source):
        here = dst.at[delta, source]
        remote(here, here, send.at[0], recv.at[delta, source], moved(0, 0, other)).wait_recv()

    order = (7, 6, 5, 3, 4, 2, 1)
    start(out_copy(kv_out, kv_got, a_send, a_recv, PAIR, 0, other))
    for delta in order:
        for to_core in range(2):
            start(out_copy(kv_out, kv_got, a_send, a_recv, PAIR, delta, to_core))
    own_a = pltpu.make_async_copy(
        kv_out.at[0, :, pl.ds(pl.multiple_of(core * PAIR, 128), PAIR)], kv_got.at[0, core], local_sem.at[0]
    )
    own_a.start()

    for part in range(8):
        columns = slice(part * 512, part * 512 + 512)
        chosen = dot(choose, queries_ref[:, columns]).astype(jnp.bfloat16)
        for delta in range(8):
            q_out[delta, :, columns] = chosen[delta * SLOT : (delta + 1) * SLOT, :]
    start(out_copy(q_out, q_got, q_send, q_recv, HALF, 0, other))
    for chunk in range(SLOT // 16):
        for delta in order:
            for to_core in range(2):
                columns = pl.ds(to_core * HALF, HALF)
                rows = pl.ds(chunk * 16, 16)
                remote(
                    q_out.at[delta, rows, columns],
                    q_got.at[delta, core, rows],
                    q_send.at[delta * 2 + to_core],
                    q_recv.at[delta, core],
                    moved(mine, delta, to_core),
                ).start()
    for delta in order:
        for to_core in range(2):
            copies.append(out_copy(q_out, q_got, q_send, q_recv, HALF, delta, to_core))
    own_q = pltpu.make_async_copy(
        q_out.at[0, :, pl.ds(pl.multiple_of(core * HALF, 128), HALF)], q_got.at[0, core], local_sem.at[1]
    )
    own_q.start()

    own_a.wait()
    landed(kv_got, a_send, a_recv, 0, other)
    for delta in range(1, 8):
        for source in range(2):
            landed(kv_got, a_send, a_recv, delta, source)

    def fields_of(table):
        fields = table.reshape(ROWS, 128).astype(jnp.float32)
        flat = fields.T
        out = []
        for lead, low in ((fields[:, 0:1], fields[:, 1:2]), (flat[0:1, :], flat[1:2, :])):
            lead = lead.astype(jnp.int32)
            out.append((lead > 0, (lead - 1) * 256 + low.astype(jnp.int32)))
        return out

    def holder_of(u):
        block = u >> 8
        return jnp.where(block < 8, block, 15 - block)

    (valid_c, u_c), (valid_r, u_r) = fields_of(kv_got[:, :, :, 512:])
    key_c = jnp.where(valid_c, holder_of(u_c), -1)
    key_r = jnp.where(valid_r, holder_of(u_r), -2)
    key_ref[...] = jnp.broadcast_to(key_c, (ROWS, 128))

    def count_before(step, total):
        base = pl.multiple_of(step * 128, 128)
        chunk = key_ref[pl.ds(base, 128), 0:1]
        hits = (chunk == key_r) & (iota((128, ROWS), 0) + base < iota((128, ROWS), 1))
        return total + jnp.sum(jnp.where(hits, 1, 0), 0, keepdims=True)

    before = lax.fori_loop(0, ROWS // 128, count_before, jnp.zeros((1, ROWS), jnp.int32))
    target = jnp.where(valid_r, key_r * PART + before, -1)

    def fill(step, carry):
        base = pl.multiple_of(step * 4 * PART, 4 * PART)
        rows = dot(bf16(iota((4 * PART, ROWS), 0) + base == target), kv_got[...].reshape(ROWS, PAIR))
        part_out[pl.ds(step * 4, 4)] = rows.astype(jnp.bfloat16).reshape(4, PART, PAIR)
        return carry

    lax.fori_loop(0, 2, fill, 0)

    def flip(mask):
        out = 0
        for bit in (4, 2, 1):
            digit = place // bit % 2
            out = out + bit * ((1 - digit) if mask & bit else digit)
        return out

    for mask in order:
        start(
            remote(
                part_out.at[flip(mask)], part_got.at[place], b_send.at[mask], b_recv.at[mask], across_cycle(mask)
            )
        )
    part_got[place] = part_out[place]

    index_c, index_r = iota((ROWS, 1), 0), iota((1, ROWS), 1)
    key_c = jnp.where(valid_c, u_c, 4096 + index_c)
    key_r = jnp.where(valid_r, u_r, 4096 + index_r)
    key_ref[...] = jnp.broadcast_to(key_c, (ROWS, 128))

    def rank_step(step, total):
        base = pl.multiple_of(step * 128, 128)
        chunk = key_ref[pl.ds(base, 128), 0:1]
        counts = jnp.sum(jnp.where(key_r < chunk, 1, 0), 1, keepdims=True)
        rank_ref[pl.ds(base, 128), :] = jnp.broadcast_to(counts, (128, 128))
        return total + jnp.sum(jnp.where(chunk < key_r, 1, 0), 0, keepdims=True)

    rank_r = lax.fori_loop(0, ROWS // 128, rank_step, jnp.zeros((1, ROWS), jnp.int32))

    def sort_step(step, total):
        base = pl.multiple_of(step * 128, 128)
        chunk = key_ref[pl.ds(base, 128), 0:1]
        ranks = rank_ref[pl.ds(base, 128), 0:1]
        return total + jnp.sum(jnp.where(ranks == iota((128, ROWS), 1), chunk, 0), 0, keepdims=True)

    sorted_r = lax.fori_loop(0, ROWS // 128, sort_step, jnp.zeros((1, ROWS), jnp.int32))

    @pl.when(at_home)
    def _():
        len_got[...] = len_out[...]

    @pl.when(jnp.logical_not(at_home))
    def _():
        lengths_copy().wait()

    lengths = len_got[...]
    begin_r = jnp.where(sorted_r < 4096, document_start(sorted_r, lengths), 8192)

    own_tile = iota((ROWS // TILE, ROWS), 1) >> TILE_BITS == iota((ROWS // TILE, ROWS), 0)
    spread = bf16(iota((ROWS, TILE * 8), 0) & (TILE - 1) == iota((ROWS, TILE * 8), 1) & (TILE - 1))
    for values, tiles_ref in ((sorted_r, last_ref), (begin_r, begin_ref)):
        parts = [
            dot(jnp.where(own_tile, half, 0).astype(jnp.float32).astype(jnp.bfloat16), spread).astype(jnp.int32)
            for half in (values >> 8, values & 255)
        ]
        tiles_ref[...] = parts[0] * 256 + parts[1]

    def turn_step(step, carry):
        low, high = carry
        base = pl.multiple_of(step * 128, 128)
        hits = iota((128, ROWS), 0) + base == rank_r
        u = jnp.sum(jnp.where(hits, key_r, 0), 1, keepdims=True)
        live = u < 4096
        start = document_start(u, lengths)
        index, tile = iota((128, 128), 0) + base, iota((128, 128), 1)
        low = low + jnp.sum(jnp.where((index == tile * TILE) & live, start >> 8, 0), 0, keepdims=True)
        high = jnp.maximum(
            high, jnp.max(jnp.where((index >> TILE_BITS == tile) & live, u >> 8, -1), 0, keepdims=True)
        )
        cos, sin = turning(jnp.where(live, u - start, 0))
        cos_ref[pl.ds(base, 128), :] = cos * SCALE
        sin_ref[pl.ds(base, 128), :] = sin * SCALE
        return low, high

    low, high = lax.fori_loop(
        0, ROWS // 128, turn_step, (jnp.zeros((1, 128), jnp.int32), jnp.full((1, 128), -1, jnp.int32))
    )
    bounds_ref[...] = jnp.zeros_like(bounds_ref)
    bounds_ref[0:1, :] = low
    bounds_ref[1:2, :] = high
    rows_c = iota((KEYS, 1), 0)
    key_u = jnp.where(rows_c < BLOCK, place * BLOCK + rows_c, (15 - place) * BLOCK + rows_c - BLOCK)
    key_cos, key_sin = turning(key_u - document_start(key_u, lengths))

    for mask in range(1, 8):
        here = part_got.at[flip(mask)]
        remote(here, here, b_send.at[mask], b_recv.at[mask], across_cycle(mask)).wait_recv()

    _, (valid, u) = fields_of(part_got[:, :, 512:])
    target = jnp.where(valid, jnp.where(u >= 2048, BLOCK, 0) + (u & 255), -1)
    placed = dot(bf16(iota((KEYS, ROWS), 0) == target), part_got[:, :, :512].reshape(ROWS, 512))
    for head in range(2):
        columns = slice(head * HEAD_SIZE, (head + 1) * HEAD_SIZE)
        entry = placed[:, columns]
        entry = entry * key_cos + pltpu.roll(entry, HEAD_SIZE // 2, 1) * key_sin
        own_ref[:, columns] = entry.astype(jnp.bfloat16)
    for half in range(2):
        rows = slice(half * BLOCK, (half + 1) * BLOCK)
        own_ref[rows, 256:] = placed[rows, 256:].T.astype(jnp.bfloat16)

    own_kv = pltpu.make_async_copy(own_ref, all_ref.at[place], local_sem.at[2])
    own_kv.start()

    def kv_copy(third, index):
        start, size, (b1, b2, b3) = THIRDS[third]
        mask, axis = ((0, b1), (0, b2), (0, b3), (b1, b2), (b1, b3), (b2, b3), (b1 ^ b2, b3))[index]
        rows = pl.ds(start, size)
        block = flip(mask)
        src = own_ref.at[rows] if mask == 0 else all_ref.at[block, rows]
        return remote(
            src, all_ref.at[block, rows], kv_send.at[third, index], kv_recv.at[third, index], across_cycle(axis)
        )

    def kv_landed(third, index):
        start, size, (b1, b2, b3) = THIRDS[third]
        mask = (b1, b2, b3, b1 ^ b2, b1 ^ b3, b2 ^ b3, 7)[index]
        here = all_ref.at[flip(mask), pl.ds(start, size)]
        remote(here, here, kv_send.at[third, index], kv_recv.at[third, index], across_cycle(4)).wait_recv()

    for index in range(3):
        for third in range(3):
            start(kv_copy(third, index))

    landed(q_got, q_send, q_recv, 0, other)
    for delta in range(1, 8):
        for source in range(2):
            landed(q_got, q_send, q_recv, delta, source)
    own_q.wait()

    def order_queries(sup):
        base = sup * SUPER
        pick = bf16(iota((SUPER, ROWS), 0) + base == rank_r)
        cos = cos_ref[base : base + SUPER, :]
        sin = sin_ref[base : base + SUPER, :]

        def one_part(part, carry):
            columns = pl.ds(pl.multiple_of(part * 256, 256), 256)
            rows = dot(pick, q_got[:, :, :, columns].reshape(ROWS, 256))
            for one in range(2):
                entry = rows[:, one * HEAD_SIZE : (one + 1) * HEAD_SIZE]
                entry = entry * cos + pltpu.roll(entry, HEAD_SIZE // 2, 1) * sin
                entry = entry.astype(jnp.bfloat16)
                first = pl.multiple_of((part % 4 * 2 + one) * TILE, TILE)
                for tile in range(SUPER // TILE):
                    sorted_ref[part // 4, sup * (SUPER // TILE) + tile, pl.ds(first, TILE), :] = entry[
                        tile * TILE : (tile + 1) * TILE
                    ]
            return carry

        lax.fori_loop(0, 8, one_part, 0)
        turned_copy(sup).start()

    def turned_copy(sup):
        tiles = pl.ds(sup * (SUPER // TILE), SUPER // TILE)
        return pltpu.make_async_copy(sorted_ref.at[:, tiles], turned_ref.at[:, tiles], out_sem.at[sup])

    for third in range(3):
        kv_landed(third, 0)
        start(kv_copy(third, 3))
        start(kv_copy(third, 4))
    for third in range(3):
        kv_landed(third, 1)
        start(kv_copy(third, 5))
    order_queries(0)
    for third in range(3):
        kv_landed(third, 3)
        start(kv_copy(third, 6))
    for sup in range(1, 4):
        order_queries(sup)
    for index in (2, 4, 5, 6):
        for third in range(3):
            kv_landed(third, index)
    own_kv.wait()
    for sup in range(4):
        turned_copy(sup).wait()
    for copy in copies:
        copy.wait_send()


def across_cycle(mask):
    x, y, z, core = coords()
    return device(x + 2 * (mask // 4), y + 2 * (mask // 2 % 2), z + 2 * (mask % 2), core)


def exchange(queries, keys, values, plan_row, lengths):
    vmem = pl.BlockSpec(memory_space=pltpu.VMEM)
    dma = pltpu.SemaphoreType.DMA
    return pl.pallas_call(
        exchange_kernel,
        out_shape=(
            jax.ShapeDtypeStruct((2, ROWS // TILE, TILE * 8, HEAD_SIZE), jnp.bfloat16),
            jax.ShapeDtypeStruct((8, KEYS, 512), jnp.bfloat16),
            jax.ShapeDtypeStruct((ROWS // TILE, TILE * 8), jnp.int32),
            jax.ShapeDtypeStruct((ROWS // TILE, TILE * 8), jnp.int32),
            jax.ShapeDtypeStruct((8, 128), jnp.int32),
            jax.ShapeDtypeStruct((ROWS, 128), jnp.int32),
        ),
        in_specs=[vmem] * 5,
        out_specs=[pl.BlockSpec(memory_space=pl.ANY)] * 2 + [vmem] * 4,
        scratch_shapes=[
            pltpu.VMEM((8, SLOT, 2 * HALF), jnp.bfloat16),
            pltpu.VMEM((8, 2, SLOT, HALF), jnp.bfloat16),
            pltpu.VMEM((8, SLOT, 2 * PAIR), jnp.bfloat16),
            pltpu.VMEM((8, 2, SLOT, PAIR), jnp.bfloat16),
            pltpu.VMEM((8, PART, PAIR), jnp.bfloat16),
            pltpu.VMEM((8, PART, PAIR), jnp.bfloat16),
            pltpu.VMEM((KEYS, 512), jnp.bfloat16),
            pltpu.VMEM((8, 128), jnp.int32),
            pltpu.VMEM((8, 128), jnp.int32),
            pltpu.VMEM((ROWS, 128), jnp.int32),
            pltpu.VMEM((ROWS, HEAD_SIZE), jnp.float32),
            pltpu.VMEM((ROWS, HEAD_SIZE), jnp.float32),
            pltpu.VMEM((2, ROWS // TILE, TILE * 8, HEAD_SIZE), jnp.bfloat16),
            dma((16,)), dma((8, 2)), dma((16,)), dma((8, 2)), dma((8,)), dma((8,)), dma((3, 7)), dma((3, 7)),
            dma(()), dma(()), dma((3,)), dma((4,)),
        ],
        compiler_params=pltpu.CompilerParams(
            collective_id=0, has_side_effects=True, vmem_limit_bytes=VMEM_LIMIT
        ),
        name="exchange",
    )(queries, keys, values, plan_row, lengths)


def back_kernel(made_ref, rank_ref, ret_ref, send_ref, send, recv, local_sem):
    x, y, z, core = coords()
    mine = sign_of(core)
    other = 1 - core
    for delta in range(1, 8):
        for worker in range(2):
            signal(moved(mine, delta, worker))
    signal(moved(0, 0, other))

    columns = pl.ds(pl.multiple_of(core * HALF, 128), HALF)

    def place_rows(first):
        rows = slice(first * 2 * SLOT, first * 2 * SLOT + 4 * SLOT)
        put = bf16(rank_ref[rows, 0:1] == iota((4 * SLOT, ROWS), 1))

        def one_part(part, carry):
            here = pl.ds(pl.multiple_of(part * 512, 512), 512)
            chosen = dot(put, made_ref[:, here]).astype(jnp.bfloat16)
            for one in range(4):
                send_ref[first + one // 2, one % 2, :, here] = chosen[one * SLOT : (one + 1) * SLOT, :]
            return carry

        lax.fori_loop(0, 4, one_part, 0)

    copies = []

    def back_copy(delta, source, first, size):
        rows = pl.ds(first, size)
        return remote(
            send_ref.at[delta, source, rows],
            ret_ref.at[delta, rows, columns],
            send.at[delta * 2 + source],
            recv.at[delta, core],
            moved(-sign_of(source), delta, source),
        )

    place_rows(6)
    pl.semaphore_wait(pltpu.get_barrier_semaphore(), 15)
    for first in (6, 4, 2, 0):
        if first < 6:
            place_rows(first)
        deltas = [delta for delta in (first + 1, first) if delta]
        for chunk in range(SLOT // 16):
            for delta in deltas:
                for source in range(2):
                    back_copy(delta, source, chunk * 16, 16).start()
        for delta in deltas:
            for source in range(2):
                copies.append(back_copy(delta, source, 0, SLOT))
    own = pltpu.make_async_copy(send_ref.at[0, core], ret_ref.at[0, :, columns], local_sem)
    own.start()
    copy = remote(
        send_ref.at[0, other], ret_ref.at[0, :, columns], send.at[0], recv.at[0, core], moved(0, 0, other)
    )
    copy.start()
    copies.append(copy)

    def landed(delta, worker):
        here = ret_ref.at[delta, :, pl.ds(pl.multiple_of(worker * HALF, 128), HALF)]
        remote(here, here, send.at[0], recv.at[delta, worker], moved(0, 0, other)).wait_recv()

    own.wait()
    landed(0, other)
    for delta in range(1, 8):
        for worker in range(2):
            landed(delta, worker)

    for copy in copies:
        copy.wait_send()


def back(made, rank):
    vmem = pl.BlockSpec(memory_space=pltpu.VMEM)
    return pl.pallas_call(
        back_kernel,
        out_shape=jax.ShapeDtypeStruct((8, SLOT, 2 * HALF), jnp.bfloat16),
        in_specs=[vmem] * 2,
        out_specs=pl.BlockSpec(memory_space=pl.ANY),
        scratch_shapes=[
            pltpu.VMEM((8, 2, SLOT, HALF), jnp.bfloat16),
            pltpu.SemaphoreType.DMA((16,)),
            pltpu.SemaphoreType.DMA((8, 2)),
            pltpu.SemaphoreType.DMA(()),
        ],
        compiler_params=pltpu.CompilerParams(
            collective_id=1, has_side_effects=True, vmem_limit_bytes=VMEM_LIMIT
        ),
        name="back",
    )(made, rank)


def restore_kernel(cycle_ref, plan_row, ret_ref, out_ref, choose_ref):
    @pl.when(pl.program_id(0) == 0)
    def _():
        plan_r = plan_row[...]
        plan_c = column_of(plan_r)
        same = (cycle_of(plan_c) == cycle_of(plan_r)) & (iota((TOK, TOK), 1) < iota((TOK, TOK), 0))
        rank = jnp.sum(jnp.where(same, 1, 0), 1, keepdims=True)
        row = jnp.bitwise_xor(cycle_of(plan_c), cycle_ref[0]) * SLOT + rank
        choose_ref[...] = bf16(iota((TOK, 8 * SLOT), 1) == row)

    rows = ret_ref[...].reshape(8 * SLOT, ret_ref.shape[2])
    out_ref[...] = dot(choose_ref[...], rows).astype(jnp.bfloat16)


def restore(my_cycle, plan_row, ret):
    width = 1024
    return pl.pallas_call(
        restore_kernel,
        grid=(2 * HALF // width,),
        out_shape=jax.ShapeDtypeStruct((TOK, 2 * HALF), jnp.bfloat16),
        in_specs=[
            pl.BlockSpec(memory_space=pltpu.SMEM),
            pl.BlockSpec((1, TOK), lambda i: (0, 0)),
            pl.BlockSpec((8, SLOT, width), lambda i: (0, 0, i)),
        ],
        out_specs=pl.BlockSpec((TOK, width), lambda i: (0, i)),
        scratch_shapes=[pltpu.VMEM((TOK, 8 * SLOT), jnp.bfloat16)],
        compiler_params=pltpu.CompilerParams(vmem_limit_bytes=VMEM_LIMIT),
        name="restore",
    )(my_cycle, plan_row, ret)


def attend_kernel(
    bounds_ref, last_ref, begin_ref, turned_ref, all_ref,
    made_ref, turned, kv_ref, made, peak, total, summed, decays, scores0, scores1, weights0, weights1, items, in_sem, out_sem,
):
    across = iota((BLOCK, TILE * 8), 0)
    tiles = ROWS // TILE
    loads = (
        pltpu.make_async_copy(turned_ref, turned, in_sem.at[0]),
        pltpu.make_async_copy(all_ref, kv_ref, in_sem.at[1]),
    )
    for load in loads:
        load.start()

    def store(tile):
        rows = pl.ds(pl.multiple_of(tile * TILE, TILE), TILE)
        return pltpu.make_async_copy(made.at[rows], made_ref.at[rows], out_sem)

    def list_tile(tile, count):
        low = bounds_ref[0, tile]
        high = bounds_ref[1, tile]

        def list_block(block, count):
            items[0, count] = tile
            items[1, count] = block
            items[2, count] = (block == low).astype(jnp.int32)
            items[3, count] = (block == high).astype(jnp.int32)
            return count + 1

        @pl.when(high < low)
        def _():
            made[pl.ds(pl.multiple_of(tile * TILE, TILE), TILE), :] = jnp.zeros((TILE, HALF), jnp.bfloat16)
            store(tile).start()

        return lax.fori_loop(low, high + 1, list_block, count)

    count = lax.fori_loop(0, tiles, list_tile, 0)
    for extra in range(3):
        items[0, count + extra] = items[0, count - 1]
        items[1, count + extra] = 32
        items[2, count + extra] = 0
        items[3, count + extra] = 0

    peak[...] = jnp.full_like(peak, NEG)
    summed[...] = jnp.zeros_like(summed)
    total[...] = jnp.zeros_like(total)
    decays[...] = jnp.ones_like(decays)
    weights1[...] = jnp.zeros_like(weights1)
    for load in loads:
        load.wait()

    def spot(block):
        block = jnp.minimum(block, 15)
        return jnp.where(block < 8, block, 15 - block), jnp.where(block < 8, 0, BLOCK)

    def score_of(item, scores):
        tile, block = items[0, item], items[1, item]
        begin = begin_ref[pl.ds(tile, 1), :]
        span = jnp.maximum(last_ref[pl.ds(tile, 1), :] - begin + 1, 0).astype(jnp.uint32)
        holder, row = spot(block)
        allowed = (across + (block * BLOCK - begin)).astype(jnp.uint32) < span
        for head in range(2):
            key = kv_ref[
                holder,
                pl.ds(pl.multiple_of(row, BLOCK), BLOCK),
                head * HEAD_SIZE : (head + 1) * HEAD_SIZE,
            ]
            score = lax.dot_general(
                key, turned[head, tile], (((1,), (1,)), ((), ())), preferred_element_type=jnp.float32
            )
            scores[head] = jnp.where(allowed, score, NEG)

    def weigh(item, scores, weights):
        opens = items[2, item] == 1
        for head in range(2):
            score = scores[head]
            old = jnp.where(opens, NEG, peak[head])
            new = jnp.maximum(old, jnp.max(score, 0, keepdims=True))
            decay = jnp.where(opens, 0.0, jnp.exp2(old - new))
            peak[head] = new
            weight = jnp.exp2(score - new)
            summed[head] = summed[head] * decay + jnp.sum(weight, 0, keepdims=True)
            weights[head] = weight.astype(jnp.bfloat16)
            decays[head] = decay

    def add(item, weights):
        holder, row = spot(items[1, item])
        for head in range(2):
            value = kv_ref[
                holder,
                pl.ds(pl.multiple_of(row + head * HEAD_SIZE, HEAD_SIZE), HEAD_SIZE),
                2 * HEAD_SIZE :,
            ]
            total[head] = total[head] * decays[head] + jnp.dot(
                value, weights[head], preferred_element_type=jnp.float32
            )

    score_of(0, scores0)

    def two_steps(pair, carry):
        item = pair * 2
        add(jnp.maximum(item - 1, 0), weights1)
        score_of(item + 1, scores1)
        keep = summed[...]
        weigh(item, scores0, weights0)
        close_after(item - 1, keep)
        add(item, weights0)
        score_of(item + 2, scores0)
        keep = summed[...]
        weigh(item + 1, scores1, weights1)
        close_after(item, keep)
        return carry

    def close_after(item, sums):
        at = jnp.maximum(item, 0)

        @pl.when((items[3, at] == 1) & (item >= 0))
        def _():
            there = pl.multiple_of(items[0, at] * TILE, TILE)
            for head in range(2):
                result = (total[head] / jnp.maximum(sums[head], 1e-30)).T.astype(jnp.bfloat16)
                for one in range(8):
                    made[pl.ds(there, TILE), pl.ds((head * 8 + one) * HEAD_SIZE, HEAD_SIZE)] = result[
                        one * TILE : (one + 1) * TILE
                    ]
            store(items[0, at]).start()

    lax.fori_loop(0, (count + 2) // 2, two_steps, 0)
    pltpu.make_async_copy(made, made_ref, out_sem).wait()


def attend(bounds, last, begin, q, kv):
    smem = pl.BlockSpec(memory_space=pltpu.SMEM)
    vmem = pl.BlockSpec(memory_space=pltpu.VMEM)
    hbm = pl.BlockSpec(memory_space=pl.ANY)
    lanes = TILE * 8
    return pl.pallas_call(
        attend_kernel,
        out_shape=jax.ShapeDtypeStruct((ROWS, HALF), jnp.bfloat16),
        in_specs=[smem, vmem, vmem, hbm, hbm],
        out_specs=hbm,
        scratch_shapes=[
            pltpu.VMEM((2, ROWS // TILE, lanes, HEAD_SIZE), jnp.bfloat16),
            pltpu.VMEM((8, KEYS, 512), jnp.bfloat16),
            pltpu.VMEM((ROWS, HALF), jnp.bfloat16),
            pltpu.VMEM((2, 1, lanes), jnp.float32),
            pltpu.VMEM((2, HEAD_SIZE, lanes), jnp.float32),
            pltpu.VMEM((2, 1, lanes), jnp.float32),
            pltpu.VMEM((2, 1, lanes), jnp.float32),
            pltpu.VMEM((2, BLOCK, lanes), jnp.float32),
            pltpu.VMEM((2, BLOCK, lanes), jnp.float32),
            pltpu.VMEM((2, BLOCK, lanes), jnp.bfloat16),
            pltpu.VMEM((2, BLOCK, lanes), jnp.bfloat16),
            pltpu.SMEM((4, ROWS // TILE * 16 + 4), jnp.int32),
            pltpu.SemaphoreType.DMA((2,)),
            pltpu.SemaphoreType.DMA(()),
        ],
        compiler_params=pltpu.CompilerParams(vmem_limit_bytes=VMEM_LIMIT),
        name="attend",
    )(bounds, last, begin, q, kv)


def local(queries, keys, values, plan, doc_lengths):
    x, y, z, _ = coords()
    my_cycle = x % 2 * 4 + y % 2 * 2 + z % 2
    plan_row = plan[None, :]
    q, kv, last, begin, bounds, rank = exchange(queries, keys, values, plan_row, doc_lengths)
    made = attend(bounds, last, begin, q, kv)
    ret = back(made, rank)
    return restore(jnp.reshape(my_cycle, (1,)).astype(jnp.int32), plan_row, ret)


def solution(mesh):
    return jax.shard_map(
        local,
        mesh=mesh,
        in_specs=(
            P(("blk", "group"), None),
            P(("blk", "group"), None),
            P(("blk", "group"), None),
            P(("blk", "group")),
            P("group", None),
        ),
        out_specs=P(("blk", "group"), None),
        check_vma=False,
    )
```

```python
import math

import jax
import jax.numpy as jnp
from jax import lax
from jax.experimental import pallas as pl
from jax.experimental.pallas import tpu as pltpu
from jax.sharding import PartitionSpec as P

QUERY_HEADS = 32
KEY_VALUE_HEADS = 4
HEAD_SIZE = 128
THETA = 500000.0

TOK = 256
SLOT = 64
KEYS = 512
BLOCK = 256
TILE = 64
TILE_BITS = 6
SUPER = 256
HALF = QUERY_HEADS // 2 * HEAD_SIZE
WIDE = HALF + 128
ROWS = 16 * SLOT
NEG = -1e30
SCALE = math.log2(math.e) / math.sqrt(HEAD_SIZE)
MESH = pl.DeviceIdType.MESH
VMEM_LIMIT = 60 * 1024 * 1024


def coords():
    b = lax.axis_index("blk")
    g = lax.axis_index("group")
    return b // 4, g % 4, (b // 2) % 2 * 2 + g // 4, b % 2


def device(x, y, z, core):
    x, y, z = lax.rem(x + 4, 4), lax.rem(y + 4, 4), lax.rem(z + 4, 4)
    return x * 4 + z // 2 * 2 + core, lax.rem(z, 2) * 4 + y


def moved(sign, delta, core):
    x, y, z, _ = coords()
    return device(x + sign * (delta // 4), y + sign * (delta // 2 % 2), z + sign * (delta % 2), core)


def sign_of(core):
    return 1 - 2 * core


def signal(target):
    pl.semaphore_signal(pltpu.get_barrier_semaphore(), inc=1, device_id=target, device_id_type=MESH)


def remote(src, dst, send, recv, target):
    return pltpu.make_async_remote_copy(
        src_ref=src, dst_ref=dst, send_sem=send, recv_sem=recv, device_id=target, device_id_type=MESH
    )


THIRDS = ((0, 176, (4, 2, 1)), (176, 176, (2, 1, 4)), (352, 160, (1, 4, 2)))
PAIR = 512
PART = 128


def iota(shape, axis):
    return lax.broadcasted_iota(jnp.int32, shape, axis)


def bf16(flags):
    return jnp.where(flags, 1.0, 0.0).astype(jnp.bfloat16)


def dot(a, b):
    return jnp.dot(a, b, preferred_element_type=jnp.float32)


def cycle_of(plan):
    return (plan >> 8) & 7


def cycle_index(plan):
    p = plan >> 11
    offset = plan & 255
    return jnp.where(offset < 128, p * 128 + offset, (31 - p) * 128 + offset - 128)


def column_of(row):
    size = row.shape[1]
    return jnp.sum(jnp.where(iota((size, size), 0) == iota((size, size), 1), row, 0), 1, keepdims=True)


def document_start(u, lengths):
    end = jnp.zeros((1, 1), jnp.int32)
    start = jnp.zeros_like(u)
    for one in range(4):
        length = lengths[0:1, one : one + 1]
        end = end + length
        start = start + jnp.where(u >= end, length, 0)
    return start


def turning(position):
    half = HEAD_SIZE // 2
    lane = iota((1, HEAD_SIZE), 1)
    spot = (lane & (half - 1)).astype(jnp.float32)
    inv_freq = jnp.exp(-math.log(THETA) * (2.0 * spot / HEAD_SIZE))
    angle = position.astype(jnp.float32) * inv_freq
    both = jnp.cos(jnp.where(lane < half, angle, angle - math.pi / 2))
    other = pltpu.roll(both, half, 1)
    first = jnp.broadcast_to(lane < half, both.shape)
    return jnp.where(first, both, other), jnp.where(first, -other, both)


def exchange_kernel(
    queries_ref, keys_ref, values_ref, plan_row, lengths_ref,
    turned_ref, all_ref, last_ref, begin_ref, bounds_ref, rank_ref,
    q_out, q_got, kv_out, kv_got, part_out, part_got, f_out, f_got, g_out, g_got, own_ref, len_out, len_got, key_ref, cos_ref, sin_ref, sorted_ref,
    q_send, q_recv, a_send, a_recv, b_send, b_recv, kv_send, kv_recv, len_send, len_recv, local_sem, out_sem,
    f_send, f_recv, g_send, g_recv,
):
    x, y, z, core = coords()
    place = x // 2 * 4 + y // 2 * 2 + z // 2
    my_cycle = x % 2 * 4 + y % 2 * 2 + z % 2
    mine = sign_of(core)
    other = 1 - core

    block_at, group_at = lax.axis_index("blk"), lax.axis_index("group")
    spot = block_at // 2
    to_device = device(
        spot // 4 * 2 + group_at // 4, spot // 2 % 2 * 2 + group_at // 2 % 2, spot % 2 * 2 + group_at % 2, block_at % 2
    )
    from_block = place * 2 + core
    at_home = (from_block == block_at) & (my_cycle == group_at)

    for delta in range(1, 8):
        for source in range(2):
            signal(moved(-sign_of(source), delta, source))
    signal(moved(0, 0, other))
    for mask in range(1, 8):
        signal(across_cycle(mask))

    @pl.when(jnp.logical_not(at_home))
    def _():
        signal((from_block, my_cycle))

    len_out[...] = jnp.zeros_like(len_out)
    len_out[0:1, 0:4] = lengths_ref[...]
    plan_r = plan_row[...]
    plan_c = column_of(plan_r)
    same = (cycle_of(plan_c) == cycle_of(plan_r)) & (iota((TOK, TOK), 0) < iota((TOK, TOK), 1))
    rank = jnp.sum(jnp.where(same, 1, 0), 0, keepdims=True)
    row = jnp.bitwise_xor(cycle_of(plan_r), my_cycle) * SLOT + rank
    choose = bf16(iota((8 * SLOT, TOK), 0) == row)
    u = cycle_index(plan_c)
    lane = iota((TOK, 128), 1)
    fields = jnp.where(lane == 0, (u >> 8) + 1, jnp.where(lane == 1, u & 255, 0))
    fields = fields.astype(jnp.float32).astype(jnp.bfloat16)
    f_out[...] = dot(choose, fields).astype(jnp.bfloat16).reshape(8, SLOT, 128)

    pl.semaphore_wait(pltpu.get_barrier_semaphore(), jnp.where(at_home, 22, 23))

    copies = []

    def start(copy):
        copy.start()
        copies.append(copy)

    def lengths_copy():
        return remote(len_out, len_got, len_send, len_recv, to_device)

    @pl.when(jnp.logical_not(at_home))
    def _():
        lengths_copy().start()

    def out_copy(src, dst, send, recv, width, delta, to_core):
        columns = pl.ds(pl.multiple_of(to_core * width, 128), width)
        slot = delta * 2 + to_core if delta else 0
        return remote(
            src.at[delta, :, columns],
            dst.at[delta, core],
            send.at[slot],
            recv.at[delta, core],
            moved(mine, delta, to_core) if delta else moved(0, 0, other),
        )

    def landed(dst, send, recv, delta, source):
        here = dst.at[delta, source]
        remote(here, here, send.at[0], recv.at[delta, source], moved(0, 0, other)).wait_recv()

    order = (7, 6, 5, 3, 4, 2, 1)

    def f_copy(delta, to_core):
        return remote(
            f_out.at[delta],
            f_got.at[delta, core],
            f_send.at[delta * 2 + to_core if delta else 0],
            f_recv.at[delta, core],
            moved(mine, delta, to_core),
        )

    start(f_copy(0, other))
    for delta in order:
        for to_core in range(2):
            start(f_copy(delta, to_core))
    f_got[0, core] = f_out[0]

    chosen_k = dot(choose, keys_ref[...]).astype(jnp.bfloat16)
    chosen_v = dot(choose, values_ref[...]).astype(jnp.bfloat16)
    for delta in range(8):
        rows = slice(delta * SLOT, (delta + 1) * SLOT)
        for half in range(2):
            kv_out[delta, :, half * PAIR : half * PAIR + 256] = chosen_k[rows, half * 256 : half * 256 + 256]
            kv_out[delta, :, half * PAIR + 256 : half * PAIR + 512] = chosen_v[rows, half * 256 : half * 256 + 256]
    start(out_copy(kv_out, kv_got, a_send, a_recv, PAIR, 0, other))
    for delta in order:
        for to_core in range(2):
            start(out_copy(kv_out, kv_got, a_send, a_recv, PAIR, delta, to_core))
    own_a = pltpu.make_async_copy(
        kv_out.at[0, :, pl.ds(pl.multiple_of(core * PAIR, 128), PAIR)], kv_got.at[0, core], local_sem.at[0]
    )
    own_a.start()

    for part in range(8):
        columns = slice(part * 512, part * 512 + 512)
        chosen = dot(choose, queries_ref[:, columns]).astype(jnp.bfloat16)
        for delta in range(8):
            q_out[delta, :, columns] = chosen[delta * SLOT : (delta + 1) * SLOT, :]
    start(out_copy(q_out, q_got, q_send, q_recv, HALF, 0, other))
    def send_queries(chunk):
        for delta in order:
            for to_core in range(2):
                columns = pl.ds(to_core * HALF, HALF)
                rows = pl.ds(chunk * 16, 16)
                remote(
                    q_out.at[delta, rows, columns],
                    q_got.at[delta, core, rows],
                    q_send.at[delta * 2 + to_core],
                    q_recv.at[delta, core],
                    moved(mine, delta, to_core),
                ).start()

    send_queries(0)
    for delta in order:
        for to_core in range(2):
            copies.append(out_copy(q_out, q_got, q_send, q_recv, HALF, delta, to_core))
    own_q = pltpu.make_async_copy(
        q_out.at[0, :, pl.ds(pl.multiple_of(core * HALF, 128), HALF)], q_got.at[0, core], local_sem.at[1]
    )
    own_q.start()

    landed(f_got, f_send, f_recv, 0, other)
    for delta in range(1, 8):
        for source in range(2):
            landed(f_got, f_send, f_recv, delta, source)

    def fields_of(table):
        fields = table.reshape(ROWS, 128).astype(jnp.float32)
        flat = fields.T
        out = []
        for lead, low in ((fields[:, 0:1], fields[:, 1:2]), (flat[0:1, :], flat[1:2, :])):
            lead = lead.astype(jnp.int32)
            out.append((lead > 0, (lead - 1) * 256 + low.astype(jnp.int32)))
        return out

    def holder_of(u):
        block = u >> 8
        return jnp.where(block < 8, block, 15 - block)

    (valid_c, u_c), (valid_r, u_r) = fields_of(f_got[...])
    key_c = jnp.where(valid_c, holder_of(u_c), -1)
    key_r = jnp.where(valid_r, holder_of(u_r), -2)
    key_ref[...] = jnp.broadcast_to(key_c, (ROWS, 128))

    def count_before(step, total):
        base = pl.multiple_of(step * 128, 128)
        chunk = key_ref[pl.ds(base, 128), 0:1]
        hits = (chunk == key_r) & (iota((128, ROWS), 0) + base < iota((128, ROWS), 1))
        return total + jnp.sum(jnp.where(hits, 1, 0), 0, keepdims=True)

    before = lax.fori_loop(0, ROWS // 128, count_before, jnp.zeros((1, ROWS), jnp.int32))
    target = jnp.where(valid_r, key_r * PART + before, -1)

    def flip(mask):
        out = 0
        for bit in (4, 2, 1):
            digit = place // bit % 2
            out = out + bit * ((1 - digit) if mask & bit else digit)
        return out

    def place_fields(step, carry):
        base = pl.multiple_of(step * 4 * PART, 4 * PART)
        rows = dot(bf16(iota((4 * PART, ROWS), 0) + base == target), f_got[...].reshape(ROWS, 128))
        g_out[pl.ds(step * 4, 4)] = rows.astype(jnp.bfloat16).reshape(4, PART, 128)
        return carry

    lax.fori_loop(0, 2, place_fields, 0)
    for mask in order:
        start(remote(g_out.at[flip(mask)], g_got.at[place], g_send.at[mask], g_recv.at[mask], across_cycle(mask)))
    send_queries(1)
    g_got[place] = g_out[place]

    own_a.wait()
    landed(kv_got, a_send, a_recv, 0, other)
    for delta in range(1, 8):
        for source in range(2):
            landed(kv_got, a_send, a_recv, delta, source)

    def fill(step, carry):
        base = pl.multiple_of(step * 4 * PART, 4 * PART)
        rows = dot(bf16(iota((4 * PART, ROWS), 0) + base == target), kv_got[...].reshape(ROWS, PAIR))
        part_out[pl.ds(step * 4, 4)] = rows.astype(jnp.bfloat16).reshape(4, PART, PAIR)
        return carry

    lax.fori_loop(0, 2, fill, 0)

    for mask in order:
        start(
            remote(
                part_out.at[flip(mask)], part_got.at[place], b_send.at[mask], b_recv.at[mask], across_cycle(mask)
            )
        )
    send_queries(2)
    part_got[place] = part_out[place]

    index_c, index_r = iota((ROWS, 1), 0), iota((1, ROWS), 1)
    key_c = jnp.where(valid_c, u_c, 4096 + index_c)
    key_r = jnp.where(valid_r, u_r, 4096 + index_r)
    key_ref[...] = jnp.broadcast_to(key_c, (ROWS, 128))

    def rank_step(step, total):
        base = pl.multiple_of(step * 128, 128)
        chunk = key_ref[pl.ds(base, 128), 0:1]
        counts = jnp.sum(jnp.where(key_r < chunk, 1, 0), 1, keepdims=True)
        rank_ref[pl.ds(base, 128), :] = jnp.broadcast_to(counts, (128, 128))
        return total + jnp.sum(jnp.where(chunk < key_r, 1, 0), 0, keepdims=True)

    rank_r = lax.fori_loop(0, ROWS // 128, rank_step, jnp.zeros((1, ROWS), jnp.int32))

    def sort_step(step, total):
        base = pl.multiple_of(step * 128, 128)
        chunk = key_ref[pl.ds(base, 128), 0:1]
        ranks = rank_ref[pl.ds(base, 128), 0:1]
        return total + jnp.sum(jnp.where(ranks == iota((128, ROWS), 1), chunk, 0), 0, keepdims=True)

    sorted_r = lax.fori_loop(0, ROWS // 128, sort_step, jnp.zeros((1, ROWS), jnp.int32))

    @pl.when(at_home)
    def _():
        len_got[...] = len_out[...]

    @pl.when(jnp.logical_not(at_home))
    def _():
        lengths_copy().wait()

    lengths = len_got[...]
    begin_r = jnp.where(sorted_r < 4096, document_start(sorted_r, lengths), 8192)

    own_tile = iota((ROWS // TILE, ROWS), 1) >> TILE_BITS == iota((ROWS // TILE, ROWS), 0)
    spread = bf16(iota((ROWS, TILE * 8), 0) & (TILE - 1) == iota((ROWS, TILE * 8), 1) & (TILE - 1))
    for values, tiles_ref in ((sorted_r, last_ref), (begin_r, begin_ref)):
        parts = [
            dot(jnp.where(own_tile, half, 0).astype(jnp.float32).astype(jnp.bfloat16), spread).astype(jnp.int32)
            for half in (values >> 8, values & 255)
        ]
        tiles_ref[...] = parts[0] * 256 + parts[1]

    def turn_step(step, carry):
        low, high = carry
        base = pl.multiple_of(step * 128, 128)
        hits = iota((128, ROWS), 0) + base == rank_r
        u = jnp.sum(jnp.where(hits, key_r, 0), 1, keepdims=True)
        live = u < 4096
        start = document_start(u, lengths)
        index, tile = iota((128, 128), 0) + base, iota((128, 128), 1)
        low = low + jnp.sum(jnp.where((index == tile * TILE) & live, start >> 8, 0), 0, keepdims=True)
        high = jnp.maximum(
            high, jnp.max(jnp.where((index >> TILE_BITS == tile) & live, u >> 8, -1), 0, keepdims=True)
        )
        cos, sin = turning(jnp.where(live, u - start, 0))
        cos_ref[pl.ds(base, 128), :] = cos * SCALE
        sin_ref[pl.ds(base, 128), :] = sin * SCALE
        return low, high

    low, high = lax.fori_loop(
        0, ROWS // 128, turn_step, (jnp.zeros((1, 128), jnp.int32), jnp.full((1, 128), -1, jnp.int32))
    )
    bounds_ref[...] = jnp.zeros_like(bounds_ref)
    bounds_ref[0:1, :] = low
    bounds_ref[1:2, :] = high
    rows_c = iota((KEYS, 1), 0)
    key_u = jnp.where(rows_c < BLOCK, place * BLOCK + rows_c, (15 - place) * BLOCK + rows_c - BLOCK)
    key_cos, key_sin = turning(key_u - document_start(key_u, lengths))

    for mask in range(1, 8):
        here = g_got.at[flip(mask)]
        remote(here, here, g_send.at[mask], g_recv.at[mask], across_cycle(mask)).wait_recv()
    _, (valid, u) = fields_of(g_got[...])
    target = jnp.where(valid, jnp.where(u >= 2048, BLOCK, 0) + (u & 255), -1)
    arrange = bf16(iota((KEYS, ROWS), 0) == target)

    for mask in range(1, 8):
        here = part_got.at[flip(mask)]
        remote(here, here, b_send.at[mask], b_recv.at[mask], across_cycle(mask)).wait_recv()

    placed = dot(arrange, part_got[...].reshape(ROWS, PAIR))
    for head in range(2):
        columns = slice(head * HEAD_SIZE, (head + 1) * HEAD_SIZE)
        entry = placed[:, columns]
        entry = entry * key_cos + pltpu.roll(entry, HEAD_SIZE // 2, 1) * key_sin
        own_ref[:, columns] = entry.astype(jnp.bfloat16)
    for half in range(2):
        rows = slice(half * BLOCK, (half + 1) * BLOCK)
        own_ref[rows, 256:] = placed[rows, 256:].T.astype(jnp.bfloat16)

    own_kv = pltpu.make_async_copy(own_ref, all_ref.at[place], local_sem.at[2])
    own_kv.start()

    def kv_copy(third, index):
        start, size, (b1, b2, b3) = THIRDS[third]
        mask, axis = ((0, b1), (0, b2), (0, b3), (b1, b2), (b1, b3), (b2, b3), (b1 ^ b2, b3))[index]
        rows = pl.ds(start, size)
        block = flip(mask)
        src = own_ref.at[rows] if mask == 0 else all_ref.at[block, rows]
        return remote(
            src, all_ref.at[block, rows], kv_send.at[third, index], kv_recv.at[third, index], across_cycle(axis)
        )

    def kv_landed(third, index):
        start, size, (b1, b2, b3) = THIRDS[third]
        mask = (b1, b2, b3, b1 ^ b2, b1 ^ b3, b2 ^ b3, 7)[index]
        here = all_ref.at[flip(mask), pl.ds(start, size)]
        remote(here, here, kv_send.at[third, index], kv_recv.at[third, index], across_cycle(4)).wait_recv()

    for index in range(3):
        for third in range(3):
            start(kv_copy(third, index))

    send_queries(3)
    landed(q_got, q_send, q_recv, 0, other)
    for delta in range(1, 8):
        for source in range(2):
            landed(q_got, q_send, q_recv, delta, source)
    own_q.wait()

    def order_queries(sup):
        base = sup * SUPER
        pick = bf16(iota((SUPER, ROWS), 0) + base == rank_r)
        cos = cos_ref[base : base + SUPER, :]
        sin = sin_ref[base : base + SUPER, :]

        def one_part(part, carry):
            columns = pl.ds(pl.multiple_of(part * 256, 256), 256)
            rows = dot(pick, q_got[:, :, :, columns].reshape(ROWS, 256))
            for one in range(2):
                entry = rows[:, one * HEAD_SIZE : (one + 1) * HEAD_SIZE]
                entry = entry * cos + pltpu.roll(entry, HEAD_SIZE // 2, 1) * sin
                entry = entry.astype(jnp.bfloat16)
                first = pl.multiple_of((part % 4 * 2 + one) * TILE, TILE)
                for tile in range(SUPER // TILE):
                    sorted_ref[part // 4, sup * (SUPER // TILE) + tile, pl.ds(first, TILE), :] = entry[
                        tile * TILE : (tile + 1) * TILE
                    ]
            return carry

        lax.fori_loop(0, 8, one_part, 0)
        turned_copy(sup).start()

    def turned_copy(sup):
        tiles = pl.ds(sup * (SUPER // TILE), SUPER // TILE)
        return pltpu.make_async_copy(sorted_ref.at[:, tiles], turned_ref.at[:, tiles], out_sem.at[sup])

    for third in range(3):
        kv_landed(third, 0)
        start(kv_copy(third, 3))
        start(kv_copy(third, 4))
    for third in range(3):
        kv_landed(third, 1)
        start(kv_copy(third, 5))
    order_queries(0)
    for third in range(3):
        kv_landed(third, 3)
        start(kv_copy(third, 6))
    for sup in range(1, 4):
        order_queries(sup)
    for index in (2, 4, 5, 6):
        for third in range(3):
            kv_landed(third, index)
    own_kv.wait()
    for sup in range(4):
        turned_copy(sup).wait()
    for copy in copies:
        copy.wait_send()


def across_cycle(mask):
    x, y, z, core = coords()
    return device(x + 2 * (mask // 4), y + 2 * (mask // 2 % 2), z + 2 * (mask % 2), core)


def exchange(queries, keys, values, plan_row, lengths):
    vmem = pl.BlockSpec(memory_space=pltpu.VMEM)
    dma = pltpu.SemaphoreType.DMA
    return pl.pallas_call(
        exchange_kernel,
        out_shape=(
            jax.ShapeDtypeStruct((2, ROWS // TILE, TILE * 8, HEAD_SIZE), jnp.bfloat16),
            jax.ShapeDtypeStruct((8, KEYS, 512), jnp.bfloat16),
            jax.ShapeDtypeStruct((ROWS // TILE, TILE * 8), jnp.int32),
            jax.ShapeDtypeStruct((ROWS // TILE, TILE * 8), jnp.int32),
            jax.ShapeDtypeStruct((8, 128), jnp.int32),
            jax.ShapeDtypeStruct((ROWS, 128), jnp.int32),
        ),
        in_specs=[vmem] * 5,
        out_specs=[pl.BlockSpec(memory_space=pl.ANY)] * 2 + [vmem] * 4,
        scratch_shapes=[
            pltpu.VMEM((8, SLOT, 2 * HALF), jnp.bfloat16),
            pltpu.VMEM((8, 2, SLOT, HALF), jnp.bfloat16),
            pltpu.VMEM((8, SLOT, 2 * PAIR), jnp.bfloat16),
            pltpu.VMEM((8, 2, SLOT, PAIR), jnp.bfloat16),
            pltpu.VMEM((8, PART, PAIR), jnp.bfloat16),
            pltpu.VMEM((8, PART, PAIR), jnp.bfloat16),
            pltpu.VMEM((8, SLOT, 128), jnp.bfloat16),
            pltpu.VMEM((8, 2, SLOT, 128), jnp.bfloat16),
            pltpu.VMEM((8, PART, 128), jnp.bfloat16),
            pltpu.VMEM((8, PART, 128), jnp.bfloat16),
            pltpu.VMEM((KEYS, 512), jnp.bfloat16),
            pltpu.VMEM((8, 128), jnp.int32),
            pltpu.VMEM((8, 128), jnp.int32),
            pltpu.VMEM((ROWS, 128), jnp.int32),
            pltpu.VMEM((ROWS, HEAD_SIZE), jnp.float32),
            pltpu.VMEM((ROWS, HEAD_SIZE), jnp.float32),
            pltpu.VMEM((2, ROWS // TILE, TILE * 8, HEAD_SIZE), jnp.bfloat16),
            dma((16,)), dma((8, 2)), dma((16,)), dma((8, 2)), dma((8,)), dma((8,)), dma((3, 7)), dma((3, 7)),
            dma(()), dma(()), dma((3,)), dma((4,)), dma((16,)), dma((8, 2)), dma((8,)), dma((8,)),
        ],
        compiler_params=pltpu.CompilerParams(
            collective_id=0, has_side_effects=True, vmem_limit_bytes=VMEM_LIMIT
        ),
        name="exchange",
    )(queries, keys, values, plan_row, lengths)


def back_kernel(made_ref, rank_ref, ret_ref, send_ref, send, recv, local_sem):
    x, y, z, core = coords()
    mine = sign_of(core)
    other = 1 - core
    for delta in range(1, 8):
        for worker in range(2):
            signal(moved(mine, delta, worker))
    signal(moved(0, 0, other))

    columns = pl.ds(pl.multiple_of(core * HALF, 128), HALF)

    def place_rows(first):
        rows = slice(first * 2 * SLOT, first * 2 * SLOT + 4 * SLOT)
        put = bf16(rank_ref[rows, 0:1] == iota((4 * SLOT, ROWS), 1))

        def one_part(part, carry):
            here = pl.ds(pl.multiple_of(part * 512, 512), 512)
            chosen = dot(put, made_ref[:, here]).astype(jnp.bfloat16)
            for one in range(4):
                send_ref[first + one // 2, one % 2, :, here] = chosen[one * SLOT : (one + 1) * SLOT, :]
            return carry

        lax.fori_loop(0, 4, one_part, 0)

    copies = []

    def back_copy(delta, source, first, size):
        rows = pl.ds(first, size)
        return remote(
            send_ref.at[delta, source, rows],
            ret_ref.at[delta, rows, columns],
            send.at[delta * 2 + source],
            recv.at[delta, core],
            moved(-sign_of(source), delta, source),
        )

    place_rows(6)
    pl.semaphore_wait(pltpu.get_barrier_semaphore(), 15)
    for first in (6, 4, 2, 0):
        if first < 6:
            place_rows(first)
        deltas = [delta for delta in (first + 1, first) if delta]
        for chunk in range(SLOT // 16):
            for delta in deltas:
                for source in range(2):
                    back_copy(delta, source, chunk * 16, 16).start()
        for delta in deltas:
            for source in range(2):
                copies.append(back_copy(delta, source, 0, SLOT))
    own = pltpu.make_async_copy(send_ref.at[0, core], ret_ref.at[0, :, columns], local_sem)
    own.start()
    copy = remote(
        send_ref.at[0, other], ret_ref.at[0, :, columns], send.at[0], recv.at[0, core], moved(0, 0, other)
    )
    copy.start()
    copies.append(copy)

    def landed(delta, worker):
        here = ret_ref.at[delta, :, pl.ds(pl.multiple_of(worker * HALF, 128), HALF)]
        remote(here, here, send.at[0], recv.at[delta, worker], moved(0, 0, other)).wait_recv()

    own.wait()
    landed(0, other)
    for delta in range(1, 8):
        for worker in range(2):
            landed(delta, worker)

    for copy in copies:
        copy.wait_send()


def back(made, rank):
    vmem = pl.BlockSpec(memory_space=pltpu.VMEM)
    return pl.pallas_call(
        back_kernel,
        out_shape=jax.ShapeDtypeStruct((8, SLOT, 2 * HALF), jnp.bfloat16),
        in_specs=[vmem] * 2,
        out_specs=pl.BlockSpec(memory_space=pl.ANY),
        scratch_shapes=[
            pltpu.VMEM((8, 2, SLOT, HALF), jnp.bfloat16),
            pltpu.SemaphoreType.DMA((16,)),
            pltpu.SemaphoreType.DMA((8, 2)),
            pltpu.SemaphoreType.DMA(()),
        ],
        compiler_params=pltpu.CompilerParams(
            collective_id=1, has_side_effects=True, vmem_limit_bytes=VMEM_LIMIT
        ),
        name="back",
    )(made, rank)


def restore_kernel(cycle_ref, plan_row, ret_ref, out_ref, choose_ref):
    @pl.when(pl.program_id(0) == 0)
    def _():
        plan_r = plan_row[...]
        plan_c = column_of(plan_r)
        same = (cycle_of(plan_c) == cycle_of(plan_r)) & (iota((TOK, TOK), 1) < iota((TOK, TOK), 0))
        rank = jnp.sum(jnp.where(same, 1, 0), 1, keepdims=True)
        row = jnp.bitwise_xor(cycle_of(plan_c), cycle_ref[0]) * SLOT + rank
        choose_ref[...] = bf16(iota((TOK, 8 * SLOT), 1) == row)

    rows = ret_ref[...].reshape(8 * SLOT, ret_ref.shape[2])
    out_ref[...] = dot(choose_ref[...], rows).astype(jnp.bfloat16)


def restore(my_cycle, plan_row, ret):
    width = 2048
    return pl.pallas_call(
        restore_kernel,
        grid=(2 * HALF // width,),
        out_shape=jax.ShapeDtypeStruct((TOK, 2 * HALF), jnp.bfloat16),
        in_specs=[
            pl.BlockSpec(memory_space=pltpu.SMEM),
            pl.BlockSpec((1, TOK), lambda i: (0, 0)),
            pl.BlockSpec((8, SLOT, width), lambda i: (0, 0, i)),
        ],
        out_specs=pl.BlockSpec((TOK, width), lambda i: (0, i)),
        scratch_shapes=[pltpu.VMEM((TOK, 8 * SLOT), jnp.bfloat16)],
        compiler_params=pltpu.CompilerParams(vmem_limit_bytes=VMEM_LIMIT),
        name="restore",
    )(my_cycle, plan_row, ret)


def attend_kernel(
    bounds_ref, last_ref, begin_ref, turned_ref, all_ref,
    made_ref, turned, kv_ref, made, peak, total, summed, decays, scores0, scores1, weights0, weights1, items, in_sem, out_sem,
):
    across = iota((BLOCK, TILE * 8), 0)
    tiles = ROWS // TILE
    loads = (
        pltpu.make_async_copy(turned_ref, turned, in_sem.at[0]),
        pltpu.make_async_copy(all_ref, kv_ref, in_sem.at[1]),
    )
    for load in loads:
        load.start()

    def store(tile):
        rows = pl.ds(pl.multiple_of(tile * TILE, TILE), TILE)
        return pltpu.make_async_copy(made.at[rows], made_ref.at[rows], out_sem)

    def list_tile(tile, count):
        low = bounds_ref[0, tile]
        high = bounds_ref[1, tile]

        def list_block(block, count):
            items[0, count] = tile
            items[1, count] = block
            items[2, count] = (block == low).astype(jnp.int32)
            items[3, count] = (block == high).astype(jnp.int32)
            return count + 1

        @pl.when(high < low)
        def _():
            made[pl.ds(pl.multiple_of(tile * TILE, TILE), TILE), :] = jnp.zeros((TILE, HALF), jnp.bfloat16)
            store(tile).start()

        return lax.fori_loop(low, high + 1, list_block, count)

    count = lax.fori_loop(0, tiles, list_tile, 0)
    for extra in range(3):
        items[0, count + extra] = items[0, count - 1]
        items[1, count + extra] = 32
        items[2, count + extra] = 0
        items[3, count + extra] = 0

    peak[...] = jnp.full_like(peak, NEG)
    summed[...] = jnp.zeros_like(summed)
    total[...] = jnp.zeros_like(total)
    decays[...] = jnp.ones_like(decays)
    weights1[...] = jnp.zeros_like(weights1)
    for load in loads:
        load.wait()

    def spot(block):
        block = jnp.minimum(block, 15)
        return jnp.where(block < 8, block, 15 - block), jnp.where(block < 8, 0, BLOCK)

    def score_of(item, scores):
        tile, block = items[0, item], items[1, item]
        begin = begin_ref[pl.ds(tile, 1), :]
        span = jnp.maximum(last_ref[pl.ds(tile, 1), :] - begin + 1, 0).astype(jnp.uint32)
        holder, row = spot(block)
        allowed = (across + (block * BLOCK - begin)).astype(jnp.uint32) < span
        for head in range(2):
            key = kv_ref[
                holder,
                pl.ds(pl.multiple_of(row, BLOCK), BLOCK),
                head * HEAD_SIZE : (head + 1) * HEAD_SIZE,
            ]
            score = lax.dot_general(
                key, turned[head, tile], (((1,), (1,)), ((), ())), preferred_element_type=jnp.float32
            )
            scores[head] = jnp.where(allowed, score, NEG)

    def weigh(item, scores, weights):
        opens = items[2, item] == 1
        for head in range(2):
            score = scores[head]
            old = jnp.where(opens, NEG, peak[head])
            new = jnp.maximum(old, jnp.max(score, 0, keepdims=True))
            decay = jnp.where(opens, 0.0, jnp.exp2(old - new))
            peak[head] = new
            weight = jnp.exp2(score - new)
            summed[head] = summed[head] * decay + jnp.sum(weight, 0, keepdims=True)
            weights[head] = weight.astype(jnp.bfloat16)
            decays[head] = decay

    def add(item, weights):
        holder, row = spot(items[1, item])
        for head in range(2):
            value = kv_ref[
                holder,
                pl.ds(pl.multiple_of(row + head * HEAD_SIZE, HEAD_SIZE), HEAD_SIZE),
                2 * HEAD_SIZE :,
            ]
            total[head] = total[head] * decays[head] + jnp.dot(
                value, weights[head], preferred_element_type=jnp.float32
            )

    score_of(0, scores0)

    def two_steps(pair, carry):
        item = pair * 2
        add(jnp.maximum(item - 1, 0), weights1)
        score_of(item + 1, scores1)
        keep = summed[...]
        weigh(item, scores0, weights0)
        close_after(item - 1, keep)
        add(item, weights0)
        score_of(item + 2, scores0)
        keep = summed[...]
        weigh(item + 1, scores1, weights1)
        close_after(item, keep)
        return carry

    def close_after(item, sums):
        at = jnp.maximum(item, 0)

        @pl.when((items[3, at] == 1) & (item >= 0))
        def _():
            there = pl.multiple_of(items[0, at] * TILE, TILE)
            for head in range(2):
                result = (total[head] / jnp.maximum(sums[head], 1e-30)).T.astype(jnp.bfloat16)
                for one in range(8):
                    made[pl.ds(there, TILE), pl.ds((head * 8 + one) * HEAD_SIZE, HEAD_SIZE)] = result[
                        one * TILE : (one + 1) * TILE
                    ]
            store(items[0, at]).start()

    lax.fori_loop(0, (count + 2) // 2, two_steps, 0)
    pltpu.make_async_copy(made, made_ref, out_sem).wait()


def attend(bounds, last, begin, q, kv):
    smem = pl.BlockSpec(memory_space=pltpu.SMEM)
    vmem = pl.BlockSpec(memory_space=pltpu.VMEM)
    hbm = pl.BlockSpec(memory_space=pl.ANY)
    lanes = TILE * 8
    return pl.pallas_call(
        attend_kernel,
        out_shape=jax.ShapeDtypeStruct((ROWS, HALF), jnp.bfloat16),
        in_specs=[smem, vmem, vmem, hbm, hbm],
        out_specs=hbm,
        scratch_shapes=[
            pltpu.VMEM((2, ROWS // TILE, lanes, HEAD_SIZE), jnp.bfloat16),
            pltpu.VMEM((8, KEYS, 512), jnp.bfloat16),
            pltpu.VMEM((ROWS, HALF), jnp.bfloat16),
            pltpu.VMEM((2, 1, lanes), jnp.float32),
            pltpu.VMEM((2, HEAD_SIZE, lanes), jnp.float32),
            pltpu.VMEM((2, 1, lanes), jnp.float32),
            pltpu.VMEM((2, 1, lanes), jnp.float32),
            pltpu.VMEM((2, BLOCK, lanes), jnp.float32),
            pltpu.VMEM((2, BLOCK, lanes), jnp.float32),
            pltpu.VMEM((2, BLOCK, lanes), jnp.bfloat16),
            pltpu.VMEM((2, BLOCK, lanes), jnp.bfloat16),
            pltpu.SMEM((4, ROWS // TILE * 16 + 4), jnp.int32),
            pltpu.SemaphoreType.DMA((2,)),
            pltpu.SemaphoreType.DMA(()),
        ],
        compiler_params=pltpu.CompilerParams(vmem_limit_bytes=VMEM_LIMIT),
        name="attend",
    )(bounds, last, begin, q, kv)


def local(queries, keys, values, plan, doc_lengths):
    x, y, z, _ = coords()
    my_cycle = x % 2 * 4 + y % 2 * 2 + z % 2
    plan_row = plan[None, :]
    q, kv, last, begin, bounds, rank = exchange(queries, keys, values, plan_row, doc_lengths)
    made = attend(bounds, last, begin, q, kv)
    ret = back(made, rank)
    return restore(jnp.reshape(my_cycle, (1,)).astype(jnp.int32), plan_row, ret)


def solution(mesh):
    return jax.shard_map(
        local,
        mesh=mesh,
        in_specs=(
            P(("blk", "group"), None),
            P(("blk", "group"), None),
            P(("blk", "group"), None),
            P(("blk", "group")),
            P("group", None),
        ),
        out_specs=P(("blk", "group"), None),
        check_vma=False,
    )
```

```python
import math

import jax
import jax.numpy as jnp
from jax import lax
from jax.experimental import pallas as pl
from jax.experimental.pallas import tpu as pltpu
from jax.sharding import PartitionSpec as P

QUERY_HEADS = 32
KEY_VALUE_HEADS = 4
HEAD_SIZE = 128
THETA = 500000.0

TOK = 256
SLOT = 64
KEYS = 512
BLOCK = 256
TILE = 64
TILE_BITS = 6
SUPER = 256
HALF = QUERY_HEADS // 2 * HEAD_SIZE
WIDE = HALF + 128
ROWS = 16 * SLOT
NEG = -1e30
SCALE = math.log2(math.e) / math.sqrt(HEAD_SIZE)
MESH = pl.DeviceIdType.MESH
VMEM_LIMIT = 60 * 1024 * 1024


def coords():
    b = lax.axis_index("blk")
    g = lax.axis_index("group")
    return b // 4, g % 4, (b // 2) % 2 * 2 + g // 4, b % 2


def device(x, y, z, core):
    x, y, z = lax.rem(x + 4, 4), lax.rem(y + 4, 4), lax.rem(z + 4, 4)
    return x * 4 + z // 2 * 2 + core, lax.rem(z, 2) * 4 + y


def moved(sign, delta, core):
    x, y, z, _ = coords()
    return device(x + sign * (delta // 4), y + sign * (delta // 2 % 2), z + sign * (delta % 2), core)


def sign_of(core):
    return 1 - 2 * core


def signal(target):
    pl.semaphore_signal(pltpu.get_barrier_semaphore(), inc=1, device_id=target, device_id_type=MESH)


def remote(src, dst, send, recv, target):
    return pltpu.make_async_remote_copy(
        src_ref=src, dst_ref=dst, send_sem=send, recv_sem=recv, device_id=target, device_id_type=MESH
    )


THIRDS = ((0, 176, (4, 2, 1)), (176, 176, (2, 1, 4)), (352, 160, (1, 4, 2)))
PAIR = 512
PART = 128


def iota(shape, axis):
    return lax.broadcasted_iota(jnp.int32, shape, axis)


def bf16(flags):
    return jnp.where(flags, 1.0, 0.0).astype(jnp.bfloat16)


def dot(a, b):
    return jnp.dot(a, b, preferred_element_type=jnp.float32)


def cycle_of(plan):
    return (plan >> 8) & 7


def cycle_index(plan):
    p = plan >> 11
    offset = plan & 255
    return jnp.where(offset < 128, p * 128 + offset, (31 - p) * 128 + offset - 128)


def column_of(row):
    size = row.shape[1]
    return jnp.sum(jnp.where(iota((size, size), 0) == iota((size, size), 1), row, 0), 1, keepdims=True)


def document_start(u, lengths):
    end = jnp.zeros((1, 1), jnp.int32)
    start = jnp.zeros_like(u)
    for one in range(4):
        length = lengths[0:1, one : one + 1]
        end = end + length
        start = start + jnp.where(u >= end, length, 0)
    return start


def turning(position):
    half = HEAD_SIZE // 2
    lane = iota((1, HEAD_SIZE), 1)
    spot = (lane & (half - 1)).astype(jnp.float32)
    inv_freq = jnp.exp(-math.log(THETA) * (2.0 * spot / HEAD_SIZE))
    angle = position.astype(jnp.float32) * inv_freq
    both = jnp.cos(jnp.where(lane < half, angle, angle - math.pi / 2))
    other = pltpu.roll(both, half, 1)
    first = jnp.broadcast_to(lane < half, both.shape)
    return jnp.where(first, both, other), jnp.where(first, -other, both)


def exchange_kernel(
    queries_ref, keys_ref, values_ref, plan_row, lengths_ref,
    turned_ref, all_ref, last_ref, begin_ref, bounds_ref, rank_ref,
    q_out, q_got, kv_out, kv_got, part_out, part_got, f_out, f_got, g_out, g_got, own_ref, len_out, len_got, key_ref, cos_ref, sin_ref, sorted_ref,
    q_send, q_recv, a_send, a_recv, b_send, b_recv, kv_send, kv_recv, len_send, len_recv, local_sem, out_sem,
    f_send, f_recv, g_send, g_recv,
):
    x, y, z, core = coords()
    place = x // 2 * 4 + y // 2 * 2 + z // 2
    my_cycle = x % 2 * 4 + y % 2 * 2 + z % 2
    mine = sign_of(core)
    other = 1 - core

    block_at, group_at = lax.axis_index("blk"), lax.axis_index("group")
    spot = block_at // 2
    to_device = device(
        spot // 4 * 2 + group_at // 4, spot // 2 % 2 * 2 + group_at // 2 % 2, spot % 2 * 2 + group_at % 2, block_at % 2
    )
    from_block = place * 2 + core
    at_home = (from_block == block_at) & (my_cycle == group_at)

    for delta in range(1, 8):
        for source in range(2):
            signal(moved(-sign_of(source), delta, source))
    signal(moved(0, 0, other))
    for mask in range(1, 8):
        signal(across_cycle(mask))

    @pl.when(jnp.logical_not(at_home))
    def _():
        signal((from_block, my_cycle))

    len_out[...] = jnp.zeros_like(len_out)
    len_out[0:1, 0:4] = lengths_ref[...]
    plan_r = plan_row[...]
    plan_c = column_of(plan_r)
    same = (cycle_of(plan_c) == cycle_of(plan_r)) & (iota((TOK, TOK), 0) < iota((TOK, TOK), 1))
    rank = jnp.sum(jnp.where(same, 1, 0), 0, keepdims=True)
    row = jnp.bitwise_xor(cycle_of(plan_r), my_cycle) * SLOT + rank
    choose = bf16(iota((8 * SLOT, TOK), 0) == row)
    u = cycle_index(plan_c)
    lane = iota((TOK, 128), 1)
    fields = jnp.where(lane == 0, (u >> 8) + 1, jnp.where(lane == 1, u & 255, 0))
    fields = fields.astype(jnp.float32).astype(jnp.bfloat16)
    f_out[...] = dot(choose, fields).astype(jnp.bfloat16).reshape(8, SLOT, 128)

    pl.semaphore_wait(pltpu.get_barrier_semaphore(), jnp.where(at_home, 22, 23))

    copies = []

    def start(copy):
        copy.start()
        copies.append(copy)

    def lengths_copy():
        return remote(len_out, len_got, len_send, len_recv, to_device)

    @pl.when(jnp.logical_not(at_home))
    def _():
        lengths_copy().start()

    def out_copy(src, dst, send, recv, width, delta, to_core):
        columns = pl.ds(pl.multiple_of(to_core * width, 128), width)
        slot = delta * 2 + to_core if delta else 0
        return remote(
            src.at[delta, :, columns],
            dst.at[delta, core],
            send.at[slot],
            recv.at[delta, core],
            moved(mine, delta, to_core) if delta else moved(0, 0, other),
        )

    def landed(dst, send, recv, delta, source):
        here = dst.at[delta, source]
        remote(here, here, send.at[0], recv.at[delta, source], moved(0, 0, other)).wait_recv()

    order = (7, 6, 5, 3, 4, 2, 1)

    def f_copy(delta, to_core):
        return remote(
            f_out.at[delta],
            f_got.at[delta, core],
            f_send.at[delta * 2 + to_core if delta else 0],
            f_recv.at[delta, core],
            moved(mine, delta, to_core),
        )

    start(f_copy(0, other))
    for delta in order:
        for to_core in range(2):
            start(f_copy(delta, to_core))
    f_got[0, core] = f_out[0]

    chosen_k = dot(choose, keys_ref[...]).astype(jnp.bfloat16)
    chosen_v = dot(choose, values_ref[...]).astype(jnp.bfloat16)
    for delta in range(8):
        rows = slice(delta * SLOT, (delta + 1) * SLOT)
        for half in range(2):
            kv_out[delta, :, half * PAIR : half * PAIR + 256] = chosen_k[rows, half * 256 : half * 256 + 256]
            kv_out[delta, :, half * PAIR + 256 : half * PAIR + 512] = chosen_v[rows, half * 256 : half * 256 + 256]
    start(out_copy(kv_out, kv_got, a_send, a_recv, PAIR, 0, other))
    for delta in order:
        for to_core in range(2):
            start(out_copy(kv_out, kv_got, a_send, a_recv, PAIR, delta, to_core))
    own_a = pltpu.make_async_copy(
        kv_out.at[0, :, pl.ds(pl.multiple_of(core * PAIR, 128), PAIR)], kv_got.at[0, core], local_sem.at[0]
    )
    own_a.start()

    for part in range(8):
        columns = slice(part * 512, part * 512 + 512)
        chosen = dot(choose, queries_ref[:, columns]).astype(jnp.bfloat16)
        for delta in range(8):
            q_out[delta, :, columns] = chosen[delta * SLOT : (delta + 1) * SLOT, :]
    start(out_copy(q_out, q_got, q_send, q_recv, HALF, 0, other))
    def send_queries(chunk):
        for delta in order:
            for to_core in range(2):
                columns = pl.ds(to_core * HALF, HALF)
                rows = pl.ds(chunk * 16, 16)
                remote(
                    q_out.at[delta, rows, columns],
                    q_got.at[delta, core, rows],
                    q_send.at[delta * 2 + to_core],
                    q_recv.at[delta, core],
                    moved(mine, delta, to_core),
                ).start()

    send_queries(0)
    for delta in order:
        for to_core in range(2):
            copies.append(out_copy(q_out, q_got, q_send, q_recv, HALF, delta, to_core))
    own_q = pltpu.make_async_copy(
        q_out.at[0, :, pl.ds(pl.multiple_of(core * HALF, 128), HALF)], q_got.at[0, core], local_sem.at[1]
    )
    own_q.start()

    landed(f_got, f_send, f_recv, 0, other)
    for delta in range(1, 8):
        for source in range(2):
            landed(f_got, f_send, f_recv, delta, source)

    def fields_of(table):
        fields = table.reshape(ROWS, 128).astype(jnp.float32)
        flat = fields.T
        out = []
        for lead, low in ((fields[:, 0:1], fields[:, 1:2]), (flat[0:1, :], flat[1:2, :])):
            lead = lead.astype(jnp.int32)
            out.append((lead > 0, (lead - 1) * 256 + low.astype(jnp.int32)))
        return out

    def holder_of(u):
        block = u >> 8
        return jnp.where(block < 8, block, 15 - block)

    (valid_c, u_c), (valid_r, u_r) = fields_of(f_got[...])
    key_c = jnp.where(valid_c, holder_of(u_c), -1)
    key_r = jnp.where(valid_r, holder_of(u_r), -2)
    key_ref[...] = jnp.broadcast_to(key_c, (ROWS, 128))

    def count_before(step, total):
        base = pl.multiple_of(step * 128, 128)
        chunk = key_ref[pl.ds(base, 128), 0:1]
        hits = (chunk == key_r) & (iota((128, ROWS), 0) + base < iota((128, ROWS), 1))
        return total + jnp.sum(jnp.where(hits, 1, 0), 0, keepdims=True)

    before = lax.fori_loop(0, ROWS // 128, count_before, jnp.zeros((1, ROWS), jnp.int32))
    target = jnp.where(valid_r, key_r * PART + before, -1)

    def flip(mask):
        out = 0
        for bit in (4, 2, 1):
            digit = place // bit % 2
            out = out + bit * ((1 - digit) if mask & bit else digit)
        return out

    def place_fields(step, carry):
        base = pl.multiple_of(step * 4 * PART, 4 * PART)
        rows = dot(bf16(iota((4 * PART, ROWS), 0) + base == target), f_got[...].reshape(ROWS, 128))
        g_out[pl.ds(step * 4, 4)] = rows.astype(jnp.bfloat16).reshape(4, PART, 128)
        return carry

    lax.fori_loop(0, 2, place_fields, 0)
    for mask in order:
        start(remote(g_out.at[flip(mask)], g_got.at[place], g_send.at[mask], g_recv.at[mask], across_cycle(mask)))
    send_queries(1)
    g_got[place] = g_out[place]

    own_a.wait()
    landed(kv_got, a_send, a_recv, 0, other)
    for delta in range(1, 8):
        for source in range(2):
            landed(kv_got, a_send, a_recv, delta, source)

    def fill(step, carry):
        base = pl.multiple_of(step * 4 * PART, 4 * PART)
        rows = dot(bf16(iota((4 * PART, ROWS), 0) + base == target), kv_got[...].reshape(ROWS, PAIR))
        part_out[pl.ds(step * 4, 4)] = rows.astype(jnp.bfloat16).reshape(4, PART, PAIR)
        return carry

    lax.fori_loop(0, 2, fill, 0)

    for mask in order:
        start(
            remote(
                part_out.at[flip(mask)], part_got.at[place], b_send.at[mask], b_recv.at[mask], across_cycle(mask)
            )
        )
    send_queries(2)
    part_got[place] = part_out[place]

    index_c, index_r = iota((ROWS, 1), 0), iota((1, ROWS), 1)
    key_c = jnp.where(valid_c, u_c, 4096 + index_c)
    key_r = jnp.where(valid_r, u_r, 4096 + index_r)
    key_ref[...] = jnp.broadcast_to(key_c, (ROWS, 128))

    def rank_step(step, total):
        base = pl.multiple_of(step * 128, 128)
        chunk = key_ref[pl.ds(base, 128), 0:1]
        counts = jnp.sum(jnp.where(key_r < chunk, 1, 0), 1, keepdims=True)
        rank_ref[pl.ds(base, 128), :] = jnp.broadcast_to(counts, (128, 128))
        return total + jnp.sum(jnp.where(chunk < key_r, 1, 0), 0, keepdims=True)

    rank_r = lax.fori_loop(0, ROWS // 128, rank_step, jnp.zeros((1, ROWS), jnp.int32))

    def sort_step(step, total):
        base = pl.multiple_of(step * 128, 128)
        chunk = key_ref[pl.ds(base, 128), 0:1]
        ranks = rank_ref[pl.ds(base, 128), 0:1]
        return total + jnp.sum(jnp.where(ranks == iota((128, ROWS), 1), chunk, 0), 0, keepdims=True)

    sorted_r = lax.fori_loop(0, ROWS // 128, sort_step, jnp.zeros((1, ROWS), jnp.int32))

    @pl.when(at_home)
    def _():
        len_got[...] = len_out[...]

    @pl.when(jnp.logical_not(at_home))
    def _():
        lengths_copy().wait()

    lengths = len_got[...]
    begin_r = jnp.where(sorted_r < 4096, document_start(sorted_r, lengths), 8192)

    own_tile = iota((ROWS // TILE, ROWS), 1) >> TILE_BITS == iota((ROWS // TILE, ROWS), 0)
    spread = bf16(iota((ROWS, TILE * 8), 0) & (TILE - 1) == iota((ROWS, TILE * 8), 1) & (TILE - 1))
    for values, tiles_ref in ((sorted_r, last_ref), (begin_r, begin_ref)):
        parts = [
            dot(jnp.where(own_tile, half, 0).astype(jnp.float32).astype(jnp.bfloat16), spread).astype(jnp.int32)
            for half in (values >> 8, values & 255)
        ]
        tiles_ref[...] = parts[0] * 256 + parts[1]

    def turn_step(step, carry):
        low, high = carry
        base = pl.multiple_of(step * 128, 128)
        hits = iota((128, ROWS), 0) + base == rank_r
        u = jnp.sum(jnp.where(hits, key_r, 0), 1, keepdims=True)
        live = u < 4096
        start = document_start(u, lengths)
        index, tile = iota((128, 128), 0) + base, iota((128, 128), 1)
        low = low + jnp.sum(jnp.where((index == tile * TILE) & live, start >> 8, 0), 0, keepdims=True)
        high = jnp.maximum(
            high, jnp.max(jnp.where((index >> TILE_BITS == tile) & live, u >> 8, -1), 0, keepdims=True)
        )
        cos, sin = turning(jnp.where(live, u - start, 0))
        cos_ref[pl.ds(base, 128), :] = cos * SCALE
        sin_ref[pl.ds(base, 128), :] = sin * SCALE
        return low, high

    low, high = lax.fori_loop(
        0, ROWS // 128, turn_step, (jnp.zeros((1, 128), jnp.int32), jnp.full((1, 128), -1, jnp.int32))
    )
    bounds_ref[...] = jnp.zeros_like(bounds_ref)
    bounds_ref[0:1, :] = low
    bounds_ref[1:2, :] = high
    rows_c = iota((KEYS, 1), 0)
    key_u = jnp.where(rows_c < BLOCK, place * BLOCK + rows_c, (15 - place) * BLOCK + rows_c - BLOCK)
    key_cos, key_sin = turning(key_u - document_start(key_u, lengths))

    for mask in range(1, 8):
        here = g_got.at[flip(mask)]
        remote(here, here, g_send.at[mask], g_recv.at[mask], across_cycle(mask)).wait_recv()
    _, (valid, u) = fields_of(g_got[...])
    target = jnp.where(valid, jnp.where(u >= 2048, BLOCK, 0) + (u & 255), -1)
    arrange = bf16(iota((KEYS, ROWS), 0) == target)

    for mask in range(1, 8):
        here = part_got.at[flip(mask)]
        remote(here, here, b_send.at[mask], b_recv.at[mask], across_cycle(mask)).wait_recv()

    placed = dot(arrange, part_got[...].reshape(ROWS, PAIR))
    for head in range(2):
        columns = slice(head * HEAD_SIZE, (head + 1) * HEAD_SIZE)
        entry = placed[:, columns]
        entry = entry * key_cos + pltpu.roll(entry, HEAD_SIZE // 2, 1) * key_sin
        own_ref[:, columns] = entry.astype(jnp.bfloat16)
    for half in range(2):
        rows = slice(half * BLOCK, (half + 1) * BLOCK)
        own_ref[rows, 256:] = placed[rows, 256:].T.astype(jnp.bfloat16)

    own_kv = pltpu.make_async_copy(own_ref, all_ref.at[place], local_sem.at[2])
    own_kv.start()

    def kv_copy(third, index):
        start, size, (b1, b2, b3) = THIRDS[third]
        mask, axis = ((0, b1), (0, b2), (0, b3), (b1, b2), (b1, b3), (b2, b3), (b1 ^ b2, b3))[index]
        rows = pl.ds(start, size)
        block = flip(mask)
        src = own_ref.at[rows] if mask == 0 else all_ref.at[block, rows]
        return remote(
            src, all_ref.at[block, rows], kv_send.at[third, index], kv_recv.at[third, index], across_cycle(axis)
        )

    def kv_landed(third, index):
        start, size, (b1, b2, b3) = THIRDS[third]
        mask = (b1, b2, b3, b1 ^ b2, b1 ^ b3, b2 ^ b3, 7)[index]
        here = all_ref.at[flip(mask), pl.ds(start, size)]
        remote(here, here, kv_send.at[third, index], kv_recv.at[third, index], across_cycle(4)).wait_recv()

    for index in range(3):
        for third in range(3):
            start(kv_copy(third, index))

    send_queries(3)
    landed(q_got, q_send, q_recv, 0, other)
    for delta in range(1, 8):
        for source in range(2):
            landed(q_got, q_send, q_recv, delta, source)
    own_q.wait()

    def order_queries(sup):
        base = sup * SUPER
        pick = bf16(iota((SUPER, ROWS), 0) + base == rank_r)
        cos = cos_ref[base : base + SUPER, :]
        sin = sin_ref[base : base + SUPER, :]

        def one_part(part, carry):
            columns = pl.ds(pl.multiple_of(part * 256, 256), 256)
            rows = dot(pick, q_got[:, :, :, columns].reshape(ROWS, 256))
            for one in range(2):
                entry = rows[:, one * HEAD_SIZE : (one + 1) * HEAD_SIZE]
                entry = entry * cos + pltpu.roll(entry, HEAD_SIZE // 2, 1) * sin
                entry = entry.astype(jnp.bfloat16)
                first = pl.multiple_of((part % 4 * 2 + one) * TILE, TILE)
                for tile in range(SUPER // TILE):
                    sorted_ref[part // 4, sup * (SUPER // TILE) + tile, pl.ds(first, TILE), :] = entry[
                        tile * TILE : (tile + 1) * TILE
                    ]
            return carry

        lax.fori_loop(0, 8, one_part, 0)
        turned_copy(sup).start()

    def turned_copy(sup):
        tiles = pl.ds(sup * (SUPER // TILE), SUPER // TILE)
        return pltpu.make_async_copy(sorted_ref.at[:, tiles], turned_ref.at[:, tiles], out_sem.at[sup])

    for third in range(3):
        kv_landed(third, 0)
        start(kv_copy(third, 3))
        start(kv_copy(third, 4))
    for third in range(3):
        kv_landed(third, 1)
        start(kv_copy(third, 5))
    order_queries(0)
    for third in range(3):
        kv_landed(third, 3)
        start(kv_copy(third, 6))
    for sup in range(1, 4):
        order_queries(sup)
    for index in (2, 4, 5, 6):
        for third in range(3):
            kv_landed(third, index)
    own_kv.wait()
    for sup in range(4):
        turned_copy(sup).wait()
    for copy in copies:
        copy.wait_send()


def across_cycle(mask):
    x, y, z, core = coords()
    return device(x + 2 * (mask // 4), y + 2 * (mask // 2 % 2), z + 2 * (mask % 2), core)


def exchange(queries, keys, values, plan_row, lengths):
    vmem = pl.BlockSpec(memory_space=pltpu.VMEM)
    dma = pltpu.SemaphoreType.DMA
    return pl.pallas_call(
        exchange_kernel,
        out_shape=(
            jax.ShapeDtypeStruct((2, ROWS // TILE, TILE * 8, HEAD_SIZE), jnp.bfloat16),
            jax.ShapeDtypeStruct((8, KEYS, 512), jnp.bfloat16),
            jax.ShapeDtypeStruct((ROWS // TILE, TILE * 8), jnp.int32),
            jax.ShapeDtypeStruct((ROWS // TILE, TILE * 8), jnp.int32),
            jax.ShapeDtypeStruct((8, 128), jnp.int32),
            jax.ShapeDtypeStruct((ROWS, 128), jnp.int32),
        ),
        in_specs=[vmem] * 5,
        out_specs=[pl.BlockSpec(memory_space=pl.ANY)] * 2 + [vmem] * 4,
        scratch_shapes=[
            pltpu.VMEM((8, SLOT, 2 * HALF), jnp.bfloat16),
            pltpu.VMEM((8, 2, SLOT, HALF), jnp.bfloat16),
            pltpu.VMEM((8, SLOT, 2 * PAIR), jnp.bfloat16),
            pltpu.VMEM((8, 2, SLOT, PAIR), jnp.bfloat16),
            pltpu.VMEM((8, PART, PAIR), jnp.bfloat16),
            pltpu.VMEM((8, PART, PAIR), jnp.bfloat16),
            pltpu.VMEM((8, SLOT, 128), jnp.bfloat16),
            pltpu.VMEM((8, 2, SLOT, 128), jnp.bfloat16),
            pltpu.VMEM((8, PART, 128), jnp.bfloat16),
            pltpu.VMEM((8, PART, 128), jnp.bfloat16),
            pltpu.VMEM((KEYS, 512), jnp.bfloat16),
            pltpu.VMEM((8, 128), jnp.int32),
            pltpu.VMEM((8, 128), jnp.int32),
            pltpu.VMEM((ROWS, 128), jnp.int32),
            pltpu.VMEM((ROWS, HEAD_SIZE), jnp.float32),
            pltpu.VMEM((ROWS, HEAD_SIZE), jnp.float32),
            pltpu.VMEM((2, ROWS // TILE, TILE * 8, HEAD_SIZE), jnp.bfloat16),
            dma((16,)), dma((8, 2)), dma((16,)), dma((8, 2)), dma((8,)), dma((8,)), dma((3, 7)), dma((3, 7)),
            dma(()), dma(()), dma((3,)), dma((4,)), dma((16,)), dma((8, 2)), dma((8,)), dma((8,)),
        ],
        compiler_params=pltpu.CompilerParams(
            collective_id=0, has_side_effects=True, vmem_limit_bytes=VMEM_LIMIT
        ),
        name="exchange",
    )(queries, keys, values, plan_row, lengths)


def back_kernel(made_ref, rank_ref, ret_ref, send_ref, send, recv, local_sem):
    x, y, z, core = coords()
    mine = sign_of(core)
    other = 1 - core
    for delta in range(1, 8):
        for worker in range(2):
            signal(moved(mine, delta, worker))
    signal(moved(0, 0, other))

    columns = pl.ds(pl.multiple_of(core * HALF, 128), HALF)

    def place_rows(pair):
        ranks = [rank_ref[delta * 2 * SLOT : (delta + 1) * 2 * SLOT, 0:1] for delta in pair]
        put = bf16(jnp.concatenate(ranks, 0) == iota((4 * SLOT, ROWS), 1))

        def one_part(part, carry):
            here = pl.ds(pl.multiple_of(part * 512, 512), 512)
            chosen = dot(put, made_ref[:, here]).astype(jnp.bfloat16)
            for one in range(4):
                send_ref[pair[one // 2], one % 2, :, here] = chosen[one * SLOT : (one + 1) * SLOT, :]
            return carry

        lax.fori_loop(0, 4, one_part, 0)

    copies = []

    def back_copy(delta, source, first, size):
        rows = pl.ds(first, size)
        return remote(
            send_ref.at[delta, source, rows],
            ret_ref.at[delta, rows, columns],
            send.at[delta * 2 + source],
            recv.at[delta, core],
            moved(-sign_of(source), delta, source),
        )

    pairs = ((7, 0), (6, 1), (5, 2), (3, 4))
    place_rows(pairs[0])
    pl.semaphore_wait(pltpu.get_barrier_semaphore(), 15)
    for pair in pairs:
        if pair != pairs[0]:
            place_rows(pair)
        deltas = [delta for delta in pair if delta]
        for chunk in range(SLOT // 16):
            for delta in deltas:
                for source in range(2):
                    back_copy(delta, source, chunk * 16, 16).start()
        for delta in deltas:
            for source in range(2):
                copies.append(back_copy(delta, source, 0, SLOT))
    own = pltpu.make_async_copy(send_ref.at[0, core], ret_ref.at[0, :, columns], local_sem)
    own.start()
    copy = remote(
        send_ref.at[0, other], ret_ref.at[0, :, columns], send.at[0], recv.at[0, core], moved(0, 0, other)
    )
    copy.start()
    copies.append(copy)

    def landed(delta, worker):
        here = ret_ref.at[delta, :, pl.ds(pl.multiple_of(worker * HALF, 128), HALF)]
        remote(here, here, send.at[0], recv.at[delta, worker], moved(0, 0, other)).wait_recv()

    own.wait()
    landed(0, other)
    for delta in range(1, 8):
        for worker in range(2):
            landed(delta, worker)

    for copy in copies:
        copy.wait_send()


def back(made, rank):
    vmem = pl.BlockSpec(memory_space=pltpu.VMEM)
    return pl.pallas_call(
        back_kernel,
        out_shape=jax.ShapeDtypeStruct((8, SLOT, 2 * HALF), jnp.bfloat16),
        in_specs=[vmem] * 2,
        out_specs=pl.BlockSpec(memory_space=pl.ANY),
        scratch_shapes=[
            pltpu.VMEM((8, 2, SLOT, HALF), jnp.bfloat16),
            pltpu.SemaphoreType.DMA((16,)),
            pltpu.SemaphoreType.DMA((8, 2)),
            pltpu.SemaphoreType.DMA(()),
        ],
        compiler_params=pltpu.CompilerParams(
            collective_id=1, has_side_effects=True, vmem_limit_bytes=VMEM_LIMIT
        ),
        name="back",
    )(made, rank)


def restore_kernel(cycle_ref, plan_row, ret_ref, out_ref, choose_ref):
    @pl.when(pl.program_id(0) == 0)
    def _():
        plan_r = plan_row[...]
        plan_c = column_of(plan_r)
        same = (cycle_of(plan_c) == cycle_of(plan_r)) & (iota((TOK, TOK), 1) < iota((TOK, TOK), 0))
        rank = jnp.sum(jnp.where(same, 1, 0), 1, keepdims=True)
        row = jnp.bitwise_xor(cycle_of(plan_c), cycle_ref[0]) * SLOT + rank
        choose_ref[...] = bf16(iota((TOK, 8 * SLOT), 1) == row)

    rows = ret_ref[...].reshape(8 * SLOT, ret_ref.shape[2])
    out_ref[...] = dot(choose_ref[...], rows).astype(jnp.bfloat16)


def restore(my_cycle, plan_row, ret):
    width = 2048
    return pl.pallas_call(
        restore_kernel,
        grid=(2 * HALF // width,),
        out_shape=jax.ShapeDtypeStruct((TOK, 2 * HALF), jnp.bfloat16),
        in_specs=[
            pl.BlockSpec(memory_space=pltpu.SMEM),
            pl.BlockSpec((1, TOK), lambda i: (0, 0)),
            pl.BlockSpec((8, SLOT, width), lambda i: (0, 0, i)),
        ],
        out_specs=pl.BlockSpec((TOK, width), lambda i: (0, i)),
        scratch_shapes=[pltpu.VMEM((TOK, 8 * SLOT), jnp.bfloat16)],
        compiler_params=pltpu.CompilerParams(vmem_limit_bytes=VMEM_LIMIT),
        name="restore",
    )(my_cycle, plan_row, ret)


def attend_kernel(
    bounds_ref, last_ref, begin_ref, turned_ref, all_ref,
    made_ref, turned, kv_ref, made, peak, total, summed, decays, scores0, scores1, weights0, weights1, items, in_sem, out_sem,
):
    across = iota((BLOCK, TILE * 8), 0)
    tiles = ROWS // TILE
    loads = (
        pltpu.make_async_copy(turned_ref, turned, in_sem.at[0]),
        pltpu.make_async_copy(all_ref, kv_ref, in_sem.at[1]),
    )
    for load in loads:
        load.start()

    def store(tile):
        rows = pl.ds(pl.multiple_of(tile * TILE, TILE), TILE)
        return pltpu.make_async_copy(made.at[rows], made_ref.at[rows], out_sem)

    def list_tile(tile, count):
        low = bounds_ref[0, tile]
        high = bounds_ref[1, tile]

        def list_block(block, count):
            items[0, count] = tile
            items[1, count] = block
            items[2, count] = (block == low).astype(jnp.int32)
            items[3, count] = (block == high).astype(jnp.int32)
            return count + 1

        @pl.when(high < low)
        def _():
            made[pl.ds(pl.multiple_of(tile * TILE, TILE), TILE), :] = jnp.zeros((TILE, HALF), jnp.bfloat16)
            store(tile).start()

        return lax.fori_loop(low, high + 1, list_block, count)

    count = lax.fori_loop(0, tiles, list_tile, 0)
    for extra in range(3):
        items[0, count + extra] = items[0, count - 1]
        items[1, count + extra] = 32
        items[2, count + extra] = 0
        items[3, count + extra] = 0

    peak[...] = jnp.full_like(peak, NEG)
    summed[...] = jnp.zeros_like(summed)
    total[...] = jnp.zeros_like(total)
    decays[...] = jnp.ones_like(decays)
    weights1[...] = jnp.zeros_like(weights1)
    for load in loads:
        load.wait()

    def spot(block):
        block = jnp.minimum(block, 15)
        return jnp.where(block < 8, block, 15 - block), jnp.where(block < 8, 0, BLOCK)

    def score_of(item, scores):
        tile, block = items[0, item], items[1, item]
        begin = begin_ref[pl.ds(tile, 1), :]
        span = jnp.maximum(last_ref[pl.ds(tile, 1), :] - begin + 1, 0).astype(jnp.uint32)
        holder, row = spot(block)
        allowed = (across + (block * BLOCK - begin)).astype(jnp.uint32) < span
        for head in range(2):
            key = kv_ref[
                holder,
                pl.ds(pl.multiple_of(row, BLOCK), BLOCK),
                head * HEAD_SIZE : (head + 1) * HEAD_SIZE,
            ]
            score = lax.dot_general(
                key, turned[head, tile], (((1,), (1,)), ((), ())), preferred_element_type=jnp.float32
            )
            scores[head] = jnp.where(allowed, score, NEG)

    def weigh(item, scores, weights):
        opens = items[2, item] == 1
        for head in range(2):
            score = scores[head]
            old = jnp.where(opens, NEG, peak[head])
            new = jnp.maximum(old, jnp.max(score, 0, keepdims=True))
            decay = jnp.where(opens, 0.0, jnp.exp2(old - new))
            peak[head] = new
            weight = jnp.exp2(score - new)
            summed[head] = summed[head] * decay + jnp.sum(weight, 0, keepdims=True)
            weights[head] = weight.astype(jnp.bfloat16)
            decays[head] = decay

    def add(item, weights):
        holder, row = spot(items[1, item])
        for head in range(2):
            value = kv_ref[
                holder,
                pl.ds(pl.multiple_of(row + head * HEAD_SIZE, HEAD_SIZE), HEAD_SIZE),
                2 * HEAD_SIZE :,
            ]
            total[head] = total[head] * decays[head] + jnp.dot(
                value, weights[head], preferred_element_type=jnp.float32
            )

    score_of(0, scores0)

    def two_steps(pair, carry):
        item = pair * 2
        add(jnp.maximum(item - 1, 0), weights1)
        score_of(item + 1, scores1)
        keep = summed[...]
        weigh(item, scores0, weights0)
        close_after(item - 1, keep)
        add(item, weights0)
        score_of(item + 2, scores0)
        keep = summed[...]
        weigh(item + 1, scores1, weights1)
        close_after(item, keep)
        return carry

    def close_after(item, sums):
        at = jnp.maximum(item, 0)

        @pl.when((items[3, at] == 1) & (item >= 0))
        def _():
            there = pl.multiple_of(items[0, at] * TILE, TILE)
            for head in range(2):
                result = (total[head] / jnp.maximum(sums[head], 1e-30)).T.astype(jnp.bfloat16)
                for one in range(8):
                    made[pl.ds(there, TILE), pl.ds((head * 8 + one) * HEAD_SIZE, HEAD_SIZE)] = result[
                        one * TILE : (one + 1) * TILE
                    ]
            store(items[0, at]).start()

    lax.fori_loop(0, (count + 2) // 2, two_steps, 0)
    pltpu.make_async_copy(made, made_ref, out_sem).wait()


def attend(bounds, last, begin, q, kv):
    smem = pl.BlockSpec(memory_space=pltpu.SMEM)
    vmem = pl.BlockSpec(memory_space=pltpu.VMEM)
    hbm = pl.BlockSpec(memory_space=pl.ANY)
    lanes = TILE * 8
    return pl.pallas_call(
        attend_kernel,
        out_shape=jax.ShapeDtypeStruct((ROWS, HALF), jnp.bfloat16),
        in_specs=[smem, vmem, vmem, hbm, hbm],
        out_specs=hbm,
        scratch_shapes=[
            pltpu.VMEM((2, ROWS // TILE, lanes, HEAD_SIZE), jnp.bfloat16),
            pltpu.VMEM((8, KEYS, 512), jnp.bfloat16),
            pltpu.VMEM((ROWS, HALF), jnp.bfloat16),
            pltpu.VMEM((2, 1, lanes), jnp.float32),
            pltpu.VMEM((2, HEAD_SIZE, lanes), jnp.float32),
            pltpu.VMEM((2, 1, lanes), jnp.float32),
            pltpu.VMEM((2, 1, lanes), jnp.float32),
            pltpu.VMEM((2, BLOCK, lanes), jnp.float32),
            pltpu.VMEM((2, BLOCK, lanes), jnp.float32),
            pltpu.VMEM((2, BLOCK, lanes), jnp.bfloat16),
            pltpu.VMEM((2, BLOCK, lanes), jnp.bfloat16),
            pltpu.SMEM((4, ROWS // TILE * 16 + 4), jnp.int32),
            pltpu.SemaphoreType.DMA((2,)),
            pltpu.SemaphoreType.DMA(()),
        ],
        compiler_params=pltpu.CompilerParams(vmem_limit_bytes=VMEM_LIMIT),
        name="attend",
    )(bounds, last, begin, q, kv)


def local(queries, keys, values, plan, doc_lengths):
    x, y, z, _ = coords()
    my_cycle = x % 2 * 4 + y % 2 * 2 + z % 2
    plan_row = plan[None, :]
    q, kv, last, begin, bounds, rank = exchange(queries, keys, values, plan_row, doc_lengths)
    made = attend(bounds, last, begin, q, kv)
    ret = back(made, rank)
    return restore(jnp.reshape(my_cycle, (1,)).astype(jnp.int32), plan_row, ret)


def solution(mesh):
    return jax.shard_map(
        local,
        mesh=mesh,
        in_specs=(
            P(("blk", "group"), None),
            P(("blk", "group"), None),
            P(("blk", "group"), None),
            P(("blk", "group")),
            P("group", None),
        ),
        out_specs=P(("blk", "group"), None),
        check_vma=False,
    )
```

```python
import math

import jax
import jax.numpy as jnp
from jax import lax
from jax.experimental import pallas as pl
from jax.experimental.pallas import tpu as pltpu
from jax.sharding import PartitionSpec as P

QUERY_HEADS = 32
KEY_VALUE_HEADS = 4
HEAD_SIZE = 128
THETA = 500000.0

TOK = 256
SLOT = 64
KEYS = 512
BLOCK = 256
TILE = 64
TILE_BITS = 6
SUPER = 256
HALF = QUERY_HEADS // 2 * HEAD_SIZE
WIDE = HALF + 128
ROWS = 16 * SLOT
NEG = -1e30
SCALE = math.log2(math.e) / math.sqrt(HEAD_SIZE)
MESH = pl.DeviceIdType.MESH
VMEM_LIMIT = 60 * 1024 * 1024


def coords():
    b = lax.axis_index("blk")
    g = lax.axis_index("group")
    return b // 4, g % 4, (b // 2) % 2 * 2 + g // 4, b % 2


def device(x, y, z, core):
    x, y, z = lax.rem(x + 4, 4), lax.rem(y + 4, 4), lax.rem(z + 4, 4)
    return x * 4 + z // 2 * 2 + core, lax.rem(z, 2) * 4 + y


def moved(sign, delta, core):
    x, y, z, _ = coords()
    return device(x + sign * (delta // 4), y + sign * (delta // 2 % 2), z + sign * (delta % 2), core)


def sign_of(core):
    return 1 - 2 * core


def signal(target):
    pl.semaphore_signal(pltpu.get_barrier_semaphore(), inc=1, device_id=target, device_id_type=MESH)


def remote(src, dst, send, recv, target):
    return pltpu.make_async_remote_copy(
        src_ref=src, dst_ref=dst, send_sem=send, recv_sem=recv, device_id=target, device_id_type=MESH
    )


THIRDS = ((0, 176, (4, 2, 1)), (176, 176, (2, 1, 4)), (352, 160, (1, 4, 2)))
PAIR = 512
PART = 128


def iota(shape, axis):
    return lax.broadcasted_iota(jnp.int32, shape, axis)


def bf16(flags):
    return jnp.where(flags, 1.0, 0.0).astype(jnp.bfloat16)


def dot(a, b):
    return jnp.dot(a, b, preferred_element_type=jnp.float32)


def cycle_of(plan):
    return (plan >> 8) & 7


def cycle_index(plan):
    p = plan >> 11
    offset = plan & 255
    return jnp.where(offset < 128, p * 128 + offset, (31 - p) * 128 + offset - 128)


def column_of(row):
    size = row.shape[1]
    return jnp.sum(jnp.where(iota((size, size), 0) == iota((size, size), 1), row, 0), 1, keepdims=True)


def document_start(u, lengths):
    end = jnp.zeros((1, 1), jnp.int32)
    start = jnp.zeros_like(u)
    for one in range(4):
        length = lengths[0:1, one : one + 1]
        end = end + length
        start = start + jnp.where(u >= end, length, 0)
    return start


def turning(position):
    half = HEAD_SIZE // 2
    lane = iota((1, HEAD_SIZE), 1)
    spot = (lane & (half - 1)).astype(jnp.float32)
    inv_freq = jnp.exp(-math.log(THETA) * (2.0 * spot / HEAD_SIZE))
    angle = position.astype(jnp.float32) * inv_freq
    both = jnp.cos(jnp.where(lane < half, angle, angle - math.pi / 2))
    other = pltpu.roll(both, half, 1)
    first = jnp.broadcast_to(lane < half, both.shape)
    return jnp.where(first, both, other), jnp.where(first, -other, both)


def exchange_kernel(
    queries_ref, keys_ref, values_ref, plan_row, lengths_ref,
    turned_ref, all_ref, last_ref, begin_ref, bounds_ref, rank_ref,
    q_out, q_got, kv_out, kv_got, part_out, part_got, f_out, f_got, g_out, g_got, own_ref, len_out, len_got, key_ref, cos_ref, sin_ref, sorted_ref,
    q_send, q_recv, a_send, a_recv, b_send, b_recv, kv_send, kv_recv, len_send, len_recv, local_sem, out_sem,
    f_send, f_recv, g_send, g_recv,
):
    x, y, z, core = coords()
    place = x // 2 * 4 + y // 2 * 2 + z // 2
    my_cycle = x % 2 * 4 + y % 2 * 2 + z % 2
    mine = sign_of(core)
    other = 1 - core

    block_at, group_at = lax.axis_index("blk"), lax.axis_index("group")
    spot = block_at // 2
    to_device = device(
        spot // 4 * 2 + group_at // 4, spot // 2 % 2 * 2 + group_at // 2 % 2, spot % 2 * 2 + group_at % 2, block_at % 2
    )
    from_block = place * 2 + core
    at_home = (from_block == block_at) & (my_cycle == group_at)

    for delta in range(1, 8):
        for source in range(2):
            signal(moved(-sign_of(source), delta, source))
    signal(moved(0, 0, other))
    for mask in range(1, 8):
        signal(across_cycle(mask))

    @pl.when(jnp.logical_not(at_home))
    def _():
        signal((from_block, my_cycle))

    len_out[...] = jnp.zeros_like(len_out)
    len_out[0:1, 0:4] = lengths_ref[...]
    plan_r = plan_row[...]
    plan_c = column_of(plan_r)
    same = (cycle_of(plan_c) == cycle_of(plan_r)) & (iota((TOK, TOK), 0) < iota((TOK, TOK), 1))
    rank = jnp.sum(jnp.where(same, 1, 0), 0, keepdims=True)
    row = jnp.bitwise_xor(cycle_of(plan_r), my_cycle) * SLOT + rank
    choose = bf16(iota((8 * SLOT, TOK), 0) == row)
    u = cycle_index(plan_c)
    lane = iota((TOK, 128), 1)
    fields = jnp.where(lane == 0, (u >> 8) + 1, jnp.where(lane == 1, u & 255, 0))
    fields = fields.astype(jnp.float32).astype(jnp.bfloat16)
    f_out[...] = dot(choose, fields).astype(jnp.bfloat16).reshape(8, SLOT, 128)

    pl.semaphore_wait(pltpu.get_barrier_semaphore(), jnp.where(at_home, 22, 23))

    copies = []

    def start(copy):
        copy.start()
        copies.append(copy)

    def lengths_copy():
        return remote(len_out, len_got, len_send, len_recv, to_device)

    @pl.when(jnp.logical_not(at_home))
    def _():
        lengths_copy().start()

    def out_copy(src, dst, send, recv, width, delta, to_core):
        columns = pl.ds(pl.multiple_of(to_core * width, 128), width)
        slot = delta * 2 + to_core if delta else 0
        return remote(
            src.at[delta, :, columns],
            dst.at[delta, core],
            send.at[slot],
            recv.at[delta, core],
            moved(mine, delta, to_core) if delta else moved(0, 0, other),
        )

    def landed(dst, send, recv, delta, source):
        here = dst.at[delta, source]
        remote(here, here, send.at[0], recv.at[delta, source], moved(0, 0, other)).wait_recv()

    order = (7, 6, 5, 3, 4, 2, 1)

    def f_copy(delta, to_core):
        return remote(
            f_out.at[delta],
            f_got.at[delta, core],
            f_send.at[delta * 2 + to_core if delta else 0],
            f_recv.at[delta, core],
            moved(mine, delta, to_core),
        )

    start(f_copy(0, other))
    for delta in order:
        for to_core in range(2):
            start(f_copy(delta, to_core))
    f_got[0, core] = f_out[0]

    chosen_k = dot(choose, keys_ref[...]).astype(jnp.bfloat16)
    chosen_v = dot(choose, values_ref[...]).astype(jnp.bfloat16)
    for delta in range(8):
        rows = slice(delta * SLOT, (delta + 1) * SLOT)
        for half in range(2):
            kv_out[delta, :, half * PAIR : half * PAIR + 256] = chosen_k[rows, half * 256 : half * 256 + 256]
            kv_out[delta, :, half * PAIR + 256 : half * PAIR + 512] = chosen_v[rows, half * 256 : half * 256 + 256]
    start(out_copy(kv_out, kv_got, a_send, a_recv, PAIR, 0, other))
    for delta in order:
        for to_core in range(2):
            start(out_copy(kv_out, kv_got, a_send, a_recv, PAIR, delta, to_core))
    own_a = pltpu.make_async_copy(
        kv_out.at[0, :, pl.ds(pl.multiple_of(core * PAIR, 128), PAIR)], kv_got.at[0, core], local_sem.at[0]
    )
    own_a.start()

    for part in range(8):
        columns = slice(part * 512, part * 512 + 512)
        chosen = dot(choose, queries_ref[:, columns]).astype(jnp.bfloat16)
        for delta in range(8):
            q_out[delta, :, columns] = chosen[delta * SLOT : (delta + 1) * SLOT, :]
    start(out_copy(q_out, q_got, q_send, q_recv, HALF, 0, other))
    def send_queries(chunk):
        for delta in order:
            for to_core in range(2):
                columns = pl.ds(to_core * HALF, HALF)
                rows = pl.ds(chunk * 16, 16)
                remote(
                    q_out.at[delta, rows, columns],
                    q_got.at[delta, core, rows],
                    q_send.at[delta * 2 + to_core],
                    q_recv.at[delta, core],
                    moved(mine, delta, to_core),
                ).start()

    send_queries(0)
    for delta in order:
        for to_core in range(2):
            copies.append(out_copy(q_out, q_got, q_send, q_recv, HALF, delta, to_core))
    own_q = pltpu.make_async_copy(
        q_out.at[0, :, pl.ds(pl.multiple_of(core * HALF, 128), HALF)], q_got.at[0, core], local_sem.at[1]
    )
    own_q.start()

    landed(f_got, f_send, f_recv, 0, other)
    for delta in range(1, 8):
        for source in range(2):
            landed(f_got, f_send, f_recv, delta, source)

    def fields_of(table):
        fields = table.reshape(ROWS, 128).astype(jnp.float32)
        flat = fields.T
        out = []
        for lead, low in ((fields[:, 0:1], fields[:, 1:2]), (flat[0:1, :], flat[1:2, :])):
            lead = lead.astype(jnp.int32)
            out.append((lead > 0, (lead - 1) * 256 + low.astype(jnp.int32)))
        return out

    def holder_of(u):
        block = u >> 8
        return jnp.where(block < 8, block, 15 - block)

    (valid_c, u_c), (valid_r, u_r) = fields_of(f_got[...])
    key_c = jnp.where(valid_c, holder_of(u_c), -1)
    key_r = jnp.where(valid_r, holder_of(u_r), -2)
    key_ref[...] = jnp.broadcast_to(key_c, (ROWS, 128))

    def count_before(step, total):
        base = pl.multiple_of(step * 128, 128)
        chunk = key_ref[pl.ds(base, 128), 0:1]
        hits = (chunk == key_r) & (iota((128, ROWS), 0) + base < iota((128, ROWS), 1))
        return total + jnp.sum(jnp.where(hits, 1, 0), 0, keepdims=True)

    before = lax.fori_loop(0, ROWS // 128, count_before, jnp.zeros((1, ROWS), jnp.int32))
    target = jnp.where(valid_r, key_r * PART + before, -1)

    def flip(mask):
        out = 0
        for bit in (4, 2, 1):
            digit = place // bit % 2
            out = out + bit * ((1 - digit) if mask & bit else digit)
        return out

    def place_fields(step, carry):
        base = pl.multiple_of(step * 4 * PART, 4 * PART)
        rows = dot(bf16(iota((4 * PART, ROWS), 0) + base == target), f_got[...].reshape(ROWS, 128))
        g_out[pl.ds(step * 4, 4)] = rows.astype(jnp.bfloat16).reshape(4, PART, 128)
        return carry

    lax.fori_loop(0, 2, place_fields, 0)
    for mask in order:
        start(remote(g_out.at[flip(mask)], g_got.at[place], g_send.at[mask], g_recv.at[mask], across_cycle(mask)))
    send_queries(1)
    g_got[place] = g_out[place]

    own_a.wait()
    landed(kv_got, a_send, a_recv, 0, other)
    for delta in range(1, 8):
        for source in range(2):
            landed(kv_got, a_send, a_recv, delta, source)

    def fill(step, carry):
        base = pl.multiple_of(step * 4 * PART, 4 * PART)
        rows = dot(bf16(iota((4 * PART, ROWS), 0) + base == target), kv_got[...].reshape(ROWS, PAIR))
        part_out[pl.ds(step * 4, 4)] = rows.astype(jnp.bfloat16).reshape(4, PART, PAIR)
        return carry

    lax.fori_loop(0, 2, fill, 0)

    for mask in order:
        start(
            remote(
                part_out.at[flip(mask)], part_got.at[place], b_send.at[mask], b_recv.at[mask], across_cycle(mask)
            )
        )
    send_queries(2)
    part_got[place] = part_out[place]

    index_c, index_r = iota((ROWS, 1), 0), iota((1, ROWS), 1)
    key_c = jnp.where(valid_c, u_c, 4096 + index_c)
    key_r = jnp.where(valid_r, u_r, 4096 + index_r)
    key_ref[...] = jnp.broadcast_to(key_c, (ROWS, 128))

    def rank_step(step, total):
        base = pl.multiple_of(step * 128, 128)
        chunk = key_ref[pl.ds(base, 128), 0:1]
        counts = jnp.sum(jnp.where(key_r < chunk, 1, 0), 1, keepdims=True)
        rank_ref[pl.ds(base, 128), :] = jnp.broadcast_to(counts, (128, 128))
        return total + jnp.sum(jnp.where(chunk < key_r, 1, 0), 0, keepdims=True)

    rank_r = lax.fori_loop(0, ROWS // 128, rank_step, jnp.zeros((1, ROWS), jnp.int32))

    def sort_step(step, total):
        base = pl.multiple_of(step * 128, 128)
        chunk = key_ref[pl.ds(base, 128), 0:1]
        ranks = rank_ref[pl.ds(base, 128), 0:1]
        return total + jnp.sum(jnp.where(ranks == iota((128, ROWS), 1), chunk, 0), 0, keepdims=True)

    sorted_r = lax.fori_loop(0, ROWS // 128, sort_step, jnp.zeros((1, ROWS), jnp.int32))

    @pl.when(at_home)
    def _():
        len_got[...] = len_out[...]

    @pl.when(jnp.logical_not(at_home))
    def _():
        lengths_copy().wait()

    lengths = len_got[...]
    begin_r = jnp.where(sorted_r < 4096, document_start(sorted_r, lengths), 8192)

    own_tile = iota((ROWS // TILE, ROWS), 1) >> TILE_BITS == iota((ROWS // TILE, ROWS), 0)
    spread = bf16(iota((ROWS, TILE * 8), 0) & (TILE - 1) == iota((ROWS, TILE * 8), 1) & (TILE - 1))
    for values, tiles_ref in ((sorted_r, last_ref), (begin_r, begin_ref)):
        parts = [
            dot(jnp.where(own_tile, half, 0).astype(jnp.float32).astype(jnp.bfloat16), spread).astype(jnp.int32)
            for half in (values >> 8, values & 255)
        ]
        tiles_ref[...] = parts[0] * 256 + parts[1]

    def turn_step(step, carry):
        low, high = carry
        base = pl.multiple_of(step * 128, 128)
        hits = iota((128, ROWS), 0) + base == rank_r
        u = jnp.sum(jnp.where(hits, key_r, 0), 1, keepdims=True)
        live = u < 4096
        start = document_start(u, lengths)
        index, tile = iota((128, 128), 0) + base, iota((128, 128), 1)
        low = low + jnp.sum(jnp.where((index == tile * TILE) & live, start >> 8, 0), 0, keepdims=True)
        high = jnp.maximum(
            high, jnp.max(jnp.where((index >> TILE_BITS == tile) & live, u >> 8, -1), 0, keepdims=True)
        )
        cos, sin = turning(jnp.where(live, u - start, 0))
        cos_ref[pl.ds(base, 128), :] = cos * SCALE
        sin_ref[pl.ds(base, 128), :] = sin * SCALE
        return low, high

    low, high = lax.fori_loop(
        0, ROWS // 128, turn_step, (jnp.zeros((1, 128), jnp.int32), jnp.full((1, 128), -1, jnp.int32))
    )
    bounds_ref[...] = jnp.zeros_like(bounds_ref)
    bounds_ref[0:1, :] = low
    bounds_ref[1:2, :] = high
    rows_c = iota((KEYS, 1), 0)
    key_u = jnp.where(rows_c < BLOCK, place * BLOCK + rows_c, (15 - place) * BLOCK + rows_c - BLOCK)
    key_cos, key_sin = turning(key_u - document_start(key_u, lengths))

    for mask in range(1, 8):
        here = g_got.at[flip(mask)]
        remote(here, here, g_send.at[mask], g_recv.at[mask], across_cycle(mask)).wait_recv()
    _, (valid, u) = fields_of(g_got[...])
    target = jnp.where(valid, jnp.where(u >= 2048, BLOCK, 0) + (u & 255), -1)
    arrange = bf16(iota((KEYS, ROWS), 0) == target)

    for mask in range(1, 8):
        here = part_got.at[flip(mask)]
        remote(here, here, b_send.at[mask], b_recv.at[mask], across_cycle(mask)).wait_recv()

    placed = dot(arrange, part_got[...].reshape(ROWS, PAIR))
    for head in range(2):
        columns = slice(head * HEAD_SIZE, (head + 1) * HEAD_SIZE)
        entry = placed[:, columns]
        entry = entry * key_cos + pltpu.roll(entry, HEAD_SIZE // 2, 1) * key_sin
        own_ref[:, columns] = entry.astype(jnp.bfloat16)
    for half in range(2):
        rows = slice(half * BLOCK, (half + 1) * BLOCK)
        own_ref[rows, 256:] = placed[rows, 256:].T.astype(jnp.bfloat16)

    own_kv = pltpu.make_async_copy(own_ref, all_ref.at[place], local_sem.at[2])
    own_kv.start()

    def kv_copy(third, index):
        start, size, (b1, b2, b3) = THIRDS[third]
        mask, axis = ((0, b1), (0, b2), (0, b3), (b1, b2), (b1, b3), (b2, b3), (b1 ^ b2, b3))[index]
        rows = pl.ds(start, size)
        block = flip(mask)
        src = own_ref.at[rows] if mask == 0 else all_ref.at[block, rows]
        return remote(
            src, all_ref.at[block, rows], kv_send.at[third, index], kv_recv.at[third, index], across_cycle(axis)
        )

    def kv_landed(third, index):
        start, size, (b1, b2, b3) = THIRDS[third]
        mask = (b1, b2, b3, b1 ^ b2, b1 ^ b3, b2 ^ b3, 7)[index]
        here = all_ref.at[flip(mask), pl.ds(start, size)]
        remote(here, here, kv_send.at[third, index], kv_recv.at[third, index], across_cycle(4)).wait_recv()

    for index in range(3):
        for third in range(3):
            start(kv_copy(third, index))

    send_queries(3)
    landed(q_got, q_send, q_recv, 0, other)
    for delta in range(1, 8):
        for source in range(2):
            landed(q_got, q_send, q_recv, delta, source)
    own_q.wait()

    def order_queries(sup):
        base = sup * SUPER
        pick = bf16(iota((SUPER, ROWS), 0) + base == rank_r)
        cos = cos_ref[base : base + SUPER, :]
        sin = sin_ref[base : base + SUPER, :]

        def one_part(part, carry):
            columns = pl.ds(pl.multiple_of(part * 256, 256), 256)
            rows = dot(pick, q_got[:, :, :, columns].reshape(ROWS, 256))
            for one in range(2):
                entry = rows[:, one * HEAD_SIZE : (one + 1) * HEAD_SIZE]
                entry = entry * cos + pltpu.roll(entry, HEAD_SIZE // 2, 1) * sin
                entry = entry.astype(jnp.bfloat16)
                first = pl.multiple_of((part % 4 * 2 + one) * TILE, TILE)
                for tile in range(SUPER // TILE):
                    sorted_ref[part // 4, sup * (SUPER // TILE) + tile, pl.ds(first, TILE), :] = entry[
                        tile * TILE : (tile + 1) * TILE
                    ]
            return carry

        lax.fori_loop(0, 8, one_part, 0)
        turned_copy(sup).start()

    def turned_copy(sup):
        tiles = pl.ds(sup * (SUPER // TILE), SUPER // TILE)
        return pltpu.make_async_copy(sorted_ref.at[:, tiles], turned_ref.at[:, tiles], out_sem.at[sup])

    for third in range(3):
        kv_landed(third, 0)
        start(kv_copy(third, 3))
        start(kv_copy(third, 4))
    for third in range(3):
        kv_landed(third, 1)
        start(kv_copy(third, 5))
    order_queries(0)
    for third in range(3):
        kv_landed(third, 3)
        start(kv_copy(third, 6))
    for sup in range(1, 4):
        order_queries(sup)
    for index in (2, 4, 5, 6):
        for third in range(3):
            kv_landed(third, index)
    own_kv.wait()
    for sup in range(4):
        turned_copy(sup).wait()
    for copy in copies:
        copy.wait_send()


def across_cycle(mask):
    x, y, z, core = coords()
    return device(x + 2 * (mask // 4), y + 2 * (mask // 2 % 2), z + 2 * (mask % 2), core)


def exchange(queries, keys, values, plan_row, lengths):
    vmem = pl.BlockSpec(memory_space=pltpu.VMEM)
    dma = pltpu.SemaphoreType.DMA
    return pl.pallas_call(
        exchange_kernel,
        out_shape=(
            jax.ShapeDtypeStruct((2, ROWS // TILE, TILE * 8, HEAD_SIZE), jnp.bfloat16),
            jax.ShapeDtypeStruct((8, KEYS, 512), jnp.bfloat16),
            jax.ShapeDtypeStruct((ROWS // TILE, TILE * 8), jnp.int32),
            jax.ShapeDtypeStruct((ROWS // TILE, TILE * 8), jnp.int32),
            jax.ShapeDtypeStruct((8, 128), jnp.int32),
            jax.ShapeDtypeStruct((ROWS, 128), jnp.int32),
        ),
        in_specs=[vmem] * 5,
        out_specs=[pl.BlockSpec(memory_space=pl.ANY)] * 2 + [vmem] * 4,
        scratch_shapes=[
            pltpu.VMEM((8, SLOT, 2 * HALF), jnp.bfloat16),
            pltpu.VMEM((8, 2, SLOT, HALF), jnp.bfloat16),
            pltpu.VMEM((8, SLOT, 2 * PAIR), jnp.bfloat16),
            pltpu.VMEM((8, 2, SLOT, PAIR), jnp.bfloat16),
            pltpu.VMEM((8, PART, PAIR), jnp.bfloat16),
            pltpu.VMEM((8, PART, PAIR), jnp.bfloat16),
            pltpu.VMEM((8, SLOT, 128), jnp.bfloat16),
            pltpu.VMEM((8, 2, SLOT, 128), jnp.bfloat16),
            pltpu.VMEM((8, PART, 128), jnp.bfloat16),
            pltpu.VMEM((8, PART, 128), jnp.bfloat16),
            pltpu.VMEM((KEYS, 512), jnp.bfloat16),
            pltpu.VMEM((8, 128), jnp.int32),
            pltpu.VMEM((8, 128), jnp.int32),
            pltpu.VMEM((ROWS, 128), jnp.int32),
            pltpu.VMEM((ROWS, HEAD_SIZE), jnp.float32),
            pltpu.VMEM((ROWS, HEAD_SIZE), jnp.float32),
            pltpu.VMEM((2, ROWS // TILE, TILE * 8, HEAD_SIZE), jnp.bfloat16),
            dma((16,)), dma((8, 2)), dma((16,)), dma((8, 2)), dma((8,)), dma((8,)), dma((3, 7)), dma((3, 7)),
            dma(()), dma(()), dma((3,)), dma((4,)), dma((16,)), dma((8, 2)), dma((8,)), dma((8,)),
        ],
        compiler_params=pltpu.CompilerParams(
            collective_id=0, has_side_effects=True, vmem_limit_bytes=VMEM_LIMIT
        ),
        name="exchange",
    )(queries, keys, values, plan_row, lengths)


def back_kernel(made_ref, rank_ref, ret_ref, send_ref, send, recv, local_sem):
    x, y, z, core = coords()
    mine = sign_of(core)
    other = 1 - core
    for delta in range(1, 8):
        for worker in range(2):
            signal(moved(mine, delta, worker))
    signal(moved(0, 0, other))

    columns = pl.ds(pl.multiple_of(core * HALF, 128), HALF)

    def place_rows(pair):
        ranks = [rank_ref[delta * 2 * SLOT : (delta + 1) * 2 * SLOT, 0:1] for delta in pair]
        put = bf16(jnp.concatenate(ranks, 0) == iota((4 * SLOT, ROWS), 1))

        def one_part(part, carry):
            here = pl.ds(pl.multiple_of(part * 512, 512), 512)
            chosen = dot(put, made_ref[:, here]).astype(jnp.bfloat16)
            for one in range(4):
                send_ref[pair[one // 2], one % 2, :, here] = chosen[one * SLOT : (one + 1) * SLOT, :]
            return carry

        lax.fori_loop(0, 4, one_part, 0)

    copies = []

    def back_copy(delta, source, first, size):
        rows = pl.ds(first, size)
        return remote(
            send_ref.at[delta, source, rows],
            ret_ref.at[delta, rows, columns],
            send.at[delta * 2 + source],
            recv.at[delta, core],
            moved(-sign_of(source), delta, source),
        )

    pairs = ((7, 0), (6, 1), (5, 2), (3, 4))
    place_rows(pairs[0])
    pl.semaphore_wait(pltpu.get_barrier_semaphore(), 15)
    for pair in pairs:
        if pair != pairs[0]:
            place_rows(pair)
        deltas = [delta for delta in pair if delta]
        for chunk in range(SLOT // 16):
            for delta in deltas:
                for source in range(2):
                    back_copy(delta, source, chunk * 16, 16).start()
        for delta in deltas:
            for source in range(2):
                copies.append(back_copy(delta, source, 0, SLOT))
    own = pltpu.make_async_copy(send_ref.at[0, core], ret_ref.at[0, :, columns], local_sem)
    own.start()
    copy = remote(
        send_ref.at[0, other], ret_ref.at[0, :, columns], send.at[0], recv.at[0, core], moved(0, 0, other)
    )
    copy.start()
    copies.append(copy)

    def landed(delta, worker):
        here = ret_ref.at[delta, :, pl.ds(pl.multiple_of(worker * HALF, 128), HALF)]
        remote(here, here, send.at[0], recv.at[delta, worker], moved(0, 0, other)).wait_recv()

    own.wait()
    landed(0, other)
    for delta in range(1, 8):
        for worker in range(2):
            landed(delta, worker)

    for copy in copies:
        copy.wait_send()


def back(made, rank):
    vmem = pl.BlockSpec(memory_space=pltpu.VMEM)
    return pl.pallas_call(
        back_kernel,
        out_shape=jax.ShapeDtypeStruct((8, SLOT, 2 * HALF), jnp.bfloat16),
        in_specs=[vmem] * 2,
        out_specs=pl.BlockSpec(memory_space=pl.ANY),
        scratch_shapes=[
            pltpu.VMEM((8, 2, SLOT, HALF), jnp.bfloat16),
            pltpu.SemaphoreType.DMA((16,)),
            pltpu.SemaphoreType.DMA((8, 2)),
            pltpu.SemaphoreType.DMA(()),
        ],
        compiler_params=pltpu.CompilerParams(
            collective_id=1, has_side_effects=True, vmem_limit_bytes=VMEM_LIMIT
        ),
        name="back",
    )(made, rank)


def restore_kernel(cycle_ref, plan_row, ret_ref, out_ref, choose_ref):
    @pl.when(pl.program_id(0) == 0)
    def _():
        plan_r = plan_row[...]
        plan_c = column_of(plan_r)
        same = (cycle_of(plan_c) == cycle_of(plan_r)) & (iota((TOK, TOK), 1) < iota((TOK, TOK), 0))
        rank = jnp.sum(jnp.where(same, 1, 0), 1, keepdims=True)
        row = jnp.bitwise_xor(cycle_of(plan_c), cycle_ref[0]) * SLOT + rank
        choose_ref[...] = bf16(iota((TOK, 8 * SLOT), 1) == row)

    rows = ret_ref[...].reshape(8 * SLOT, ret_ref.shape[2])
    out_ref[...] = dot(choose_ref[...], rows).astype(jnp.bfloat16)


def restore(my_cycle, plan_row, ret):
    width = 2048
    return pl.pallas_call(
        restore_kernel,
        grid=(2 * HALF // width,),
        out_shape=jax.ShapeDtypeStruct((TOK, 2 * HALF), jnp.bfloat16),
        in_specs=[
            pl.BlockSpec(memory_space=pltpu.SMEM),
            pl.BlockSpec((1, TOK), lambda i: (0, 0)),
            pl.BlockSpec((8, SLOT, width), lambda i: (0, 0, i)),
        ],
        out_specs=pl.BlockSpec((TOK, width), lambda i: (0, i)),
        scratch_shapes=[pltpu.VMEM((TOK, 8 * SLOT), jnp.bfloat16)],
        compiler_params=pltpu.CompilerParams(vmem_limit_bytes=VMEM_LIMIT),
        name="restore",
    )(my_cycle, plan_row, ret)


def attend_kernel(
    bounds_ref, last_ref, begin_ref, turned_ref, all_ref,
    made_ref, turned, kv_ref, made, peak, total, summed, decays, scores0, scores1, weights0, weights1, items, in_sem, out_sem,
):
    across = iota((BLOCK, TILE * 8), 0)
    tiles = ROWS // TILE
    loads = (
        pltpu.make_async_copy(turned_ref, turned, in_sem.at[0]),
        pltpu.make_async_copy(all_ref, kv_ref, in_sem.at[1]),
    )
    for load in loads:
        load.start()

    def store(tile):
        rows = pl.ds(pl.multiple_of(tile * TILE, TILE), TILE)
        return pltpu.make_async_copy(made.at[rows], made_ref.at[rows], out_sem)

    def list_tile(tile, count):
        low = bounds_ref[0, tile]
        high = bounds_ref[1, tile]

        def list_block(block, count):
            items[0, count] = tile
            items[1, count] = block
            items[2, count] = (block == low).astype(jnp.int32)
            items[3, count] = (block == high).astype(jnp.int32)
            return count + 1

        @pl.when(high < low)
        def _():
            made[pl.ds(pl.multiple_of(tile * TILE, TILE), TILE), :] = jnp.zeros((TILE, HALF), jnp.bfloat16)
            store(tile).start()

        return lax.fori_loop(low, high + 1, list_block, count)

    count = lax.fori_loop(0, tiles, list_tile, 0)
    for extra in range(3):
        items[0, count + extra] = 0
        items[1, count + extra] = 32
        items[2, count + extra] = 0
        items[3, count + extra] = 0

    peak[...] = jnp.full_like(peak, NEG)
    summed[...] = jnp.zeros_like(summed)
    total[...] = jnp.zeros_like(total)
    decays[...] = jnp.ones_like(decays)
    weights1[...] = jnp.zeros_like(weights1)
    for load in loads:
        load.wait()

    def spot(block):
        block = jnp.minimum(block, 15)
        return jnp.where(block < 8, block, 15 - block), jnp.where(block < 8, 0, BLOCK)

    def score_of(item, scores):
        tile, block = items[0, item], items[1, item]
        begin = begin_ref[pl.ds(tile, 1), :]
        span = jnp.maximum(last_ref[pl.ds(tile, 1), :] - begin + 1, 0).astype(jnp.uint32)
        holder, row = spot(block)
        allowed = (across + (block * BLOCK - begin)).astype(jnp.uint32) < span
        for head in range(2):
            key = kv_ref[
                holder,
                pl.ds(pl.multiple_of(row, BLOCK), BLOCK),
                head * HEAD_SIZE : (head + 1) * HEAD_SIZE,
            ]
            score = lax.dot_general(
                key, turned[head, tile], (((1,), (1,)), ((), ())), preferred_element_type=jnp.float32
            )
            scores[head] = jnp.where(allowed, score, NEG)

    def weigh(item, scores, weights):
        opens = items[2, item] == 1
        for head in range(2):
            score = scores[head]
            old = jnp.where(opens, NEG, peak[head])
            new = jnp.maximum(old, jnp.max(score, 0, keepdims=True))
            decay = jnp.where(opens, 0.0, jnp.exp2(old - new))
            peak[head] = new
            weight = jnp.exp2(score - new)
            summed[head] = summed[head] * decay + jnp.sum(weight, 0, keepdims=True)
            weights[head] = weight.astype(jnp.bfloat16)
            decays[head] = decay

    def add(item, weights):
        holder, row = spot(items[1, item])
        for head in range(2):
            value = kv_ref[
                holder,
                pl.ds(pl.multiple_of(row + head * HEAD_SIZE, HEAD_SIZE), HEAD_SIZE),
                2 * HEAD_SIZE :,
            ]
            total[head] = total[head] * decays[head] + jnp.dot(
                value, weights[head], preferred_element_type=jnp.float32
            )

    score_of(0, scores0)

    def two_steps(pair, carry):
        item = pair * 2
        add(jnp.maximum(item - 1, 0), weights1)
        score_of(item + 1, scores1)
        keep = summed[...]
        weigh(item, scores0, weights0)
        close_after(item - 1, keep)
        add(item, weights0)
        score_of(item + 2, scores0)
        keep = summed[...]
        weigh(item + 1, scores1, weights1)
        close_after(item, keep)
        return carry

    def close_after(item, sums):
        at = jnp.maximum(item, 0)

        @pl.when((items[3, at] == 1) & (item >= 0))
        def _():
            there = pl.multiple_of(items[0, at] * TILE, TILE)
            for head in range(2):
                result = (total[head] / jnp.maximum(sums[head], 1e-30)).T.astype(jnp.bfloat16)
                for one in range(8):
                    made[pl.ds(there, TILE), pl.ds((head * 8 + one) * HEAD_SIZE, HEAD_SIZE)] = result[
                        one * TILE : (one + 1) * TILE
                    ]
            store(items[0, at]).start()

    lax.fori_loop(0, (count + 2) // 2, two_steps, 0)
    pltpu.make_async_copy(made, made_ref, out_sem).wait()


def attend(bounds, last, begin, q, kv):
    smem = pl.BlockSpec(memory_space=pltpu.SMEM)
    vmem = pl.BlockSpec(memory_space=pltpu.VMEM)
    hbm = pl.BlockSpec(memory_space=pl.ANY)
    lanes = TILE * 8
    return pl.pallas_call(
        attend_kernel,
        out_shape=jax.ShapeDtypeStruct((ROWS, HALF), jnp.bfloat16),
        in_specs=[smem, vmem, vmem, hbm, hbm],
        out_specs=hbm,
        scratch_shapes=[
            pltpu.VMEM((2, ROWS // TILE, lanes, HEAD_SIZE), jnp.bfloat16),
            pltpu.VMEM((8, KEYS, 512), jnp.bfloat16),
            pltpu.VMEM((ROWS, HALF), jnp.bfloat16),
            pltpu.VMEM((2, 1, lanes), jnp.float32),
            pltpu.VMEM((2, HEAD_SIZE, lanes), jnp.float32),
            pltpu.VMEM((2, 1, lanes), jnp.float32),
            pltpu.VMEM((2, 1, lanes), jnp.float32),
            pltpu.VMEM((2, BLOCK, lanes), jnp.float32),
            pltpu.VMEM((2, BLOCK, lanes), jnp.float32),
            pltpu.VMEM((2, BLOCK, lanes), jnp.bfloat16),
            pltpu.VMEM((2, BLOCK, lanes), jnp.bfloat16),
            pltpu.SMEM((4, ROWS // TILE * 16 + 4), jnp.int32),
            pltpu.SemaphoreType.DMA((2,)),
            pltpu.SemaphoreType.DMA(()),
        ],
        compiler_params=pltpu.CompilerParams(vmem_limit_bytes=VMEM_LIMIT),
        name="attend",
    )(bounds, last, begin, q, kv)


def local(queries, keys, values, plan, doc_lengths):
    x, y, z, _ = coords()
    my_cycle = x % 2 * 4 + y % 2 * 2 + z % 2
    plan_row = plan[None, :]
    q, kv, last, begin, bounds, rank = exchange(queries, keys, values, plan_row, doc_lengths)
    made = attend(bounds, last, begin, q, kv)
    ret = back(made, rank)
    return restore(jnp.reshape(my_cycle, (1,)).astype(jnp.int32), plan_row, ret)


def solution(mesh):
    return jax.shard_map(
        local,
        mesh=mesh,
        in_specs=(
            P(("blk", "group"), None),
            P(("blk", "group"), None),
            P(("blk", "group"), None),
            P(("blk", "group")),
            P("group", None),
        ),
        out_specs=P(("blk", "group"), None),
        check_vma=False,
    )
```
